32 devices in a mesh: slide: 4 (over y, core), tile: 8 (over z, x).
Axes of the slice: x: 2, y: 2, z: 4, core: 2. Of those that a mesh axis runs over, the one named last changes fastest.
Arguments:
- slide_image: bfloat16 [4, 16, 32, 2048], P('slide', 'tile'), may hold values from -6 to 6
- cotangent: bfloat16 [4, 16, 32, 2048], P('slide', 'tile'), may hold values from -0.0234375 to 0.0234375
- weight_one: bfloat16 [3, 3, 64, 64], replicated, may hold values from -0.25 to 0.25
- weight_two: bfloat16 [3, 3, 64, 64], replicated, may hold values from -0.25 to 0.25
- tissue: int32 [4, 16], P('slide', 'tile'), may hold values from 0 to 1, as said below
- neighbours: int32 [4, 16, 8], P('slide', 'tile'), may hold values from -1 to 15, as said below
Outputs:
- output: bfloat16 [4, 16, 32, 2048], P('slide', 'tile')
- grad_input: bfloat16 [4, 16, 32, 2048], P('slide', 'tile')
- grad_one: float32 [3, 3, 64, 64], replicated
- grad_two: float32 [3, 3, 64, 64], replicated
The draws below stay inside these ranges and needn't reach their ends.
Inputs may be any that keep to these rules, and one draw needn't show every extreme that they name: The tissue tiles of a slide lie on a grid 4 tiles wide in raster order, and device k of the tile axis holds 1 to 2 of them in its first slots, later devices holding later tiles. `neighbours`: slots with tissue 0 have all -1. Neighbour relations are mutual, name only tissue slots, and every neighbour's slot lies on a device at most 5 positions away along the tile axis; that distance is reached in every slide.
All inputs are finite; a program needn't handle non-finite values.
Results may differ from the reference program's by a relative error of at most 0.017.
Values may be sent and summed in bfloat16 or wider, within the bound.
No kernel may reach another device: no remote copies, remote signals or barrier semaphores. Data moves between devices by JAX's collectives and lax.ppermute only.
A program may use at most 64 MiB of HBM per device.

```python
import jax
import jax.numpy as jnp
from jax import lax

C = 64
TS = 32
TILE_DEV = 2
GW = 4
TILES = 16
SLIDES = 4
N_SLIDE = 4
N_TILE = 8


def one_layout(key):
    count_key, gap_key = jax.random.split(key)
    device = jnp.arange(N_TILE, dtype=jnp.int32)
    counts = jax.random.randint(count_key, (N_TILE,), 1, TILE_DEV + 1, dtype=jnp.int32)
    counts = jnp.where(device <= GW + 1, 1, counts).astype(jnp.int32)
    ends = jnp.cumsum(counts).astype(jnp.int32)
    starts = (ends - counts).astype(jnp.int32)
    total = ends[-1]
    index = jnp.arange(TILES, dtype=jnp.int32)
    gaps = jax.random.randint(gap_key, (TILES,), 0, 2, dtype=jnp.int32)
    gaps = jnp.where(index <= GW + 1, 0, gaps).astype(jnp.int32)
    places = (index + jnp.cumsum(gaps)).astype(jnp.int32)
    owner = index // TILE_DEV
    local_slot = index % TILE_DEV
    present = local_slot < counts[owner]
    order = jnp.clip(starts[owner] + local_slot, 0, TILES - 1)
    place = places[order]
    row_pos = place // GW
    col_pos = place % GW
    moves = ((-1, 0), (1, 0), (0, -1), (0, 1), (-1, -1), (-1, 1), (1, -1), (1, 1))
    columns = []
    for step_row, step_col in moves:
        target = place + step_row * GW + step_col
        inside = (col_pos + step_col >= 0) & (col_pos + step_col < GW) & (row_pos + step_row >= 0)
        found = jnp.clip(jnp.searchsorted(places, target).astype(jnp.int32), 0, TILES - 1)
        hit = inside & (places[found] == target) & (found < total) & present
        holder = jnp.clip(jnp.searchsorted(ends, found, side='right').astype(jnp.int32), 0, N_TILE - 1)
        neighbour_slot = holder * TILE_DEV + found - starts[holder]
        columns.append(jnp.where(hit, neighbour_slot, -1).astype(jnp.int32))
    return (present.astype(jnp.int32), jnp.stack(columns, axis=-1).astype(jnp.int32))


def slide_layout(key):
    keys = jax.random.split(key, N_SLIDE)
    return jax.vmap(one_layout)(keys)


def draw_tissue(key, part):
    return slide_layout(key)[0]


def draw_neighbours(key, part):
    return slide_layout(key)[1]


def block_levels(rng, dims, cuts, low, largest):
    def one(axis_at, parts):
        heights = jax.random.uniform(jax.random.fold_in(jax.random.fold_in(rng, 6), axis_at), (parts,), jnp.float32, low / len(cuts), largest / len(cuts))
        return jnp.repeat(jnp.exp(heights), dims[axis_at] // parts).reshape((-1,) + (1,) * (len(dims) - axis_at - 1))

    gain = one(*cuts[0])
    for cut in cuts[1:]:
        gain = gain * one(*cut)
    return gain


def gaussian(own_key, shape, deviation, limit, shards=(), held_as=jnp.bfloat16):
    level = block_levels(own_key, shape, shards, -0.22, 0.18) if shards else 1.0
    entries = jax.random.normal(own_key, shape, jnp.float32) * deviation * level
    return jnp.minimum(jnp.maximum(entries, -limit), limit).astype(held_as)


def setup_inputs(seed: int = 0) -> dict:
    streams_of = jax.random.split(jax.random.key(seed), 7)
    slide_image = gaussian(streams_of[0], (SLIDES, TILES, TS, TS * C), 1.0, 6.0, ((0, 4), (1, 8)))
    cotangent = gaussian(streams_of[1], (SLIDES, TILES, TS, TS * C), (SLIDES * TILES * TS * TS) ** -0.5, 0.0234375, ((0, 4), (1, 8)))
    weight_one = gaussian(streams_of[2], (3, 3, C, C), (9 * C) ** -0.5, 0.25)
    weight_two = gaussian(streams_of[3], (3, 3, C, C), (9 * C) ** -0.5, 0.25)
    tissue = draw_tissue(jax.random.fold_in(streams_of[6], 71), 0)
    neighbours = draw_neighbours(jax.random.fold_in(streams_of[6], 71), 0)
    return dict(slide_image=slide_image, cotangent=cotangent, weight_one=weight_one, weight_two=weight_two, tissue=tissue, neighbours=neighbours)


STRIP_OF_DIRECTION = (1, 0, 3, 2, 1, 1, 0, 0)

def edge_strips(blocks):
    return jnp.stack([blocks[:, 0], blocks[:, -1], blocks[:, :, 0], blocks[:, :, -1]], axis=1)

def pad_tiles(blocks, fetched):
    top = jnp.concatenate([fetched[:, 4, -1:], fetched[:, 0], fetched[:, 5, :1]], axis=1)
    bottom = jnp.concatenate([fetched[:, 6, -1:], fetched[:, 1], fetched[:, 7, :1]], axis=1)
    middle = jnp.concatenate([fetched[:, 2][:, :, None], blocks, fetched[:, 3][:, :, None]], axis=2)
    return jnp.concatenate([top[:, None], middle, bottom[:, None]], axis=1)

def fetch_all(blocks, links):
    strips = edge_strips(blocks)
    count = strips.shape[0]
    flat_pool = strips.reshape(count * 4, strips.shape[2], strips.shape[3])
    which = jnp.array(STRIP_OF_DIRECTION, dtype=jnp.int32)
    lookup = jnp.clip(links, 0, count - 1) * 4 + which[None, :]
    fetched = jnp.take(flat_pool, lookup.astype(jnp.int32), axis=0)
    return jnp.where((links >= 0)[:, :, None, None], fetched, jnp.zeros_like(fetched))

def convolve(padded, kernel):
    return lax.conv_general_dilated(padded.astype(jnp.float32), kernel.astype(jnp.float32), (1, 1), 'VALID', dimension_numbers=('NHWC', 'HWIO', 'NHWC'), precision=lax.Precision.HIGHEST)

def flipped(kernel):
    return jnp.transpose(kernel[::-1, ::-1], (0, 1, 3, 2))

def weight_grad(padded, delta_field):
    side = delta_field.shape[1]
    terms = []
    for row_shift in range(3):
        for col_shift in range(3):
            window = padded[:, row_shift:row_shift + side, col_shift:col_shift + side].astype(jnp.float32)
            terms.append(jnp.einsum('nijc,nijo->co', window, delta_field.astype(jnp.float32), precision=lax.Precision.HIGHEST))
    stacked = jnp.stack(terms, axis=0)
    return stacked.reshape(3, 3, stacked.shape[1], stacked.shape[2])

def reference(slide_image, cotangent, weight_one, weight_two, tissue, neighbours):

    def one_slide(item):
        picture, upstream_in, present_in, links = item
        keep_mask = (present_in > 0)[:, None, None, None]
        inputs = jnp.where(keep_mask, picture.reshape(TILES, TS, TS, C), 0).astype(jnp.bfloat16)
        padded_in = pad_tiles(inputs, fetch_all(inputs, links))
        hidden = jnp.where(keep_mask, jax.nn.relu(convolve(padded_in, weight_one)), 0.0).astype(jnp.bfloat16)
        padded_hidden = pad_tiles(hidden, fetch_all(hidden, links))
        output = jnp.where(keep_mask, convolve(padded_hidden, weight_two), 0.0).astype(jnp.bfloat16)
        upstream = jnp.where(keep_mask, upstream_in.reshape(TILES, TS, TS, C), 0).astype(jnp.bfloat16)
        padded_up = pad_tiles(upstream, fetch_all(upstream, links))
        back_hidden = convolve(padded_up, flipped(weight_two))
        delta = jnp.where(hidden > 0, back_hidden, 0.0).astype(jnp.bfloat16)
        padded_delta = pad_tiles(delta, fetch_all(delta, links))
        grad_input = jnp.where(keep_mask, convolve(padded_delta, flipped(weight_one)), 0.0).astype(jnp.bfloat16)
        grad_two = weight_grad(padded_hidden, upstream)
        grad_one = weight_grad(padded_in, delta)
        return (output.reshape(TILES, TS, TS * C), grad_input.reshape(TILES, TS, TS * C), grad_one, grad_two)
    output, grad_input, grad_one, grad_two = lax.map(one_slide, (slide_image, cotangent, tissue, neighbours))
    return (output, grad_input, lax.optimization_barrier(jnp.sum(grad_one, axis=0)), lax.optimization_barrier(jnp.sum(grad_two, axis=0)))
```

```python
import functools

import jax
import jax.numpy as jnp
from jax import lax
from jax.experimental import pallas as pl
from jax.experimental.pallas import tpu as pltpu
from jax.sharding import PartitionSpec as P

F32 = jnp.float32
BF16 = jnp.bfloat16
LANES = 128
SMEM = pl.BlockSpec(memory_space=pltpu.SMEM)
VMEM = pl.BlockSpec(memory_space=pltpu.VMEM)


def pack_kernel(links_ref, image_ref, cotangent_ref, out_ref, strip_ref):
    slots, side, width = image_ref.shape
    pairs = width // LANES
    for slot in range(slots):
        for field, ref in enumerate((image_ref, cotangent_ref)):
            top = ref[slot, 0:16, :].astype(F32)
            bottom = ref[slot, side - 16 : side, :].astype(F32)
            for pair in range(pairs):
                lanes = slice(pair * LANES, (pair + 1) * LANES)
                rows = slice(2 * pair, 2 * pair + 2)
                strip_ref[slot, field, 0, rows, :] = top[0:2, lanes]
                strip_ref[slot, field, 1, rows, :] = bottom[14:16, lanes]
    for slot in range(slots):
        for direction in range(8):
            link = links_ref[slot, direction]

            @pl.when(link >= 0)
            def _(slot=slot, direction=direction, link=link):
                device = link // slots
                there = link % slots
                for field, ref in enumerate((image_ref, cotangent_ref)):
                    if direction < 2:
                        strip = strip_ref[slot, field, direction].astype(BF16)
                        out_ref[device, slot, there, field] = strip
                    elif direction == 2:
                        out_ref[device, slot, there, field] = ref[slot, :, 0:LANES]
                    elif direction == 3:
                        out_ref[device, slot, there, field] = ref[slot, :, width - LANES : width]
                    else:
                        which = 0 if direction < 6 else 1
                        first = 0 if direction % 2 == 0 else side - 16
                        corner = strip_ref[slot, field, which, first : first + 16, :]
                        out_ref[device, slot, there, field, 0:16, :] = corner.astype(BF16)


def mix_kernel(
    links_ref, tissue_ref, image_ref, cotangent_ref, halo_ref, one_ref, two_ref,
    output_ref, grad_input_ref, grads_ref,
    wide_in, wide_up, narrow_hidden, narrow_delta, own_delta,
    taps_in, taps_up, taps_hidden, taps_delta,
    forward_one, forward_two, back_one, back_two, acc_ref,
):
    slots, side, width = image_ref.shape
    pairs = width // LANES
    half = LANES // 2
    tall = side + 16

    zero = jnp.zeros((half, half), BF16)
    for source, forward, back in ((one_ref, forward_one, back_one), (two_ref, forward_two, back_two)):
        for a in range(3):
            taps = [source[a, b] for b in range(3)]
            left = jnp.concatenate(taps + [zero], axis=0)
            right = jnp.concatenate([zero] + taps, axis=0)
            forward[a * 256 : (a + 1) * 256, :] = jnp.concatenate([left, right], axis=1)
            turned = [source[2 - a, 2 - b] for b in range(3)]
            upper = jnp.concatenate(turned + [zero], axis=1)
            lower = jnp.concatenate([zero] + turned, axis=1)
            back[:, a * 256 : (a + 1) * 256] = jnp.concatenate([upper, lower], axis=0)

    for field, (ref, wide) in enumerate(((image_ref, wide_in), (cotangent_ref, wide_up))):
        wide[...] = jnp.zeros(wide.shape, F32)
        for slot in range(slots):
            present = tissue_ref[0, slot] > 0
            for pair in range(pairs):
                block = ref[slot, :, pair * LANES : (pair + 1) * LANES].astype(F32)
                wide[slot, pair + 1, 16 : 16 + side, :] = jnp.where(present, block, 0.0)
            for direction in range(8):
                link = links_ref[slot, direction]

                @pl.when(link >= 0)
                def _(slot=slot, direction=direction, link=link, field=field, wide=wide):
                    got = halo_ref[link // slots, link % slots, slot, field].astype(F32)
                    if direction == 2:
                        wide[slot, 0, 16 : 16 + side, :] = got
                    elif direction == 3:
                        wide[slot, pairs + 1, 16 : 16 + side, :] = got
                    else:
                        north = direction in (0, 4, 5)
                        row = 14 if north else 16 + side
                        if direction < 2:
                            for pair in range(pairs):
                                wide[slot, pair + 1, row : row + 2, :] = got[2 * pair : 2 * pair + 2, :]
                        else:
                            west = direction in (4, 6)
                            at = 14 if west else 0
                            column = 0 if west else pairs + 1
                            wide[slot, column, row : row + 2, :] = got[at : at + 2, :]

    def spread(field, taps, count, start, rows):
        def step(pair, carry):
            for slot in range(slots):
                for a in range(3):
                    block = field[slot, pair, start + a - 1 : start + a - 1 + rows, :].astype(BF16)
                    taps[slot, pair + 1, :, a * 256 : a * 256 + LANES] = block
                    taps[slot, pair, :, a * 256 + LANES : (a + 1) * 256] = block
            return carry

        lax.fori_loop(0, count, step, 0)

    spread(wide_in, taps_in, pairs + 2, 8, tall)
    spread(wide_up, taps_up, pairs + 2, 8, tall)

    row = lax.broadcasted_iota(jnp.int32, (tall, LANES), 0)
    lane = lax.broadcasted_iota(jnp.int32, (tall, LANES), 1)

    def column_mask(north, here, south):
        value = jnp.where(row == 7, north, jnp.where(row == 8 + side, south, here))
        return jnp.where((row >= 7) & (row <= 8 + side), value, 0)

    def across(taps, slot, count, rows):
        return taps[slot, 1 : count + 1].reshape(count * rows, 768)

    contract_last = (((1,), (1,)), ((), ()))
    for slot in range(slots):
        there = [(links_ref[slot, k] >= 0).astype(jnp.int32) for k in range(8)]
        own = tissue_ref[0, slot]
        middle = column_mask(there[0], own, there[1])
        west = jnp.where(lane < half, column_mask(there[4], there[2], there[6]), middle)
        east = jnp.where(lane < half, middle, column_mask(there[5], there[3], there[7]))
        inside = (row >= 8) & (row < 8 + side)

        first = jnp.dot(
            across(taps_in, slot, pairs + 1, tall), forward_one[...], preferred_element_type=F32
        )
        acc_ref[0] = first.reshape(pairs + 1, tall, LANES)
        second = lax.dot_general(
            across(taps_up, slot, pairs + 1, tall), back_two[...], contract_last,
            preferred_element_type=F32,
        )
        acc_ref[1] = second.reshape(pairs + 1, tall, LANES)

        def finish(pair, mask, own_mask, slot=slot):
            hidden = jnp.where(mask > 0, jnp.maximum(acc_ref[0, pair], 0.0), 0.0)
            hidden = hidden.astype(BF16).astype(F32)
            delta = jnp.where(hidden > 0, acc_ref[1, pair], 0.0)
            narrow_hidden[slot, pair] = hidden
            narrow_delta[slot, pair] = delta
            own_delta[slot, pair] = jnp.where(own_mask, delta, 0.0).astype(BF16)

        finish(0, west, inside & (lane >= half))
        finish(pairs, east, inside & (lane < half))

        def middle_step(pair, carry, middle=middle, inside=inside):
            finish(pair, middle, inside)
            return carry

        lax.fori_loop(1, pairs, middle_step, 0)

    spread(narrow_hidden, taps_hidden, pairs + 1, 8, side)
    spread(narrow_delta, taps_delta, pairs + 1, 8, side)

    first_grad = None
    second_grad = None
    contract_first = (((0,), (0,)), ((), ()))
    for slot in range(slots):
        out = jnp.dot(across(taps_hidden, slot, pairs, side), forward_two[...], preferred_element_type=F32)
        back = lax.dot_general(
            across(taps_delta, slot, pairs, side), back_one[...], contract_last, preferred_element_type=F32
        )
        for pair in range(pairs):
            lanes = slice(pair * LANES, (pair + 1) * LANES)
            rows = slice(pair * side, (pair + 1) * side)
            output_ref[slot, :, lanes] = out[rows].astype(BF16)
            grad_input_ref[slot, :, lanes] = back[rows].astype(BF16)
        upstream = wide_up[slot, 1 : pairs + 1, 16 : 16 + side, :].reshape(pairs * side, LANES)
        term_two = lax.dot_general(
            upstream.astype(BF16), across(taps_hidden, slot, pairs, side), contract_first,
            preferred_element_type=F32,
        )
        deltas = own_delta[slot].reshape((pairs + 1) * tall, LANES)
        term_one = lax.dot_general(
            deltas, across(taps_in, slot, pairs + 1, tall), contract_first, preferred_element_type=F32
        )
        first_grad = term_one if first_grad is None else first_grad + term_one
        second_grad = term_two if second_grad is None else second_grad + term_two

    total = grads_ref.shape[0]
    lane = lax.broadcasted_iota(jnp.int32, (192, LANES), 1)
    for a in range(3):
        lanes = slice(a * 256, (a + 1) * 256)
        one = first_grad[:, lanes].T
        two = second_grad[:, lanes].T
        left = one[0:192] + pltpu.roll(one[64:256], half, 1)
        right = pltpu.roll(two[0:192], half, 1) + two[64:256]
        grads_ref[a * 192 : (a + 1) * 192, :] = jnp.where(lane < half, left, right)
    if total > 576:
        grads_ref[576:total, :] = jnp.zeros((total - 576, LANES), F32)


def local(slide_image, cotangent, weight_one, weight_two, tissue, neighbours):
    devices_tile = lax.axis_size("tile")
    devices = devices_tile * lax.axis_size("slide")
    _, slots, side, width = slide_image.shape
    pairs = width // LANES
    tall = side + 16
    image, upstream = slide_image[0], cotangent[0]
    links = neighbours[0]
    packed = pl.pallas_call(
        pack_kernel,
        out_shape=jax.ShapeDtypeStruct((devices_tile, slots, slots, 2, 32, LANES), BF16),
        in_specs=[SMEM, VMEM, VMEM],
        out_specs=VMEM,
        scratch_shapes=[pltpu.VMEM((slots, 2, 2, 32, LANES), F32)],
        compiler_params=pltpu.CompilerParams(vmem_limit_bytes=48 * 2**20),
        name="pack",
    )(links, image, upstream)
    halo = lax.all_to_all(packed, "tile", 0, 0, tiled=True)

    chunk = -(-576 // devices)
    chunk = -(-chunk // 8) * 8
    total = chunk * devices
    output, grad_input, grads = pl.pallas_call(
        mix_kernel,
        out_shape=(
            jax.ShapeDtypeStruct((slots, side, width), BF16),
            jax.ShapeDtypeStruct((slots, side, width), BF16),
            jax.ShapeDtypeStruct((total, LANES), F32),
        ),
        in_specs=[SMEM, SMEM] + [VMEM] * 5,
        out_specs=(VMEM,) * 3,
        scratch_shapes=[
            pltpu.VMEM((slots, pairs + 2, side + 32, LANES), F32),
            pltpu.VMEM((slots, pairs + 2, side + 32, LANES), F32),
            pltpu.VMEM((slots, pairs + 1, tall, LANES), F32),
            pltpu.VMEM((slots, pairs + 1, tall, LANES), F32),
            pltpu.VMEM((slots, pairs + 1, tall, LANES), BF16),
            pltpu.VMEM((slots, pairs + 3, tall, 768), BF16),
            pltpu.VMEM((slots, pairs + 3, tall, 768), BF16),
            pltpu.VMEM((slots, pairs + 2, side, 768), BF16),
            pltpu.VMEM((slots, pairs + 2, side, 768), BF16),
            pltpu.VMEM((768, LANES), BF16),
            pltpu.VMEM((768, LANES), BF16),
            pltpu.VMEM((LANES, 768), BF16),
            pltpu.VMEM((LANES, 768), BF16),
            pltpu.VMEM((2, pairs + 1, tall, LANES), F32),
        ],
        compiler_params=pltpu.CompilerParams(vmem_limit_bytes=48 * 2**20),
        name="mix",
    )(links, tissue, image, upstream, halo, weight_one, weight_two)

    parts = lax.all_to_all(grads.reshape(devices, chunk, LANES), ("slide", "tile"), 0, 0, tiled=True)
    mine = jnp.sum(parts, axis=0)
    whole = lax.all_gather(mine, ("slide", "tile"), axis=0, tiled=True)[:576]
    shape = weight_one.shape
    return (
        output[None],
        grad_input[None],
        whole[:, : LANES // 2].reshape(shape),
        whole[:, LANES // 2 :].reshape(shape),
    )


def solution(mesh):
    placed = (
        P("slide", "tile", None, None),
        P("slide", "tile", None, None),
        P(),
        P(),
        P("slide", "tile"),
        P("slide", "tile", None),
    )
    return jax.shard_map(
        local,
        mesh=mesh,
        in_specs=placed,
        out_specs=(P("slide", "tile", None, None), P("slide", "tile", None, None), P(), P()),
        check_vma=False,
    )
```

```python
import functools

import jax
import jax.numpy as jnp
from jax import lax
from jax.experimental import pallas as pl
from jax.experimental.pallas import tpu as pltpu
from jax.sharding import PartitionSpec as P

F32 = jnp.float32
BF16 = jnp.bfloat16
LANES = 128
SMEM = pl.BlockSpec(memory_space=pltpu.SMEM)
VMEM = pl.BlockSpec(memory_space=pltpu.VMEM)


CORNERS = 192
BLOCK = CORNERS + 16


def strip_row(field, slot):
    return field * 96 + slot * 32


def column_row(field):
    return field * 96 + 64


def corner_row(field, slot, there):
    return 2 * ((field * 2 + slot) * 2 + there)


def pack_kernel(links_ref, image_ref, cotangent_ref, out_ref, strip_ref, corner_ref):
    slots, side, width = image_ref.shape
    pairs = width // LANES
    me = lax.axis_index("tile")
    for slot in range(slots):
        for field, ref in enumerate((image_ref, cotangent_ref)):
            top = ref[slot, 0:16, :].astype(F32)
            bottom = ref[slot, side - 16 : side, :].astype(F32)
            for pair in range(pairs):
                lanes = slice(pair * LANES, (pair + 1) * LANES)
                rows = slice(2 * pair, 2 * pair + 2)
                strip_ref[slot, field, 0, rows, :] = top[0:2, lanes]
                strip_ref[slot, field, 1, rows, :] = bottom[14:16, lanes]
    for slot in range(slots):
        for direction in range(8):
            link = links_ref[slot, direction]

            @pl.when(link >= 0)
            def _(slot=slot, direction=direction, link=link):
                device = link // slots
                there = link % slots
                for field, ref in enumerate((image_ref, cotangent_ref)):
                    if direction < 2:
                        rows = slice(strip_row(field, slot), strip_row(field, slot) + 32)
                        out_ref[device, rows, :] = strip_ref[slot, field, direction].astype(BF16)
                    elif direction < 4:
                        first = jnp.where(device == me, strip_row(field, slot), column_row(field))
                        lanes = slice(0, LANES) if direction == 2 else slice(width - LANES, width)
                        out_ref[device, pl.ds(pl.multiple_of(first, 32), 32), :] = ref[slot, :, lanes]
                    else:
                        which = 0 if direction < 6 else 1
                        first = 0 if direction % 2 == 0 else side - 2
                        corner = strip_ref[slot, field, which, first : first + 2, :]
                        for target in range(slots):
                            row = corner_row(field, slot, target)

                            @pl.when(there == target)
                            def _(row=row, corner=corner):
                                corner_ref[device, row : row + 2, :] = corner

    def place(device, carry):
        out_ref[device, CORNERS:BLOCK, :] = corner_ref[device].astype(BF16)
        return carry

    lax.fori_loop(0, out_ref.shape[0], place, 0)


def mix_kernel(
    links_ref, tissue_ref, image_ref, cotangent_ref, halo_ref, one_ref, two_ref,
    output_ref, grad_input_ref, grads_ref,
    wide_in, wide_up, narrow_hidden, narrow_delta, own_delta,
    taps_in, taps_up, taps_hidden, taps_delta,
    forward_one, forward_two, back_one, back_two, acc_ref,
):
    slots, side, width = image_ref.shape
    pairs = width // LANES
    half = LANES // 2
    tall = side + 16
    me = lax.axis_index("tile")

    zero = jnp.zeros((half, half), BF16)
    for source, forward, back in ((one_ref, forward_one, back_one), (two_ref, forward_two, back_two)):
        for a in range(3):
            taps = [source[a, b] for b in range(3)]
            left = jnp.concatenate(taps + [zero], axis=0)
            right = jnp.concatenate([zero] + taps, axis=0)
            forward[a * 256 : (a + 1) * 256, :] = jnp.concatenate([left, right], axis=1)
            turned = [source[2 - a, 2 - b] for b in range(3)]
            upper = jnp.concatenate(turned + [zero], axis=1)
            lower = jnp.concatenate([zero] + turned, axis=1)
            back[:, a * 256 : (a + 1) * 256] = jnp.concatenate([upper, lower], axis=0)

    for field, (ref, wide) in enumerate(((image_ref, wide_in), (cotangent_ref, wide_up))):
        wide[...] = jnp.zeros(wide.shape, F32)
        for slot in range(slots):
            present = tissue_ref[0, slot] > 0
            for pair in range(pairs):
                block = ref[slot, :, pair * LANES : (pair + 1) * LANES].astype(F32)
                wide[slot, pair + 1, 16 : 16 + side, :] = jnp.where(present, block, 0.0)
            for direction in range(8):
                link = links_ref[slot, direction]

                @pl.when(link >= 0)
                def _(slot=slot, direction=direction, link=link, field=field, wide=wide):
                    device, there = link // slots, link % slots
                    if direction in (2, 3):
                        column = 0 if direction == 2 else pairs + 1
                        at_home = strip_row(field, 0) + there * 32
                        first = pl.multiple_of(jnp.where(device == me, at_home, column_row(field)), 32)
                        got = halo_ref[device, pl.ds(first, 32), :].astype(F32)
                        wide[slot, column, 16 : 16 + side, :] = got
                    else:
                        row = 14 if direction in (0, 4, 5) else 16 + side
                        if direction < 2:
                            at = pl.multiple_of(strip_row(field, 0) + there * 32, 32)
                            got = halo_ref[device, pl.ds(at, 32), :].astype(F32)
                            for pair in range(pairs):
                                wide[slot, pair + 1, row : row + 2, :] = got[2 * pair : 2 * pair + 2, :]
                        else:
                            column = 0 if direction in (4, 6) else pairs + 1
                            got = halo_ref[device, CORNERS:BLOCK, :].astype(F32)
                            one, two = (corner_row(field, k, slot) for k in range(2))
                            corner = jnp.where(there == 0, got[one : one + 2], got[two : two + 2])
                            wide[slot, column, row : row + 2, :] = corner

    def spread(field, taps, count, start, rows):
        def step(pair, carry):
            for slot in range(slots):
                for a in range(3):
                    block = field[slot, pair, start + a - 1 : start + a - 1 + rows, :].astype(BF16)
                    taps[slot, pair + 1, :, a * 256 : a * 256 + LANES] = block
                    taps[slot, pair, :, a * 256 + LANES : (a + 1) * 256] = block
            return carry

        lax.fori_loop(0, count, step, 0)

    spread(wide_in, taps_in, pairs + 2, 8, tall)
    spread(wide_up, taps_up, pairs + 2, 8, tall)

    row = lax.broadcasted_iota(jnp.int32, (tall, LANES), 0)
    lane = lax.broadcasted_iota(jnp.int32, (tall, LANES), 1)

    def column_mask(north, here, south):
        value = jnp.where(row == 7, north, jnp.where(row == 8 + side, south, here))
        return jnp.where((row >= 7) & (row <= 8 + side), value, 0)

    def across(taps, slot, count, rows):
        return taps[slot, 1 : count + 1].reshape(count * rows, 768)

    contract_last = (((1,), (1,)), ((), ()))
    for slot in range(slots):
        there = [(links_ref[slot, k] >= 0).astype(jnp.int32) for k in range(8)]
        own = tissue_ref[0, slot]
        middle = column_mask(there[0], own, there[1])
        west = jnp.where(lane < half, column_mask(there[4], there[2], there[6]), middle)
        east = jnp.where(lane < half, middle, column_mask(there[5], there[3], there[7]))
        inside = (row >= 8) & (row < 8 + side)

        first = jnp.dot(
            across(taps_in, slot, pairs + 1, tall), forward_one[...], preferred_element_type=F32
        )
        acc_ref[0] = first.reshape(pairs + 1, tall, LANES)
        second = lax.dot_general(
            across(taps_up, slot, pairs + 1, tall), back_two[...], contract_last,
            preferred_element_type=F32,
        )
        acc_ref[1] = second.reshape(pairs + 1, tall, LANES)

        def finish(pair, mask, own_mask, slot=slot):
            hidden = jnp.where(mask > 0, jnp.maximum(acc_ref[0, pair], 0.0), 0.0)
            hidden = hidden.astype(BF16).astype(F32)
            delta = jnp.where(hidden > 0, acc_ref[1, pair], 0.0)
            narrow_hidden[slot, pair] = hidden
            narrow_delta[slot, pair] = delta
            own_delta[slot, pair] = jnp.where(own_mask, delta, 0.0).astype(BF16)

        finish(0, west, inside & (lane >= half))
        finish(pairs, east, inside & (lane < half))

        def middle_step(pair, carry, middle=middle, inside=inside):
            finish(pair, middle, inside)
            return carry

        lax.fori_loop(1, pairs, middle_step, 0)

    spread(narrow_hidden, taps_hidden, pairs + 1, 8, side)
    spread(narrow_delta, taps_delta, pairs + 1, 8, side)

    first_grad = None
    second_grad = None
    contract_first = (((0,), (0,)), ((), ()))
    for slot in range(slots):
        out = jnp.dot(across(taps_hidden, slot, pairs, side), forward_two[...], preferred_element_type=F32)
        back = lax.dot_general(
            across(taps_delta, slot, pairs, side), back_one[...], contract_last, preferred_element_type=F32
        )
        for pair in range(pairs):
            lanes = slice(pair * LANES, (pair + 1) * LANES)
            rows = slice(pair * side, (pair + 1) * side)
            output_ref[slot, :, lanes] = out[rows].astype(BF16)
            grad_input_ref[slot, :, lanes] = back[rows].astype(BF16)
        upstream = wide_up[slot, 1 : pairs + 1, 16 : 16 + side, :].reshape(pairs * side, LANES)
        term_two = lax.dot_general(
            upstream.astype(BF16), across(taps_hidden, slot, pairs, side), contract_first,
            preferred_element_type=F32,
        )
        deltas = own_delta[slot].reshape((pairs + 1) * tall, LANES)
        term_one = lax.dot_general(
            deltas, across(taps_in, slot, pairs + 1, tall), contract_first, preferred_element_type=F32
        )
        first_grad = term_one if first_grad is None else first_grad + term_one
        second_grad = term_two if second_grad is None else second_grad + term_two

    total = grads_ref.shape[0]
    lane = lax.broadcasted_iota(jnp.int32, (192, LANES), 1)
    for a in range(3):
        lanes = slice(a * 256, (a + 1) * 256)
        one = first_grad[:, lanes].T
        two = second_grad[:, lanes].T
        left = one[0:192] + pltpu.roll(one[64:256], half, 1)
        right = pltpu.roll(two[0:192], half, 1) + two[64:256]
        grads_ref[a * 192 : (a + 1) * 192, :] = jnp.where(lane < half, left, right).astype(BF16)
    if total > 576:
        grads_ref[576:total, :] = jnp.zeros((total - 576, LANES), BF16)


def sum_kernel(parts_ref, sums_ref):
    total = jnp.sum(parts_ref[...].astype(F32), axis=0).astype(BF16)
    sums_ref[...] = jnp.broadcast_to(total[None], sums_ref.shape)


def split_kernel(whole_ref, one_ref, two_ref):
    chunk = whole_ref.shape[1]
    rows, half = one_ref.shape
    for part in range(rows // chunk):
        block = whole_ref[part].astype(F32)
        one_ref[part * chunk : (part + 1) * chunk, :] = block[:, :half]
        two_ref[part * chunk : (part + 1) * chunk, :] = block[:, half:]


def local(slide_image, cotangent, weight_one, weight_two, tissue, neighbours):
    devices_tile = lax.axis_size("tile")
    devices = devices_tile * lax.axis_size("slide")
    _, slots, side, width = slide_image.shape
    pairs = width // LANES
    tall = side + 16
    image, upstream = slide_image[0], cotangent[0]
    links = neighbours[0]
    packed = pl.pallas_call(
        pack_kernel,
        out_shape=jax.ShapeDtypeStruct((devices_tile, BLOCK, LANES), BF16),
        in_specs=[SMEM, VMEM, VMEM],
        out_specs=VMEM,
        scratch_shapes=[
            pltpu.VMEM((slots, 2, 2, 32, LANES), F32),
            pltpu.VMEM((devices_tile, 16, LANES), F32),
        ],
        compiler_params=pltpu.CompilerParams(vmem_limit_bytes=48 * 2**20),
        name="pack",
    )(links, image, upstream)
    halo = lax.all_to_all(packed, "tile", 0, 0, tiled=True)

    chunk = -(-576 // devices)
    chunk = -(-chunk // 8) * 8
    total = chunk * devices
    output, grad_input, grads = pl.pallas_call(
        mix_kernel,
        out_shape=(
            jax.ShapeDtypeStruct((slots, side, width), BF16),
            jax.ShapeDtypeStruct((slots, side, width), BF16),
            jax.ShapeDtypeStruct((total, LANES), BF16),
        ),
        in_specs=[SMEM, SMEM] + [VMEM] * 5,
        out_specs=(VMEM,) * 3,
        scratch_shapes=[
            pltpu.VMEM((slots, pairs + 2, side + 32, LANES), F32),
            pltpu.VMEM((slots, pairs + 2, side + 32, LANES), F32),
            pltpu.VMEM((slots, pairs + 1, tall, LANES), F32),
            pltpu.VMEM((slots, pairs + 1, tall, LANES), F32),
            pltpu.VMEM((slots, pairs + 1, tall, LANES), BF16),
            pltpu.VMEM((slots, pairs + 3, tall, 768), BF16),
            pltpu.VMEM((slots, pairs + 3, tall, 768), BF16),
            pltpu.VMEM((slots, pairs + 2, side, 768), BF16),
            pltpu.VMEM((slots, pairs + 2, side, 768), BF16),
            pltpu.VMEM((768, LANES), BF16),
            pltpu.VMEM((768, LANES), BF16),
            pltpu.VMEM((LANES, 768), BF16),
            pltpu.VMEM((LANES, 768), BF16),
            pltpu.VMEM((2, pairs + 1, tall, LANES), F32),
        ],
        compiler_params=pltpu.CompilerParams(vmem_limit_bytes=48 * 2**20),
        name="mix",
    )(links, tissue, image, upstream, halo, weight_one, weight_two)

    parts = lax.all_to_all(grads.reshape(devices, chunk, LANES), ("slide", "tile"), 0, 0, tiled=True)
    sums = pl.pallas_call(
        sum_kernel,
        out_shape=jax.ShapeDtypeStruct(parts.shape, BF16),
        in_specs=[VMEM],
        out_specs=VMEM,
        name="sum",
    )(parts)
    whole = lax.all_to_all(sums, ("slide", "tile"), 0, 0, tiled=True)
    grad_one, grad_two = pl.pallas_call(
        split_kernel,
        out_shape=(jax.ShapeDtypeStruct((576, LANES // 2), F32),) * 2,
        in_specs=[VMEM],
        out_specs=(VMEM, VMEM),
        name="split",
    )(whole)
    shape = weight_one.shape
    return output[None], grad_input[None], grad_one.reshape(shape), grad_two.reshape(shape)


def solution(mesh):
    placed = (
        P("slide", "tile", None, None),
        P("slide", "tile", None, None),
        P(),
        P(),
        P("slide", "tile"),
        P("slide", "tile", None),
    )
    return jax.shard_map(
        local,
        mesh=mesh,
        in_specs=placed,
        out_specs=(P("slide", "tile", None, None), P("slide", "tile", None, None), P(), P()),
        check_vma=False,
    )
```

```python
import functools

import jax
import jax.numpy as jnp
from jax import lax
from jax.experimental import pallas as pl
from jax.experimental.pallas import tpu as pltpu
from jax.sharding import PartitionSpec as P

F32 = jnp.float32
BF16 = jnp.bfloat16
LANES = 128
SMEM = pl.BlockSpec(memory_space=pltpu.SMEM)
VMEM = pl.BlockSpec(memory_space=pltpu.VMEM)
ANY = pl.BlockSpec(memory_space=pl.ANY)
PACK_LIMIT = 60 * 2**20


CORNERS = 192
BLOCK = CORNERS + 16


def strip_row(field, slot):
    return field * 96 + slot * 32


def column_row(field):
    return field * 96 + 64


def corner_row(field, slot, there):
    return 2 * ((field * 2 + slot) * 2 + there)


def band_weights(source, forward, back):
    half = LANES // 2
    zero = jnp.zeros((half, half), BF16)
    for a in range(3):
        taps = [source[a, b] for b in range(3)]
        left = jnp.concatenate(taps + [zero], axis=0)
        right = jnp.concatenate([zero] + taps, axis=0)
        forward[a * 256 : (a + 1) * 256, :] = jnp.concatenate([left, right], axis=1)
        turned = [source[2 - a, 2 - b] for b in range(3)]
        upper = jnp.concatenate(turned + [zero], axis=1)
        lower = jnp.concatenate([zero] + turned, axis=1)
        back[:, a * 256 : (a + 1) * 256] = jnp.concatenate([upper, lower], axis=0)


def pack_kernel(
    links_hbm, image_hbm, cotangent_hbm, out_ref,
    links_ref, image_ref, cotangent_ref, strip_ref, corner_ref, sems,
):
    sources = (links_hbm, image_hbm, cotangent_hbm)
    targets = (links_ref, image_ref, cotangent_ref)
    copies = [
        pltpu.make_async_copy(source, target, sems.at[k])
        for k, (source, target) in enumerate(zip(sources, targets))
    ]
    for copy in copies:
        copy.start()
    for copy in copies:
        copy.wait()
    slots, side, width = image_ref.shape
    pairs = width // LANES
    me = lax.axis_index("tile")
    for slot in range(slots):
        for field, ref in enumerate((image_ref, cotangent_ref)):
            top = ref[slot, 0:16, :].astype(F32)
            bottom = ref[slot, side - 16 : side, :].astype(F32)
            for pair in range(pairs):
                lanes = slice(pair * LANES, (pair + 1) * LANES)
                rows = slice(2 * pair, 2 * pair + 2)
                strip_ref[slot, field, 0, rows, :] = top[0:2, lanes]
                strip_ref[slot, field, 1, rows, :] = bottom[14:16, lanes]
    for slot in range(slots):
        for direction in range(8):
            link = links_ref[slot, direction]

            @pl.when(link >= 0)
            def _(slot=slot, direction=direction, link=link):
                device = link // slots
                there = link % slots
                for field, ref in enumerate((image_ref, cotangent_ref)):
                    if direction < 2:
                        rows = slice(strip_row(field, slot), strip_row(field, slot) + 32)
                        out_ref[device, rows, :] = strip_ref[slot, field, direction].astype(BF16)
                    elif direction < 4:
                        first = jnp.where(device == me, strip_row(field, slot), column_row(field))
                        lanes = slice(0, LANES) if direction == 2 else slice(width - LANES, width)
                        out_ref[device, pl.ds(pl.multiple_of(first, 32), 32), :] = ref[slot, :, lanes]
                    else:
                        which = 0 if direction < 6 else 1
                        first = 0 if direction % 2 == 0 else side - 2
                        corner = strip_ref[slot, field, which, first : first + 2, :]
                        for target in range(slots):
                            row = corner_row(field, slot, target)

                            @pl.when(there == target)
                            def _(row=row, corner=corner):
                                corner_ref[device, row : row + 2, :] = corner

    def place(device, carry):
        out_ref[device, CORNERS:BLOCK, :] = corner_ref[device].astype(BF16)
        return carry

    lax.fori_loop(0, out_ref.shape[0], place, 0)


def mix_kernel(
    links_ref, tissue_ref, image_ref, cotangent_ref, halo_ref, one_ref, two_ref,
    output_hbm, grad_input_hbm, grads_ref,
    wide_in, wide_up, narrow_hidden, narrow_delta, own_delta,
    taps_in, taps_up, taps_hidden, taps_delta, forward_ref, back_ref, acc_ref, output_ref, grad_input_ref, sems,
):
    slots, side, width = image_ref.shape
    pairs = width // LANES
    half = LANES // 2
    tall = side + 16
    me = lax.axis_index("tile")

    band_weights(one_ref, forward_ref.at[0], back_ref.at[0])
    band_weights(two_ref, forward_ref.at[1], back_ref.at[1])

    for field, (ref, wide) in enumerate(((image_ref, wide_in), (cotangent_ref, wide_up))):
        wide[:, :, 0:16, :] = jnp.zeros((slots, pairs + 2, 16, LANES), F32)
        wide[:, :, 16 + side : 32 + side, :] = jnp.zeros((slots, pairs + 2, 16, LANES), F32)
        for column in (0, pairs + 1):
            wide[:, column, 16 : 16 + side, :] = jnp.zeros((slots, side, LANES), F32)
        for slot in range(slots):
            present = tissue_ref[0, slot] > 0
            for pair in range(pairs):
                block = ref[slot, :, pair * LANES : (pair + 1) * LANES].astype(F32)
                wide[slot, pair + 1, 16 : 16 + side, :] = jnp.where(present, block, 0.0)
            for direction in range(8):
                link = links_ref[slot, direction]

                @pl.when(link >= 0)
                def _(slot=slot, direction=direction, link=link, field=field, wide=wide):
                    device, there = link // slots, link % slots
                    if direction in (2, 3):
                        column = 0 if direction == 2 else pairs + 1
                        at_home = strip_row(field, 0) + there * 32
                        first = pl.multiple_of(jnp.where(device == me, at_home, column_row(field)), 32)
                        got = halo_ref[device, pl.ds(first, 32), :].astype(F32)
                        wide[slot, column, 16 : 16 + side, :] = got
                    else:
                        row = 14 if direction in (0, 4, 5) else 16 + side
                        if direction < 2:
                            at = pl.multiple_of(strip_row(field, 0) + there * 32, 32)
                            got = halo_ref[device, pl.ds(at, 32), :].astype(F32)
                            for pair in range(pairs):
                                wide[slot, pair + 1, row : row + 2, :] = got[2 * pair : 2 * pair + 2, :]
                        else:
                            column = 0 if direction in (4, 6) else pairs + 1
                            got = halo_ref[device, CORNERS:BLOCK, :].astype(F32)
                            one, two = (corner_row(field, k, slot) for k in range(2))
                            corner = jnp.where(there == 0, got[one : one + 2], got[two : two + 2])
                            wide[slot, column, row : row + 2, :] = corner

    def spread(field, taps, count, start, rows):
        def step(pair, carry):
            for slot in range(slots):
                for a in range(3):
                    block = field[slot, pair, start + a - 1 : start + a - 1 + rows, :].astype(BF16)
                    taps[slot, pair + 1, :, a * 256 : a * 256 + LANES] = block
                    taps[slot, pair, :, a * 256 + LANES : (a + 1) * 256] = block
            return carry

        lax.fori_loop(0, count, step, 0, unroll=True)

    spread(wide_in, taps_in, pairs + 2, 8, tall)
    spread(wide_up, taps_up, pairs + 2, 8, tall)

    row = lax.broadcasted_iota(jnp.int32, (tall, LANES), 0)
    lane = lax.broadcasted_iota(jnp.int32, (tall, LANES), 1)

    def column_mask(north, here, south):
        value = jnp.where(row == 7, north, jnp.where(row == 8 + side, south, here))
        return jnp.where((row >= 7) & (row <= 8 + side), value, 0)

    def across(taps, slot, count, rows):
        return taps[slot, 1 : count + 1].reshape(count * rows, 768)

    contract_last = (((1,), (1,)), ((), ()))
    for slot in range(slots):
        there = [(links_ref[slot, k] >= 0).astype(jnp.int32) for k in range(8)]
        own = tissue_ref[0, slot]
        middle = column_mask(there[0], own, there[1])
        west = jnp.where(lane < half, column_mask(there[4], there[2], there[6]), middle)
        east = jnp.where(lane < half, middle, column_mask(there[5], there[3], there[7]))
        inside = (row >= 8) & (row < 8 + side)

        first = jnp.dot(
            across(taps_in, slot, pairs + 1, tall), forward_ref[0], preferred_element_type=F32
        )
        acc_ref[0] = first.reshape(pairs + 1, tall, LANES)
        second = lax.dot_general(
            across(taps_up, slot, pairs + 1, tall), back_ref[1], contract_last,
            preferred_element_type=F32,
        )
        acc_ref[1] = second.reshape(pairs + 1, tall, LANES)

        def finish(pair, mask, own_mask, slot=slot):
            hidden = jnp.where(mask > 0, jnp.maximum(acc_ref[0, pair], 0.0), 0.0)
            hidden = hidden.astype(BF16).astype(F32)
            delta = jnp.where(hidden > 0, acc_ref[1, pair], 0.0)
            narrow_hidden[slot, pair] = hidden
            narrow_delta[slot, pair] = delta
            own_delta[slot, pair] = jnp.where(own_mask, delta, 0.0).astype(BF16)

        finish(0, west, inside & (lane >= half))
        finish(pairs, east, inside & (lane < half))

        def middle_step(pair, carry, middle=middle, inside=inside):
            finish(pair, middle, inside)
            return carry

        lax.fori_loop(1, pairs, middle_step, 0, unroll=True)

    spread(narrow_hidden, taps_hidden, pairs + 1, 8, side)
    spread(narrow_delta, taps_delta, pairs + 1, 8, side)

    first_grad = None
    second_grad = None
    copies = []
    contract_first = (((0,), (0,)), ((), ()))
    for slot in range(slots):
        out = jnp.dot(across(taps_hidden, slot, pairs, side), forward_ref[1], preferred_element_type=F32)
        back = lax.dot_general(
            across(taps_delta, slot, pairs, side), back_ref[0], contract_last, preferred_element_type=F32
        )
        for pair in range(pairs):
            lanes = slice(pair * LANES, (pair + 1) * LANES)
            rows = slice(pair * side, (pair + 1) * side)
            output_ref[slot, :, lanes] = out[rows].astype(BF16)
            grad_input_ref[slot, :, lanes] = back[rows].astype(BF16)
        for k, (source, target) in enumerate(((output_ref, output_hbm), (grad_input_ref, grad_input_hbm))):
            copies.append(pltpu.make_async_copy(source.at[slot], target.at[slot], sems.at[2 * slot + k]))
            copies[-1].start()
    for slot in range(slots):
        upstream = wide_up[slot, 1 : pairs + 1, 16 : 16 + side, :].reshape(pairs * side, LANES)
        term_two = lax.dot_general(
            upstream.astype(BF16), across(taps_hidden, slot, pairs, side), contract_first,
            preferred_element_type=F32,
        )
        deltas = own_delta[slot].reshape((pairs + 1) * tall, LANES)
        term_one = lax.dot_general(
            deltas, across(taps_in, slot, pairs + 1, tall), contract_first, preferred_element_type=F32
        )
        first_grad = term_one if first_grad is None else first_grad + term_one
        second_grad = term_two if second_grad is None else second_grad + term_two

    total = grads_ref.shape[0]
    lane = lax.broadcasted_iota(jnp.int32, (192, LANES), 1)
    for a in range(3):
        lanes = slice(a * 256, (a + 1) * 256)
        one = first_grad[:, lanes].T
        two = second_grad[:, lanes].T
        left = one[0:192] + pltpu.roll(one[64:256], half, 1)
        right = pltpu.roll(two[0:192], half, 1) + two[64:256]
        grads_ref[a * 192 : (a + 1) * 192, :] = jnp.where(lane < half, left, right).astype(BF16)
    if total > 576:
        grads_ref[576:total, :] = jnp.zeros((total - 576, LANES), BF16)
    for copy in copies:
        copy.wait()


def sum_kernel(parts_ref, sums_ref):
    total = parts_ref[0].astype(F32)
    for part in range(1, parts_ref.shape[0]):
        total += parts_ref[part].astype(F32)
    total = total.astype(BF16)
    for part in range(parts_ref.shape[0]):
        sums_ref[part] = total


def split_kernel(whole_ref, one_ref, two_ref):
    chunk = whole_ref.shape[1]
    rows, half = one_ref.shape
    for part in range(rows // chunk):
        block = whole_ref[part].astype(F32)
        one_ref[part * chunk : (part + 1) * chunk, :] = block[:, :half]
        two_ref[part * chunk : (part + 1) * chunk, :] = block[:, half:]


def local(slide_image, cotangent, weight_one, weight_two, tissue, neighbours):
    devices_tile = lax.axis_size("tile")
    devices = devices_tile * lax.axis_size("slide")
    _, slots, side, width = slide_image.shape
    pairs = width // LANES
    tall = side + 16
    image, upstream = slide_image[0], cotangent[0]
    links = neighbours[0]
    packed = pl.pallas_call(
        pack_kernel,
        out_shape=jax.ShapeDtypeStruct((devices_tile, BLOCK, LANES), BF16),
        in_specs=[ANY] * 3,
        out_specs=VMEM,
        scratch_shapes=[
            pltpu.SMEM(links.shape, jnp.int32),
            pltpu.VMEM(image.shape, BF16),
            pltpu.VMEM(image.shape, BF16),
            pltpu.VMEM((slots, 2, 2, 32, LANES), F32),
            pltpu.VMEM((devices_tile, 16, LANES), F32),
            pltpu.SemaphoreType.DMA((3,)),
        ],
        compiler_params=pltpu.CompilerParams(vmem_limit_bytes=PACK_LIMIT),
        name="pack",
    )(links, image, upstream)
    halo = lax.all_to_all(packed, "tile", 0, 0, tiled=True)

    chunk = -(-576 // devices)
    chunk = -(-chunk // 8) * 8
    total = chunk * devices
    output, grad_input, grads = pl.pallas_call(
        mix_kernel,
        out_shape=(
            jax.ShapeDtypeStruct((slots, side, width), BF16),
            jax.ShapeDtypeStruct((slots, side, width), BF16),
            jax.ShapeDtypeStruct((total, LANES), BF16),
        ),
        in_specs=[SMEM, SMEM] + [VMEM] * 5,
        out_specs=(ANY, ANY, VMEM),
        scratch_shapes=[
            pltpu.VMEM((slots, pairs + 2, side + 32, LANES), F32),
            pltpu.VMEM((slots, pairs + 2, side + 32, LANES), F32),
            pltpu.VMEM((slots, pairs + 1, tall, LANES), F32),
            pltpu.VMEM((slots, pairs + 1, tall, LANES), F32),
            pltpu.VMEM((slots, pairs + 1, tall, LANES), BF16),
            pltpu.VMEM((slots, pairs + 3, tall, 768), BF16),
            pltpu.VMEM((slots, pairs + 3, tall, 768), BF16),
            pltpu.VMEM((slots, pairs + 2, side, 768), BF16),
            pltpu.VMEM((slots, pairs + 2, side, 768), BF16),
            pltpu.VMEM((2, 768, LANES), BF16),
            pltpu.VMEM((2, LANES, 768), BF16),
            pltpu.VMEM((2, pairs + 1, tall, LANES), F32),
            pltpu.VMEM((slots, side, width), BF16),
            pltpu.VMEM((slots, side, width), BF16),
            pltpu.SemaphoreType.DMA((2 * slots,)),
        ],
        compiler_params=pltpu.CompilerParams(vmem_limit_bytes=48 * 2**20),
        name="mix",
    )(links, tissue, image, upstream, halo, weight_one, weight_two)

    parts = lax.all_to_all(grads.reshape(devices, chunk, LANES), ("slide", "tile"), 0, 0, tiled=True)
    sums = pl.pallas_call(
        sum_kernel,
        out_shape=jax.ShapeDtypeStruct(parts.shape, BF16),
        in_specs=[VMEM],
        out_specs=VMEM,
        name="sum",
    )(parts)
    whole = lax.all_to_all(sums, ("slide", "tile"), 0, 0, tiled=True)
    grad_one, grad_two = pl.pallas_call(
        split_kernel,
        out_shape=(jax.ShapeDtypeStruct((576, LANES // 2), F32),) * 2,
        in_specs=[VMEM],
        out_specs=(VMEM, VMEM),
        name="split",
    )(whole)
    shape = weight_one.shape
    return output[None], grad_input[None], grad_one.reshape(shape), grad_two.reshape(shape)


def solution(mesh):
    placed = (
        P("slide", "tile", None, None),
        P("slide", "tile", None, None),
        P(),
        P(),
        P("slide", "tile"),
        P("slide", "tile", None),
    )
    return jax.shard_map(
        local,
        mesh=mesh,
        in_specs=placed,
        out_specs=(P("slide", "tile", None, None), P("slide", "tile", None, None), P(), P()),
        check_vma=False,
    )
```

```python
import functools

import jax
import jax.numpy as jnp
from jax import lax
from jax.experimental import pallas as pl
from jax.experimental.pallas import tpu as pltpu
from jax.sharding import PartitionSpec as P

F32 = jnp.float32
BF16 = jnp.bfloat16
LANES = 128
SMEM = pl.BlockSpec(memory_space=pltpu.SMEM)
VMEM = pl.BlockSpec(memory_space=pltpu.VMEM)
ANY = pl.BlockSpec(memory_space=pl.ANY)
PACK_LIMIT = 60 * 2**20


CORNERS = 192
BLOCK = CORNERS + 16


def strip_row(field, slot):
    return field * 96 + slot * 32


def column_row(field):
    return field * 96 + 64


def corner_row(field, slot, there):
    return 2 * ((field * 2 + slot) * 2 + there)


def band_weights(source, forward, back):
    half = LANES // 2
    zero = jnp.zeros((half, half), BF16)
    for a in range(3):
        taps = [source[a, b] for b in range(3)]
        left = jnp.concatenate(taps + [zero], axis=0)
        right = jnp.concatenate([zero] + taps, axis=0)
        forward[a * 256 : (a + 1) * 256, :] = jnp.concatenate([left, right], axis=1)
        turned = [source[2 - a, 2 - b] for b in range(3)]
        upper = jnp.concatenate(turned + [zero], axis=1)
        lower = jnp.concatenate([zero] + turned, axis=1)
        back[:, a * 256 : (a + 1) * 256] = jnp.concatenate([upper, lower], axis=0)


def pack_kernel(
    links_hbm, image_hbm, cotangent_hbm, out_ref,
    links_ref, image_ref, cotangent_ref, strip_ref, corner_ref, sems,
):
    sources = (links_hbm, image_hbm, cotangent_hbm)
    targets = (links_ref, image_ref, cotangent_ref)
    copies = [
        pltpu.make_async_copy(source, target, sems.at[k])
        for k, (source, target) in enumerate(zip(sources, targets))
    ]
    for copy in copies:
        copy.start()
    for copy in copies:
        copy.wait()
    slots, side, width = image_ref.shape
    pairs = width // LANES
    me = lax.axis_index("tile")
    for slot in range(slots):
        for field, ref in enumerate((image_ref, cotangent_ref)):
            top = ref[slot, 0:16, :].astype(F32)
            bottom = ref[slot, side - 16 : side, :].astype(F32)
            for pair in range(pairs):
                lanes = slice(pair * LANES, (pair + 1) * LANES)
                rows = slice(2 * pair, 2 * pair + 2)
                strip_ref[slot, field, 0, rows, :] = top[0:2, lanes]
                strip_ref[slot, field, 1, rows, :] = bottom[14:16, lanes]
    for slot in range(slots):
        for direction in range(8):
            link = links_ref[slot, direction]

            @pl.when(link >= 0)
            def _(slot=slot, direction=direction, link=link):
                device = link // slots
                there = link % slots
                for field, ref in enumerate((image_ref, cotangent_ref)):
                    if direction < 2:
                        rows = slice(strip_row(field, slot), strip_row(field, slot) + 32)
                        out_ref[device, rows, :] = strip_ref[slot, field, direction].astype(BF16)
                    elif direction < 4:
                        first = jnp.where(device == me, strip_row(field, slot), column_row(field))
                        lanes = slice(0, LANES) if direction == 2 else slice(width - LANES, width)
                        out_ref[device, pl.ds(pl.multiple_of(first, 32), 32), :] = ref[slot, :, lanes]
                    else:
                        which = 0 if direction < 6 else 1
                        first = 0 if direction % 2 == 0 else side - 2
                        corner = strip_ref[slot, field, which, first : first + 2, :]
                        for target in range(slots):
                            row = corner_row(field, slot, target)

                            @pl.when(there == target)
                            def _(row=row, corner=corner):
                                corner_ref[device, row : row + 2, :] = corner

    def place(device, carry):
        out_ref[device, CORNERS:BLOCK, :] = corner_ref[device].astype(BF16)
        return carry

    lax.fori_loop(0, out_ref.shape[0], place, 0)


def mix_kernel(
    links_ref, tissue_ref, image_ref, cotangent_ref, halo_ref, one_ref, two_ref,
    output_hbm, grad_input_hbm, grads_ref,
    wide_in, wide_up, narrow_hidden, narrow_delta, own_delta,
    taps_in, taps_up, taps_hidden, taps_delta, forward_ref, back_ref, acc_ref, output_ref, grad_input_ref, sems,
):
    slots, side, width = image_ref.shape
    pairs = width // LANES
    half = LANES // 2
    tall = side + 16
    me = lax.axis_index("tile")

    band_weights(one_ref, forward_ref.at[0], back_ref.at[0])
    band_weights(two_ref, forward_ref.at[1], back_ref.at[1])

    for field, (ref, wide) in enumerate(((image_ref, wide_in), (cotangent_ref, wide_up))):
        wide[:, :, 0:16, :] = jnp.zeros((slots, pairs + 2, 16, LANES), F32)
        wide[:, :, 16 + side : 32 + side, :] = jnp.zeros((slots, pairs + 2, 16, LANES), F32)
        for column in (0, pairs + 1):
            wide[:, column, 16 : 16 + side, :] = jnp.zeros((slots, side, LANES), F32)
        for slot in range(slots):
            present = tissue_ref[0, slot] > 0
            for pair in range(pairs):
                block = ref[slot, :, pair * LANES : (pair + 1) * LANES].astype(F32)
                wide[slot, pair + 1, 16 : 16 + side, :] = jnp.where(present, block, 0.0)
            for direction in range(8):
                link = links_ref[slot, direction]

                @pl.when(link >= 0)
                def _(slot=slot, direction=direction, link=link, field=field, wide=wide):
                    device, there = link // slots, link % slots
                    if direction in (2, 3):
                        column = 0 if direction == 2 else pairs + 1
                        at_home = strip_row(field, 0) + there * 32
                        first = pl.multiple_of(jnp.where(device == me, at_home, column_row(field)), 32)
                        got = halo_ref[device, pl.ds(first, 32), :].astype(F32)
                        wide[slot, column, 16 : 16 + side, :] = got
                    else:
                        row = 14 if direction in (0, 4, 5) else 16 + side
                        if direction < 2:
                            at = pl.multiple_of(strip_row(field, 0) + there * 32, 32)
                            got = halo_ref[device, pl.ds(at, 32), :].astype(F32)
                            for pair in range(pairs):
                                wide[slot, pair + 1, row : row + 2, :] = got[2 * pair : 2 * pair + 2, :]
                        else:
                            column = 0 if direction in (4, 6) else pairs + 1
                            got = halo_ref[device, CORNERS:BLOCK, :].astype(F32)
                            one, two = (corner_row(field, k, slot) for k in range(2))
                            corner = jnp.where(there == 0, got[one : one + 2], got[two : two + 2])
                            wide[slot, column, row : row + 2, :] = corner

    def spread(field, taps, count, start, rows):
        def step(pair, carry):
            for slot in range(slots):
                for a in range(3):
                    block = field[slot, pair, start + a - 1 : start + a - 1 + rows, :].astype(BF16)
                    taps[slot, pair + 1, :, a * 256 : a * 256 + LANES] = block
                    taps[slot, pair, :, a * 256 + LANES : (a + 1) * 256] = block
            return carry

        lax.fori_loop(0, count, step, 0, unroll=True)

    spread(wide_in, taps_in, pairs + 2, 8, tall)
    spread(wide_up, taps_up, pairs + 2, 8, tall)

    row = lax.broadcasted_iota(jnp.int32, (tall, LANES), 0)
    lane = lax.broadcasted_iota(jnp.int32, (tall, LANES), 1)

    def column_mask(north, here, south):
        value = jnp.where(row == 7, north, jnp.where(row == 8 + side, south, here))
        return jnp.where((row >= 7) & (row <= 8 + side), value, 0)

    def across(taps, slot, count, rows):
        return taps[slot, 1 : count + 1].reshape(count * rows, 768)

    contract_last = (((1,), (1,)), ((), ()))
    for slot in range(slots):
        there = [(links_ref[slot, k] >= 0).astype(jnp.int32) for k in range(8)]
        own = tissue_ref[0, slot]
        middle = column_mask(there[0], own, there[1])
        west = jnp.where(lane < half, column_mask(there[4], there[2], there[6]), middle)
        east = jnp.where(lane < half, middle, column_mask(there[5], there[3], there[7]))
        inside = (row >= 8) & (row < 8 + side)

        first = jnp.dot(
            across(taps_in, slot, pairs + 1, tall), forward_ref[0], preferred_element_type=F32
        )
        acc_ref[0] = first.reshape(pairs + 1, tall, LANES)
        second = lax.dot_general(
            across(taps_up, slot, pairs + 1, tall), back_ref[1], contract_last,
            preferred_element_type=F32,
        )
        acc_ref[1] = second.reshape(pairs + 1, tall, LANES)

        def finish(pair, mask, own_mask, slot=slot):
            hidden = jnp.where(mask > 0, jnp.maximum(acc_ref[0, pair], 0.0), 0.0)
            hidden = hidden.astype(BF16).astype(F32)
            delta = jnp.where(hidden > 0, acc_ref[1, pair], 0.0)
            narrow_hidden[slot, pair] = hidden
            narrow_delta[slot, pair] = delta
            own_delta[slot, pair] = jnp.where(own_mask, delta, 0.0).astype(BF16)

        finish(0, west, inside & (lane >= half))
        finish(pairs, east, inside & (lane < half))

        def middle_step(pair, carry, middle=middle, inside=inside):
            finish(pair, middle, inside)
            return carry

        lax.fori_loop(1, pairs, middle_step, 0, unroll=True)

    spread(narrow_hidden, taps_hidden, pairs + 1, 8, side)
    spread(narrow_delta, taps_delta, pairs + 1, 8, side)

    first_grad = None
    second_grad = None
    copies = []
    contract_first = (((0,), (0,)), ((), ()))
    for slot in range(slots):
        out = jnp.dot(across(taps_hidden, slot, pairs, side), forward_ref[1], preferred_element_type=F32)
        back = lax.dot_general(
            across(taps_delta, slot, pairs, side), back_ref[0], contract_last, preferred_element_type=F32
        )
        for pair in range(pairs):
            lanes = slice(pair * LANES, (pair + 1) * LANES)
            rows = slice(pair * side, (pair + 1) * side)
            output_ref[slot, :, lanes] = out[rows].astype(BF16)
            grad_input_ref[slot, :, lanes] = back[rows].astype(BF16)
        for k, (source, target) in enumerate(((output_ref, output_hbm), (grad_input_ref, grad_input_hbm))):
            copies.append(pltpu.make_async_copy(source.at[slot], target.at[slot], sems.at[2 * slot + k]))
            copies[-1].start()
    for slot in range(slots):
        upstream = wide_up[slot, 1 : pairs + 1, 16 : 16 + side, :].reshape(pairs * side, LANES)
        term_two = lax.dot_general(
            upstream.astype(BF16), across(taps_hidden, slot, pairs, side), contract_first,
            preferred_element_type=F32,
        )
        deltas = own_delta[slot].reshape((pairs + 1) * tall, LANES)
        term_one = lax.dot_general(
            deltas, across(taps_in, slot, pairs + 1, tall), contract_first, preferred_element_type=F32
        )
        first_grad = term_one if first_grad is None else first_grad + term_one
        second_grad = term_two if second_grad is None else second_grad + term_two

    total = grads_ref.shape[0]
    lane = lax.broadcasted_iota(jnp.int32, (192, LANES), 1)
    for a in range(3):
        lanes = slice(a * 256, (a + 1) * 256)
        one = first_grad[:, lanes].T
        two = second_grad[:, lanes].T
        left = one[0:192] + pltpu.roll(one[64:256], half, 1)
        right = pltpu.roll(two[0:192], half, 1) + two[64:256]
        grads_ref[a * 192 : (a + 1) * 192, :] = jnp.where(lane < half, left, right).astype(BF16)
    if total > 576:
        grads_ref[576:total, :] = jnp.zeros((total - 576, LANES), BF16)
    for copy in copies:
        copy.wait()


def local(slide_image, cotangent, weight_one, weight_two, tissue, neighbours):
    devices_tile = lax.axis_size("tile")
    devices = devices_tile * lax.axis_size("slide")
    _, slots, side, width = slide_image.shape
    pairs = width // LANES
    tall = side + 16
    image, upstream = slide_image[0], cotangent[0]
    links = neighbours[0]
    packed = pl.pallas_call(
        pack_kernel,
        out_shape=jax.ShapeDtypeStruct((devices_tile, BLOCK, LANES), BF16),
        in_specs=[ANY] * 3,
        out_specs=VMEM,
        scratch_shapes=[
            pltpu.SMEM(links.shape, jnp.int32),
            pltpu.VMEM(image.shape, BF16),
            pltpu.VMEM(image.shape, BF16),
            pltpu.VMEM((slots, 2, 2, 32, LANES), F32),
            pltpu.VMEM((devices_tile, 16, LANES), F32),
            pltpu.SemaphoreType.DMA((3,)),
        ],
        compiler_params=pltpu.CompilerParams(vmem_limit_bytes=PACK_LIMIT),
        name="pack",
    )(links, image, upstream)
    halo = lax.all_to_all(packed, "tile", 0, 0, tiled=True)

    chunk = -(-576 // devices)
    chunk = -(-chunk // 8) * 8
    total = chunk * devices
    output, grad_input, grads = pl.pallas_call(
        mix_kernel,
        out_shape=(
            jax.ShapeDtypeStruct((slots, side, width), BF16),
            jax.ShapeDtypeStruct((slots, side, width), BF16),
            jax.ShapeDtypeStruct((total, LANES), BF16),
        ),
        in_specs=[SMEM, SMEM] + [VMEM] * 5,
        out_specs=(ANY, ANY, VMEM),
        scratch_shapes=[
            pltpu.VMEM((slots, pairs + 2, side + 32, LANES), F32),
            pltpu.VMEM((slots, pairs + 2, side + 32, LANES), F32),
            pltpu.VMEM((slots, pairs + 1, tall, LANES), F32),
            pltpu.VMEM((slots, pairs + 1, tall, LANES), F32),
            pltpu.VMEM((slots, pairs + 1, tall, LANES), BF16),
            pltpu.VMEM((slots, pairs + 3, tall, 768), BF16),
            pltpu.VMEM((slots, pairs + 3, tall, 768), BF16),
            pltpu.VMEM((slots, pairs + 2, side, 768), BF16),
            pltpu.VMEM((slots, pairs + 2, side, 768), BF16),
            pltpu.VMEM((2, 768, LANES), BF16),
            pltpu.VMEM((2, LANES, 768), BF16),
            pltpu.VMEM((2, pairs + 1, tall, LANES), F32),
            pltpu.VMEM((slots, side, width), BF16),
            pltpu.VMEM((slots, side, width), BF16),
            pltpu.SemaphoreType.DMA((2 * slots,)),
        ],
        compiler_params=pltpu.CompilerParams(vmem_limit_bytes=48 * 2**20),
        name="mix",
    )(links, tissue, image, upstream, halo, weight_one, weight_two)

    parts = lax.all_to_all(grads.reshape(devices, chunk, LANES), ("slide", "tile"), 0, 0, tiled=True)
    mine = jnp.sum(lax.optimization_barrier(parts.astype(F32)), axis=0).astype(BF16)
    sums = jnp.broadcast_to(mine[None], parts.shape)
    whole = lax.all_to_all(sums, ("slide", "tile"), 0, 0, tiled=True)
    whole = lax.optimization_barrier(whole.reshape(total, LANES).astype(F32))
    grad_one = whole[:576, : LANES // 2]
    grad_two = whole[:576, LANES // 2 :]
    shape = weight_one.shape
    return output[None], grad_input[None], grad_one.reshape(shape), grad_two.reshape(shape)


def solution(mesh):
    placed = (
        P("slide", "tile", None, None),
        P("slide", "tile", None, None),
        P(),
        P(),
        P("slide", "tile"),
        P("slide", "tile", None),
    )
    return jax.shard_map(
        local,
        mesh=mesh,
        in_specs=placed,
        out_specs=(P("slide", "tile", None, None), P("slide", "tile", None, None), P(), P()),
        check_vma=False,
    )
```

```python
import functools

import jax
import jax.numpy as jnp
from jax import lax
from jax.experimental import pallas as pl
from jax.experimental.pallas import tpu as pltpu
from jax.sharding import PartitionSpec as P

F32 = jnp.float32
BF16 = jnp.bfloat16
LANES = 128
SMEM = pl.BlockSpec(memory_space=pltpu.SMEM)
VMEM = pl.BlockSpec(memory_space=pltpu.VMEM)
ANY = pl.BlockSpec(memory_space=pl.ANY)
PACK_LIMIT = 60 * 2**20


BLOCK = 2 * 96


def strip_row(field, slot):
    return field * 96 + slot * 32


def column_row(field):
    return field * 96 + 64


def band_weights(source, forward, back):
    half = LANES // 2
    zero = jnp.zeros((half, half), BF16)
    for a in range(3):
        taps = [source[a, b] for b in range(3)]
        left = jnp.concatenate(taps + [zero], axis=0)
        right = jnp.concatenate([zero] + taps, axis=0)
        forward[a * 256 : (a + 1) * 256, :] = jnp.concatenate([left, right], axis=1)
        turned = [source[2 - a, 2 - b] for b in range(3)]
        upper = jnp.concatenate(turned + [zero], axis=1)
        lower = jnp.concatenate([zero] + turned, axis=1)
        back[:, a * 256 : (a + 1) * 256] = jnp.concatenate([upper, lower], axis=0)


def pack_kernel(
    links_hbm, image_hbm, cotangent_hbm, out_ref,
    links_ref, image_ref, cotangent_ref, strip_ref, sems,
):
    slots, side, width = image_ref.shape
    pairs = width // LANES
    copies = [pltpu.make_async_copy(links_hbm, links_ref, sems.at[2 * slots])]
    copies[0].start()
    fields = ((image_hbm, image_ref), (cotangent_hbm, cotangent_ref))
    for field, (source, target) in enumerate(fields):
        for slot in range(slots):
            copy = pltpu.make_async_copy(source.at[slot], target.at[slot], sems.at[field * slots + slot])
            copy.start()
            copies.append(copy)
    me = lax.axis_index("tile")
    copies[0].wait()
    for field, (_, ref) in enumerate(fields):
        for slot in range(slots):
            copies[1 + field * slots + slot].wait()
            top = ref[slot, 0:16, :].astype(F32)
            bottom = ref[slot, side - 16 : side, :].astype(F32)
            for pair in range(pairs):
                lanes = slice(pair * LANES, (pair + 1) * LANES)
                rows = slice(2 * pair, 2 * pair + 2)
                strip_ref[0, rows, :] = top[0:2, lanes]
                strip_ref[1, rows, :] = bottom[14:16, lanes]
            for direction in range(8):
                link = links_ref[slot, direction]

                @pl.when(link >= 0)
                def _(slot=slot, direction=direction, link=link, field=field, ref=ref):
                    device = link // slots
                    if direction in (2, 3):
                        first = jnp.where(device == me, strip_row(field, slot), column_row(field))
                        lanes = slice(0, LANES) if direction == 2 else slice(width - LANES, width)
                        out_ref[device, pl.ds(pl.multiple_of(first, 32), 32), :] = ref[slot, :, lanes]
                    else:
                        which = 0 if direction in (0, 4, 5) else 1
                        first = strip_row(field, slot)
                        out_ref[device, first : first + 32, :] = strip_ref[which].astype(BF16)


def mix_kernel(
    links_ref, tissue_ref, image_ref, cotangent_ref, halo_ref, one_ref, two_ref,
    output_hbm, grad_input_hbm, grads_ref,
    wide_in, wide_up, narrow_hidden, narrow_delta, own_delta,
    taps_in, taps_up, taps_hidden, taps_delta, forward_ref, back_ref, acc_ref, output_ref, grad_input_ref, sems,
):
    slots, side, width = image_ref.shape
    pairs = width // LANES
    half = LANES // 2
    tall = side + 16
    me = lax.axis_index("tile")

    band_weights(one_ref, forward_ref.at[0], back_ref.at[0])
    band_weights(two_ref, forward_ref.at[1], back_ref.at[1])

    for field, (ref, wide) in enumerate(((image_ref, wide_in), (cotangent_ref, wide_up))):
        wide[:, :, 0:16, :] = jnp.zeros((slots, pairs + 2, 16, LANES), F32)
        wide[:, :, 16 + side : 32 + side, :] = jnp.zeros((slots, pairs + 2, 16, LANES), F32)
        for column in (0, pairs + 1):
            wide[:, column, 16 : 16 + side, :] = jnp.zeros((slots, side, LANES), F32)
        for slot in range(slots):
            present = tissue_ref[0, slot] > 0
            for pair in range(pairs):
                block = ref[slot, :, pair * LANES : (pair + 1) * LANES].astype(F32)
                wide[slot, pair + 1, 16 : 16 + side, :] = jnp.where(present, block, 0.0)
            for direction in range(8):
                link = links_ref[slot, direction]

                @pl.when(link >= 0)
                def _(slot=slot, direction=direction, link=link, field=field, wide=wide):
                    device, there = link // slots, link % slots
                    if direction in (2, 3):
                        column = 0 if direction == 2 else pairs + 1
                        at_home = strip_row(field, 0) + there * 32
                        first = pl.multiple_of(jnp.where(device == me, at_home, column_row(field)), 32)
                        got = halo_ref[device, pl.ds(first, 32), :].astype(F32)
                        wide[slot, column, 16 : 16 + side, :] = got
                    else:
                        row = 14 if direction in (0, 4, 5) else 16 + side
                        at = pl.multiple_of(strip_row(field, 0) + there * 32, 32)
                        got = halo_ref[device, pl.ds(at, 32), :].astype(F32)
                        if direction < 2:
                            for pair in range(pairs):
                                wide[slot, pair + 1, row : row + 2, :] = got[2 * pair : 2 * pair + 2, :]
                        elif direction in (4, 6):
                            wide[slot, 0, row : row + 2, :] = got[2 * pairs - 2 : 2 * pairs, :]
                        else:
                            wide[slot, pairs + 1, row : row + 2, :] = got[0:2, :]

    def spread(field, taps, count, start, rows):
        def step(pair, carry):
            for slot in range(slots):
                for a in range(3):
                    block = field[slot, pair, start + a - 1 : start + a - 1 + rows, :].astype(BF16)
                    taps[slot, pair + 1, :, a * 256 : a * 256 + LANES] = block
                    taps[slot, pair, :, a * 256 + LANES : (a + 1) * 256] = block
            return carry

        lax.fori_loop(0, count, step, 0, unroll=True)

    spread(wide_in, taps_in, pairs + 2, 8, tall)
    spread(wide_up, taps_up, pairs + 2, 8, tall)

    row = lax.broadcasted_iota(jnp.int32, (tall, LANES), 0)
    lane = lax.broadcasted_iota(jnp.int32, (tall, LANES), 1)

    def column_mask(north, here, south):
        value = jnp.where(row == 7, north, jnp.where(row == 8 + side, south, here))
        return jnp.where((row >= 7) & (row <= 8 + side), value, 0)

    def across(taps, slot, count, rows):
        return taps[slot, 1 : count + 1].reshape(count * rows, 768)

    contract_last = (((1,), (1,)), ((), ()))
    for slot in range(slots):
        there = [(links_ref[slot, k] >= 0).astype(jnp.int32) for k in range(8)]
        own = tissue_ref[0, slot]
        middle = column_mask(there[0], own, there[1])
        west = jnp.where(lane < half, column_mask(there[4], there[2], there[6]), middle)
        east = jnp.where(lane < half, middle, column_mask(there[5], there[3], there[7]))
        inside = (row >= 8) & (row < 8 + side)

        first = jnp.dot(
            across(taps_in, slot, pairs + 1, tall), forward_ref[0], preferred_element_type=F32
        )
        acc_ref[0] = first.reshape(pairs + 1, tall, LANES)
        second = lax.dot_general(
            across(taps_up, slot, pairs + 1, tall), back_ref[1], contract_last,
            preferred_element_type=F32,
        )
        acc_ref[1] = second.reshape(pairs + 1, tall, LANES)

        def finish(pair, mask, own_mask, slot=slot):
            hidden = jnp.where(mask > 0, jnp.maximum(acc_ref[0, pair], 0.0), 0.0)
            hidden = hidden.astype(BF16).astype(F32)
            delta = jnp.where(hidden > 0, acc_ref[1, pair], 0.0)
            narrow_hidden[slot, pair] = hidden
            narrow_delta[slot, pair] = delta
            own_delta[slot, pair] = jnp.where(own_mask, delta, 0.0).astype(BF16)

        finish(0, west, inside & (lane >= half))
        finish(pairs, east, inside & (lane < half))

        def middle_step(pair, carry, middle=middle, inside=inside):
            finish(pair, middle, inside)
            return carry

        lax.fori_loop(1, pairs, middle_step, 0, unroll=True)

    spread(narrow_hidden, taps_hidden, pairs + 1, 8, side)
    spread(narrow_delta, taps_delta, pairs + 1, 8, side)

    first_grad = None
    second_grad = None
    copies = []
    contract_first = (((0,), (0,)), ((), ()))
    for slot in range(slots):
        out = jnp.dot(across(taps_hidden, slot, pairs, side), forward_ref[1], preferred_element_type=F32)
        back = lax.dot_general(
            across(taps_delta, slot, pairs, side), back_ref[0], contract_last, preferred_element_type=F32
        )
        for pair in range(pairs):
            lanes = slice(pair * LANES, (pair + 1) * LANES)
            rows = slice(pair * side, (pair + 1) * side)
            output_ref[slot, :, lanes] = out[rows].astype(BF16)
            grad_input_ref[slot, :, lanes] = back[rows].astype(BF16)
        for k, (source, target) in enumerate(((output_ref, output_hbm), (grad_input_ref, grad_input_hbm))):
            copies.append(pltpu.make_async_copy(source.at[slot], target.at[slot], sems.at[2 * slot + k]))
            copies[-1].start()
    for slot in range(slots):
        upstream = wide_up[slot, 1 : pairs + 1, 16 : 16 + side, :].reshape(pairs * side, LANES)
        term_two = lax.dot_general(
            upstream.astype(BF16), across(taps_hidden, slot, pairs, side), contract_first,
            preferred_element_type=F32,
        )
        deltas = own_delta[slot].reshape((pairs + 1) * tall, LANES)
        term_one = lax.dot_general(
            deltas, across(taps_in, slot, pairs + 1, tall), contract_first, preferred_element_type=F32
        )
        first_grad = term_one if first_grad is None else first_grad + term_one
        second_grad = term_two if second_grad is None else second_grad + term_two

    total = grads_ref.shape[0]
    lane = lax.broadcasted_iota(jnp.int32, (192, LANES), 1)
    for a in range(3):
        lanes = slice(a * 256, (a + 1) * 256)
        one = first_grad[:, lanes].T
        two = second_grad[:, lanes].T
        left = one[0:192] + pltpu.roll(one[64:256], half, 1)
        right = pltpu.roll(two[0:192], half, 1) + two[64:256]
        grads_ref[a * 192 : (a + 1) * 192, :] = jnp.where(lane < half, left, right).astype(BF16)
    if total > 576:
        grads_ref[576:total, :] = jnp.zeros((total - 576, LANES), BF16)
    for copy in copies:
        copy.wait()


def local(slide_image, cotangent, weight_one, weight_two, tissue, neighbours):
    devices_tile = lax.axis_size("tile")
    devices = devices_tile * lax.axis_size("slide")
    _, slots, side, width = slide_image.shape
    pairs = width // LANES
    tall = side + 16
    image, upstream = slide_image[0], cotangent[0]
    links = neighbours[0]
    packed = pl.pallas_call(
        pack_kernel,
        out_shape=jax.ShapeDtypeStruct((devices_tile, BLOCK, LANES), BF16),
        in_specs=[ANY] * 3,
        out_specs=VMEM,
        scratch_shapes=[
            pltpu.SMEM(links.shape, jnp.int32),
            pltpu.VMEM(image.shape, BF16),
            pltpu.VMEM(image.shape, BF16),
            pltpu.VMEM((2, 32, LANES), F32),
            pltpu.SemaphoreType.DMA((2 * slots + 1,)),
        ],
        compiler_params=pltpu.CompilerParams(vmem_limit_bytes=PACK_LIMIT),
        name="pack",
    )(links, image, upstream)
    halo = lax.all_to_all(packed, "tile", 0, 0, tiled=True)

    chunk = -(-576 // devices)
    chunk = -(-chunk // 8) * 8
    total = chunk * devices
    output, grad_input, grads = pl.pallas_call(
        mix_kernel,
        out_shape=(
            jax.ShapeDtypeStruct((slots, side, width), BF16),
            jax.ShapeDtypeStruct((slots, side, width), BF16),
            jax.ShapeDtypeStruct((total, LANES), BF16),
        ),
        in_specs=[SMEM, SMEM] + [VMEM] * 5,
        out_specs=(ANY, ANY, VMEM),
        scratch_shapes=[
            pltpu.VMEM((slots, pairs + 2, side + 32, LANES), F32),
            pltpu.VMEM((slots, pairs + 2, side + 32, LANES), F32),
            pltpu.VMEM((slots, pairs + 1, tall, LANES), F32),
            pltpu.VMEM((slots, pairs + 1, tall, LANES), F32),
            pltpu.VMEM((slots, pairs + 1, tall, LANES), BF16),
            pltpu.VMEM((slots, pairs + 3, tall, 768), BF16),
            pltpu.VMEM((slots, pairs + 3, tall, 768), BF16),
            pltpu.VMEM((slots, pairs + 2, side, 768), BF16),
            pltpu.VMEM((slots, pairs + 2, side, 768), BF16),
            pltpu.VMEM((2, 768, LANES), BF16),
            pltpu.VMEM((2, LANES, 768), BF16),
            pltpu.VMEM((2, pairs + 1, tall, LANES), F32),
            pltpu.VMEM((slots, side, width), BF16),
            pltpu.VMEM((slots, side, width), BF16),
            pltpu.SemaphoreType.DMA((2 * slots,)),
        ],
        compiler_params=pltpu.CompilerParams(vmem_limit_bytes=48 * 2**20),
        name="mix",
    )(links, tissue, image, upstream, halo, weight_one, weight_two)

    parts = lax.all_to_all(grads.reshape(devices, chunk, LANES), ("slide", "tile"), 0, 0, tiled=True)
    mine = jnp.sum(lax.optimization_barrier(parts.astype(F32)), axis=0).astype(BF16)
    sums = jnp.broadcast_to(mine[None], parts.shape)
    whole = lax.all_to_all(sums, ("slide", "tile"), 0, 0, tiled=True)
    whole = lax.optimization_barrier(whole.reshape(total, LANES).astype(F32))
    grad_one = whole[:576, : LANES // 2]
    grad_two = whole[:576, LANES // 2 :]
    shape = weight_one.shape
    return output[None], grad_input[None], grad_one.reshape(shape), grad_two.reshape(shape)


def solution(mesh):
    placed = (
        P("slide", "tile", None, None),
        P("slide", "tile", None, None),
        P(),
        P(),
        P("slide", "tile"),
        P("slide", "tile", None),
    )
    return jax.shard_map(
        local,
        mesh=mesh,
        in_specs=placed,
        out_specs=(P("slide", "tile", None, None), P("slide", "tile", None, None), P(), P()),
        check_vma=False,
    )
```

```python
import functools

import jax
import jax.numpy as jnp
from jax import lax
from jax.experimental import pallas as pl
from jax.experimental.pallas import tpu as pltpu
from jax.sharding import PartitionSpec as P

F32 = jnp.float32
BF16 = jnp.bfloat16
LANES = 128
SMEM = pl.BlockSpec(memory_space=pltpu.SMEM)
VMEM = pl.BlockSpec(memory_space=pltpu.VMEM)
ANY = pl.BlockSpec(memory_space=pl.ANY)
PACK_LIMIT = 60 * 2**20


BLOCK = 2 * 96


def strip_row(field, slot):
    return field * 96 + slot * 32


def column_row(field):
    return field * 96 + 64


def band_weights(source, forward, back):
    half = LANES // 2
    zero = jnp.zeros((half, half), BF16)
    for a in range(3):
        taps = [source[a, b] for b in range(3)]
        left = jnp.concatenate(taps + [zero], axis=0)
        right = jnp.concatenate([zero] + taps, axis=0)
        forward[a * 256 : (a + 1) * 256, :] = jnp.concatenate([left, right], axis=1)
        turned = [source[2 - a, 2 - b] for b in range(3)]
        upper = jnp.concatenate(turned + [zero], axis=1)
        lower = jnp.concatenate([zero] + turned, axis=1)
        back[:, a * 256 : (a + 1) * 256] = jnp.concatenate([upper, lower], axis=0)


def pack_kernel(
    links_hbm, image_hbm, cotangent_hbm, out_ref,
    links_ref, image_ref, cotangent_ref, strip_ref, sems,
):
    slots, side, width = image_ref.shape
    pairs = width // LANES
    copies = [pltpu.make_async_copy(links_hbm, links_ref, sems.at[2 * slots])]
    copies[0].start()
    fields = ((image_hbm, image_ref), (cotangent_hbm, cotangent_ref))
    for field, (source, target) in enumerate(fields):
        for slot in range(slots):
            copy = pltpu.make_async_copy(source.at[slot], target.at[slot], sems.at[field * slots + slot])
            copy.start()
            copies.append(copy)
    me = lax.axis_index("tile")
    copies[0].wait()
    for field, (_, ref) in enumerate(fields):
        for slot in range(slots):
            copies[1 + field * slots + slot].wait()
            top = ref[slot, 0:16, :].astype(F32)
            bottom = ref[slot, side - 16 : side, :].astype(F32)
            for pair in range(pairs):
                lanes = slice(pair * LANES, (pair + 1) * LANES)
                rows = slice(2 * pair, 2 * pair + 2)
                strip_ref[0, rows, :] = top[0:2, lanes]
                strip_ref[1, rows, :] = bottom[14:16, lanes]
            for direction in range(8):
                link = links_ref[slot, direction]

                @pl.when(link >= 0)
                def _(slot=slot, direction=direction, link=link, field=field, ref=ref):
                    device = link // slots
                    if direction in (2, 3):
                        first = jnp.where(device == me, strip_row(field, slot), column_row(field))
                        lanes = slice(0, LANES) if direction == 2 else slice(width - LANES, width)
                        out_ref[device, pl.ds(pl.multiple_of(first, 32), 32), :] = ref[slot, :, lanes]
                    else:
                        which = 0 if direction in (0, 4, 5) else 1
                        first = strip_row(field, slot)
                        out_ref[device, first : first + 32, :] = strip_ref[which].astype(BF16)


def mix_kernel(
    links_ref, tissue_ref, image_ref, cotangent_ref, halo_ref, one_ref, two_ref,
    output_hbm, grad_input_hbm, grads_ref,
    wide_in, wide_up, narrow_hidden, narrow_delta, own_delta,
    taps_in, taps_up, taps_hidden, taps_delta, forward_ref, back_ref, acc_ref, output_ref, grad_input_ref, sems,
):
    slots, side, width = image_ref.shape
    pairs = width // LANES
    half = LANES // 2
    tall = side + 16
    me = lax.axis_index("tile")

    band_weights(one_ref, forward_ref.at[0], back_ref.at[0])
    band_weights(two_ref, forward_ref.at[1], back_ref.at[1])

    for field, (ref, wide) in enumerate(((image_ref, wide_in), (cotangent_ref, wide_up))):
        wide[:, :, 0:16, :] = jnp.zeros((slots, pairs + 2, 16, LANES), F32)
        wide[:, :, 16 + side : 32 + side, :] = jnp.zeros((slots, pairs + 2, 16, LANES), F32)
        for column in (0, pairs + 1):
            wide[:, column, 16 : 16 + side, :] = jnp.zeros((slots, side, LANES), F32)
        for slot in range(slots):
            present = tissue_ref[0, slot] > 0
            for pair in range(pairs):
                block = ref[slot, :, pair * LANES : (pair + 1) * LANES].astype(F32)
                wide[slot, pair + 1, 16 : 16 + side, :] = jnp.where(present, block, 0.0)
            for direction in range(8):
                link = links_ref[slot, direction]

                @pl.when(link >= 0)
                def _(slot=slot, direction=direction, link=link, field=field, wide=wide):
                    device, there = link // slots, link % slots
                    if direction in (2, 3):
                        column = 0 if direction == 2 else pairs + 1
                        at_home = strip_row(field, 0) + there * 32
                        first = pl.multiple_of(jnp.where(device == me, at_home, column_row(field)), 32)
                        got = halo_ref[device, pl.ds(first, 32), :].astype(F32)
                        wide[slot, column, 16 : 16 + side, :] = got
                    else:
                        row = 14 if direction in (0, 4, 5) else 16 + side
                        at = pl.multiple_of(strip_row(field, 0) + there * 32, 32)
                        got = halo_ref[device, pl.ds(at, 32), :].astype(F32)
                        if direction < 2:
                            for pair in range(pairs):
                                wide[slot, pair + 1, row : row + 2, :] = got[2 * pair : 2 * pair + 2, :]
                        elif direction in (4, 6):
                            wide[slot, 0, row : row + 2, :] = got[2 * pairs - 2 : 2 * pairs, :]
                        else:
                            wide[slot, pairs + 1, row : row + 2, :] = got[0:2, :]

    def spread(field, taps, count, start, rows):
        def step(pair, carry):
            for slot in range(slots):
                for a in range(3):
                    block = field[slot, pair, start + a - 1 : start + a - 1 + rows, :].astype(BF16)
                    taps[slot, pair + 1, :, a * 256 : a * 256 + LANES] = block
                    taps[slot, pair, :, a * 256 + LANES : (a + 1) * 256] = block
            return carry

        lax.fori_loop(0, count, step, 0, unroll=True)

    spread(wide_in, taps_in, pairs + 2, 8, tall)
    spread(wide_up, taps_up, pairs + 2, 8, tall)

    row = lax.broadcasted_iota(jnp.int32, (tall, LANES), 0)
    lane = lax.broadcasted_iota(jnp.int32, (tall, LANES), 1)

    def column_mask(north, here, south):
        value = jnp.where(row == 7, north, jnp.where(row == 8 + side, south, here))
        return jnp.where((row >= 7) & (row <= 8 + side), value, 0)

    def across(taps, slot, count, rows):
        return taps[slot, 1 : count + 1].reshape(count * rows, 768)

    contract_last = (((1,), (1,)), ((), ()))
    for slot in range(slots):
        there = [(links_ref[slot, k] >= 0).astype(jnp.int32) for k in range(8)]
        own = tissue_ref[0, slot]
        middle = column_mask(there[0], own, there[1])
        west = jnp.where(lane < half, column_mask(there[4], there[2], there[6]), middle)
        east = jnp.where(lane < half, middle, column_mask(there[5], there[3], there[7]))
        inside = (row >= 8) & (row < 8 + side)

        first = jnp.dot(
            across(taps_in, slot, pairs + 1, tall), forward_ref[0], preferred_element_type=F32
        )
        acc_ref[0] = first.reshape(pairs + 1, tall, LANES)
        second = lax.dot_general(
            across(taps_up, slot, pairs + 1, tall), back_ref[1], contract_last,
            preferred_element_type=F32,
        )
        acc_ref[1] = second.reshape(pairs + 1, tall, LANES)

        def finish(pair, mask, own_mask, slot=slot):
            hidden = jnp.where(mask > 0, jnp.maximum(acc_ref[0, pair], 0.0), 0.0)
            hidden = hidden.astype(BF16).astype(F32)
            delta = jnp.where(hidden > 0, acc_ref[1, pair], 0.0)
            narrow_hidden[slot, pair] = hidden
            narrow_delta[slot, pair] = delta
            own_delta[slot, pair] = jnp.where(own_mask, delta, 0.0).astype(BF16)

        finish(0, west, inside & (lane >= half))
        finish(pairs, east, inside & (lane < half))

        def middle_step(pair, carry, middle=middle, inside=inside):
            finish(pair, middle, inside)
            return carry

        lax.fori_loop(1, pairs, middle_step, 0, unroll=True)

    spread(narrow_hidden, taps_hidden, pairs + 1, 8, side)
    spread(narrow_delta, taps_delta, pairs + 1, 8, side)

    first_grad = None
    second_grad = None
    copies = []
    contract_first = (((0,), (0,)), ((), ()))
    for slot in range(slots):
        out = jnp.dot(across(taps_hidden, slot, pairs, side), forward_ref[1], preferred_element_type=F32)
        back = lax.dot_general(
            across(taps_delta, slot, pairs, side), back_ref[0], contract_last, preferred_element_type=F32
        )
        for pair in range(pairs):
            lanes = slice(pair * LANES, (pair + 1) * LANES)
            rows = slice(pair * side, (pair + 1) * side)
            output_ref[slot, :, lanes] = out[rows].astype(BF16)
            grad_input_ref[slot, :, lanes] = back[rows].astype(BF16)
        for k, (source, target) in enumerate(((output_ref, output_hbm), (grad_input_ref, grad_input_hbm))):
            copies.append(pltpu.make_async_copy(source.at[slot], target.at[slot], sems.at[2 * slot + k]))
            copies[-1].start()
    for slot in range(slots):
        upstream = wide_up[slot, 1 : pairs + 1, 16 : 16 + side, :].reshape(pairs * side, LANES)
        term_two = lax.dot_general(
            upstream.astype(BF16), across(taps_hidden, slot, pairs, side), contract_first,
            preferred_element_type=F32,
        )
        deltas = own_delta[slot].reshape((pairs + 1) * tall, LANES)
        term_one = lax.dot_general(
            deltas, across(taps_in, slot, pairs + 1, tall), contract_first, preferred_element_type=F32
        )
        first_grad = term_one if first_grad is None else first_grad + term_one
        second_grad = term_two if second_grad is None else second_grad + term_two

    total = grads_ref.shape[0]
    lane = lax.broadcasted_iota(jnp.int32, (192, LANES), 1)
    for a in range(3):
        lanes = slice(a * 256, (a + 1) * 256)
        one = first_grad[:, lanes].T
        two = second_grad[:, lanes].T
        left = one[0:192] + pltpu.roll(one[64:256], half, 1)
        right = pltpu.roll(two[0:192], half, 1) + two[64:256]
        grads_ref[a * 192 : (a + 1) * 192, :] = jnp.where(lane < half, left, right).astype(BF16)
    if total > 576:
        grads_ref[576:total, :] = jnp.zeros((total - 576, LANES), BF16)
    for copy in copies:
        copy.wait()


def local(slide_image, cotangent, weight_one, weight_two, tissue, neighbours):
    devices_tile = lax.axis_size("tile")
    devices = devices_tile * lax.axis_size("slide")
    _, slots, side, width = slide_image.shape
    pairs = width // LANES
    tall = side + 16
    image, upstream = slide_image[0], cotangent[0]
    links = neighbours[0]
    packed = pl.pallas_call(
        pack_kernel,
        out_shape=jax.ShapeDtypeStruct((devices_tile, BLOCK, LANES), BF16),
        in_specs=[ANY] * 3,
        out_specs=VMEM,
        scratch_shapes=[
            pltpu.SMEM(links.shape, jnp.int32),
            pltpu.VMEM(image.shape, BF16),
            pltpu.VMEM(image.shape, BF16),
            pltpu.VMEM((2, 32, LANES), F32),
            pltpu.SemaphoreType.DMA((2 * slots + 1,)),
        ],
        compiler_params=pltpu.CompilerParams(vmem_limit_bytes=PACK_LIMIT),
        name="pack",
    )(links, image, upstream)
    halo = lax.all_to_all(packed, "tile", 0, 0, tiled=True)

    chunk = -(-576 // (2 * devices))
    total = 2 * chunk * devices
    output, grad_input, grads = pl.pallas_call(
        mix_kernel,
        out_shape=(
            jax.ShapeDtypeStruct((slots, side, width), BF16),
            jax.ShapeDtypeStruct((slots, side, width), BF16),
            jax.ShapeDtypeStruct((total, LANES), BF16),
        ),
        in_specs=[SMEM, SMEM] + [VMEM] * 5,
        out_specs=(ANY, ANY, VMEM),
        scratch_shapes=[
            pltpu.VMEM((slots, pairs + 2, side + 32, LANES), F32),
            pltpu.VMEM((slots, pairs + 2, side + 32, LANES), F32),
            pltpu.VMEM((slots, pairs + 1, tall, LANES), F32),
            pltpu.VMEM((slots, pairs + 1, tall, LANES), F32),
            pltpu.VMEM((slots, pairs + 1, tall, LANES), BF16),
            pltpu.VMEM((slots, pairs + 3, tall, 768), BF16),
            pltpu.VMEM((slots, pairs + 3, tall, 768), BF16),
            pltpu.VMEM((slots, pairs + 2, side, 768), BF16),
            pltpu.VMEM((slots, pairs + 2, side, 768), BF16),
            pltpu.VMEM((2, 768, LANES), BF16),
            pltpu.VMEM((2, LANES, 768), BF16),
            pltpu.VMEM((2, pairs + 1, tall, LANES), F32),
            pltpu.VMEM((slots, side, width), BF16),
            pltpu.VMEM((slots, side, width), BF16),
            pltpu.SemaphoreType.DMA((2 * slots,)),
        ],
        compiler_params=pltpu.CompilerParams(vmem_limit_bytes=48 * 2**20),
        name="mix",
    )(links, tissue, image, upstream, halo, weight_one, weight_two)

    parts = lax.all_to_all(grads.reshape(devices, chunk, 2, LANES), ("slide", "tile"), 0, 0, tiled=True)
    mine = jnp.sum(lax.optimization_barrier(parts.astype(F32)), axis=0).astype(BF16)
    sums = jnp.broadcast_to(mine[None], parts.shape)
    whole = lax.all_to_all(sums, ("slide", "tile"), 0, 0, tiled=True)
    whole = lax.optimization_barrier(whole.reshape(total, LANES).astype(F32))
    grad_one = whole[:576, : LANES // 2]
    grad_two = whole[:576, LANES // 2 :]
    shape = weight_one.shape
    return output[None], grad_input[None], grad_one.reshape(shape), grad_two.reshape(shape)


def solution(mesh):
    placed = (
        P("slide", "tile", None, None),
        P("slide", "tile", None, None),
        P(),
        P(),
        P("slide", "tile"),
        P("slide", "tile", None),
    )
    return jax.shard_map(
        local,
        mesh=mesh,
        in_specs=placed,
        out_specs=(P("slide", "tile", None, None), P("slide", "tile", None, None), P(), P()),
        check_vma=False,
    )
```

```python
import functools

import jax
import jax.numpy as jnp
from jax import lax
from jax.experimental import pallas as pl
from jax.experimental.pallas import tpu as pltpu
from jax.sharding import PartitionSpec as P

F32 = jnp.float32
BF16 = jnp.bfloat16
LANES = 128
VMEM = pl.BlockSpec(memory_space=pltpu.VMEM)
ANY = pl.BlockSpec(memory_space=pl.ANY)
PACK_LIMIT = 60 * 2**20


BLOCK = 2 * 96


def strip_row(field, slot):
    return field * 96 + slot * 32


def column_row(field):
    return field * 96 + 64


def band_weights(source, forward, back):
    half = LANES // 2
    zero = jnp.zeros((half, half), BF16)
    for a in range(3):
        taps = [source[a, b] for b in range(3)]
        left = jnp.concatenate(taps + [zero], axis=0)
        right = jnp.concatenate([zero] + taps, axis=0)
        forward[a * 256 : (a + 1) * 256, :] = jnp.concatenate([left, right], axis=1)
        turned = [source[2 - a, 2 - b] for b in range(3)]
        upper = jnp.concatenate(turned + [zero], axis=1)
        lower = jnp.concatenate([zero] + turned, axis=1)
        back[:, a * 256 : (a + 1) * 256] = jnp.concatenate([upper, lower], axis=0)


def pack_kernel(
    links_hbm, image_hbm, cotangent_hbm, out_ref,
    links_ref, image_ref, cotangent_ref, strip_ref, sems,
):
    slots, side, width = image_ref.shape
    pairs = width // LANES
    copies = [pltpu.make_async_copy(links_hbm, links_ref, sems.at[2 * slots])]
    copies[0].start()
    fields = ((image_hbm, image_ref), (cotangent_hbm, cotangent_ref))
    for field, (source, target) in enumerate(fields):
        for slot in range(slots):
            copy = pltpu.make_async_copy(source.at[slot], target.at[slot], sems.at[field * slots + slot])
            copy.start()
            copies.append(copy)
    me = lax.axis_index("tile")
    copies[0].wait()
    for field, (_, ref) in enumerate(fields):
        for slot in range(slots):
            copies[1 + field * slots + slot].wait()
            top = ref[slot, 0:16, :].astype(F32)
            bottom = ref[slot, side - 16 : side, :].astype(F32)
            for pair in range(pairs):
                lanes = slice(pair * LANES, (pair + 1) * LANES)
                rows = slice(2 * pair, 2 * pair + 2)
                strip_ref[0, rows, :] = top[0:2, lanes]
                strip_ref[1, rows, :] = bottom[14:16, lanes]
            for direction in range(8):
                link = links_ref[slot, direction]

                @pl.when(link >= 0)
                def _(slot=slot, direction=direction, link=link, field=field, ref=ref):
                    device = link // slots
                    if direction in (2, 3):
                        first = jnp.where(device == me, strip_row(field, slot), column_row(field))
                        lanes = slice(0, LANES) if direction == 2 else slice(width - LANES, width)
                        out_ref[device, pl.ds(pl.multiple_of(first, 32), 32), :] = ref[slot, :, lanes]
                    else:
                        which = 0 if direction in (0, 4, 5) else 1
                        first = strip_row(field, slot)
                        out_ref[device, first : first + 32, :] = strip_ref[which].astype(BF16)


def mix_kernel(
    links_hbm, tissue_hbm, image_ref, cotangent_ref, halo_ref, one_ref, two_ref,
    output_hbm, grad_input_hbm, grads_ref,
    links_ref, tissue_ref, wide_in, wide_up, narrow_hidden, narrow_delta,
    taps_in, taps_up, taps_hidden, taps_delta, forward_ref, back_ref, acc_ref, output_ref, grad_input_ref, sems,
):
    slots, side, width = image_ref.shape
    pairs = width // LANES
    half = LANES // 2
    tall = side + 16
    me = lax.axis_index("tile")

    small = [
        pltpu.make_async_copy(tissue_hbm, tissue_ref, sems.at[2 * slots]),
        pltpu.make_async_copy(links_hbm, links_ref, sems.at[2 * slots + 1]),
    ]
    for copy in small:
        copy.start()
    band_weights(one_ref, forward_ref.at[0], back_ref.at[0])
    band_weights(two_ref, forward_ref.at[1], back_ref.at[1])
    for copy in small:
        copy.wait()

    for field, (ref, wide) in enumerate(((image_ref, wide_in), (cotangent_ref, wide_up))):
        wide[:, :, 0:16, :] = jnp.zeros((slots, pairs + 2, 16, LANES), F32)
        wide[:, :, 16 + side : 32 + side, :] = jnp.zeros((slots, pairs + 2, 16, LANES), F32)
        for slot in range(slots):
            present = tissue_ref[0, slot] > 0
            for pair in range(pairs):
                block = ref[slot, :, pair * LANES : (pair + 1) * LANES].astype(F32)
                wide[slot, pair + 1, 16 : 16 + side, :] = jnp.where(present, block, 0.0)
            for direction in range(8):
                link = links_ref[slot, direction]
                device, there = jnp.maximum(link, 0) // slots, jnp.maximum(link, 0) % slots
                first = strip_row(field, 0) + there * 32
                if direction in (2, 3):
                    first = jnp.where(device == me, first, column_row(field))
                got = halo_ref[device, pl.ds(pl.multiple_of(first, 32), 32), :].astype(F32)
                got = jnp.where(link >= 0, got, 0.0)
                row = 14 if direction in (0, 4, 5) else 16 + side
                if direction in (2, 3):
                    wide[slot, 0 if direction == 2 else pairs + 1, 16 : 16 + side, :] = got
                elif direction < 2:
                    for pair in range(pairs):
                        wide[slot, pair + 1, row : row + 2, :] = got[2 * pair : 2 * pair + 2, :]
                elif direction in (4, 6):
                    wide[slot, 0, row : row + 2, :] = got[2 * pairs - 2 : 2 * pairs, :]
                else:
                    wide[slot, pairs + 1, row : row + 2, :] = got[0:2, :]

    def spread(field, taps, count, start, rows):
        for pair in range(count):
            for slot in range(slots):
                for a in range(3):
                    taps[slot, a, pair] = field[slot, pair, start + a - 1 : start + a - 1 + rows, :].astype(BF16)

    spread(wide_in, taps_in, pairs + 2, 8, tall)
    spread(wide_up, taps_up, pairs + 2, 8, tall)

    row = lax.broadcasted_iota(jnp.int32, (tall, LANES), 0)
    lane = lax.broadcasted_iota(jnp.int32, (tall, LANES), 1)

    def column_mask(north, here, south):
        value = jnp.where(row == 7, north, jnp.where(row == 8 + side, south, here))
        return jnp.where((row >= 7) & (row <= 8 + side), value, 0)

    def across(taps, slot, count, rows):
        parts = [
            taps[slot, a, right : count + right].reshape(count * rows, LANES)
            for a in range(3)
            for right in range(2)
        ]
        return jnp.concatenate(parts, axis=1)

    contract_last = (((1,), (1,)), ((), ()))
    for slot in range(slots):
        there = [(links_ref[slot, k] >= 0).astype(jnp.int32) for k in range(8)]
        own = tissue_ref[0, slot]
        middle = column_mask(there[0], own, there[1])
        west = jnp.where(lane < half, column_mask(there[4], there[2], there[6]), middle)
        east = jnp.where(lane < half, middle, column_mask(there[5], there[3], there[7]))

        first = jnp.dot(
            across(taps_in, slot, pairs + 1, tall), forward_ref[0], preferred_element_type=F32
        )
        acc_ref[slot, 0] = first.reshape(pairs + 1, tall, LANES)
        second = lax.dot_general(
            across(taps_up, slot, pairs + 1, tall), back_ref[1], contract_last,
            preferred_element_type=F32,
        )
        acc_ref[slot, 1] = second.reshape(pairs + 1, tall, LANES)

        for pair in range(pairs + 1):
            mask = west if pair == 0 else east if pair == pairs else middle
            hidden = jnp.where(mask > 0, jnp.maximum(acc_ref[slot, 0, pair], 0.0), 0.0)
            hidden = hidden.astype(BF16).astype(F32)
            narrow_hidden[slot, pair] = hidden
            narrow_delta[slot, pair] = jnp.where(hidden > 0, acc_ref[slot, 1, pair], 0.0)

    spread(narrow_hidden, taps_hidden, pairs + 1, 8, side)
    spread(narrow_delta, taps_delta, pairs + 1, 8, side)

    first_grad = None
    second_grad = None
    copies = []
    contract_first = (((0,), (0,)), ((), ()))
    for slot in range(slots):
        out = jnp.dot(across(taps_hidden, slot, pairs, side), forward_ref[1], preferred_element_type=F32)
        back = lax.dot_general(
            across(taps_delta, slot, pairs, side), back_ref[0], contract_last, preferred_element_type=F32
        )
        for pair in range(pairs):
            lanes = slice(pair * LANES, (pair + 1) * LANES)
            rows = slice(pair * side, (pair + 1) * side)
            output_ref[slot, :, lanes] = out[rows].astype(BF16)
            grad_input_ref[slot, :, lanes] = back[rows].astype(BF16)
        for k, (source, target) in enumerate(((output_ref, output_hbm), (grad_input_ref, grad_input_hbm))):
            copies.append(pltpu.make_async_copy(source.at[slot], target.at[slot], sems.at[2 * slot + k]))
            copies[-1].start()
    for slot in range(slots):
        own_in, own_up = (
            wide[slot, 1 : pairs + 1, 16 : 16 + side, :].reshape(pairs * side, LANES).astype(BF16)
            for wide in (wide_in, wide_up)
        )
        term_one = lax.dot_general(
            own_in, across(taps_delta, slot, pairs, side), contract_first, preferred_element_type=F32
        )
        term_two = lax.dot_general(
            own_up, across(taps_hidden, slot, pairs, side), contract_first, preferred_element_type=F32
        )
        first_grad = term_one if first_grad is None else first_grad + term_one
        second_grad = term_two if second_grad is None else second_grad + term_two

    total = grads_ref.shape[0]
    lane = lax.broadcasted_iota(jnp.int32, (half, LANES), 1)
    for a in range(3):
        one = first_grad[:, (2 - a) * 256 : (3 - a) * 256]
        two = second_grad[:, a * 256 : (a + 1) * 256].T
        blocks = [one[:half, 0:LANES], one[:half, LANES:256], one[half:, 0:LANES], one[half:, LANES:256]]
        turned = [pltpu.roll(block, half, 1) for block in blocks]
        left = (blocks[0] + turned[2], turned[0] + blocks[3], blocks[1] + turned[3])
        for b in range(3):
            upper = two[b * half : (b + 1) * half]
            lower = two[(b + 1) * half : (b + 2) * half]
            right = pltpu.roll(upper, half, 1) + lower
            rows = slice((a * 3 + b) * half, (a * 3 + b + 1) * half)
            grads_ref[rows, :] = jnp.where(lane < half, left[2 - b], right).astype(BF16)
    if total > 576:
        grads_ref[576:total, :] = jnp.zeros((total - 576, LANES), BF16)
    for copy in copies:
        copy.wait()


def local(slide_image, cotangent, weight_one, weight_two, tissue, neighbours):
    devices_tile = lax.axis_size("tile")
    devices = devices_tile * lax.axis_size("slide")
    _, slots, side, width = slide_image.shape
    pairs = width // LANES
    tall = side + 16
    image, upstream = slide_image[0], cotangent[0]
    links = neighbours[0]
    packed = pl.pallas_call(
        pack_kernel,
        out_shape=jax.ShapeDtypeStruct((devices_tile, BLOCK, LANES), BF16),
        in_specs=[ANY] * 3,
        out_specs=VMEM,
        scratch_shapes=[
            pltpu.SMEM(links.shape, jnp.int32),
            pltpu.VMEM(image.shape, BF16),
            pltpu.VMEM(image.shape, BF16),
            pltpu.VMEM((2, 32, LANES), F32),
            pltpu.SemaphoreType.DMA((2 * slots + 1,)),
        ],
        compiler_params=pltpu.CompilerParams(vmem_limit_bytes=PACK_LIMIT),
        name="pack",
    )(links, image, upstream)
    halo = lax.all_to_all(packed, "tile", 0, 0, tiled=True)

    chunk = -(-576 // (2 * devices))
    total = 2 * chunk * devices
    output, grad_input, grads = pl.pallas_call(
        mix_kernel,
        out_shape=(
            jax.ShapeDtypeStruct((slots, side, width), BF16),
            jax.ShapeDtypeStruct((slots, side, width), BF16),
            jax.ShapeDtypeStruct((total, LANES), BF16),
        ),
        in_specs=[ANY, ANY] + [VMEM] * 5,
        out_specs=(ANY, ANY, VMEM),
        scratch_shapes=[
            pltpu.SMEM(links.shape, jnp.int32),
            pltpu.SMEM(tissue.shape, jnp.int32),
            pltpu.VMEM((slots, pairs + 2, side + 32, LANES), F32),
            pltpu.VMEM((slots, pairs + 2, side + 32, LANES), F32),
            pltpu.VMEM((slots, pairs + 1, tall, LANES), F32),
            pltpu.VMEM((slots, pairs + 1, tall, LANES), F32),
            pltpu.VMEM((slots, 3, pairs + 2, tall, LANES), BF16),
            pltpu.VMEM((slots, 3, pairs + 2, tall, LANES), BF16),
            pltpu.VMEM((slots, 3, pairs + 1, side, LANES), BF16),
            pltpu.VMEM((slots, 3, pairs + 1, side, LANES), BF16),
            pltpu.VMEM((2, 768, LANES), BF16),
            pltpu.VMEM((2, LANES, 768), BF16),
            pltpu.VMEM((slots, 2, pairs + 1, tall, LANES), F32),
            pltpu.VMEM((slots, side, width), BF16),
            pltpu.VMEM((slots, side, width), BF16),
            pltpu.SemaphoreType.DMA((2 * slots + 2,)),
        ],
        compiler_params=pltpu.CompilerParams(vmem_limit_bytes=48 * 2**20),
        name="mix",
    )(links, tissue, image, upstream, halo, weight_one, weight_two)

    parts = lax.all_to_all(grads.reshape(devices, chunk, 2, LANES), ("slide", "tile"), 0, 0, tiled=True)
    mine = jnp.sum(lax.optimization_barrier(parts.astype(F32)), axis=0).astype(BF16)
    sums = jnp.broadcast_to(mine[None], parts.shape)
    whole = lax.all_to_all(sums, ("slide", "tile"), 0, 0, tiled=True)
    whole = lax.optimization_barrier(whole.reshape(total, LANES).astype(F32))
    grad_one = whole[:576, : LANES // 2]
    grad_two = whole[:576, LANES // 2 :]
    shape = weight_one.shape
    return output[None], grad_input[None], grad_one.reshape(shape), grad_two.reshape(shape)


def solution(mesh):
    placed = (
        P("slide", "tile", None, None),
        P("slide", "tile", None, None),
        P(),
        P(),
        P("slide", "tile"),
        P("slide", "tile", None),
    )
    return jax.shard_map(
        local,
        mesh=mesh,
        in_specs=placed,
        out_specs=(P("slide", "tile", None, None), P("slide", "tile", None, None), P(), P()),
        check_vma=False,
    )
```

```python
import functools

import jax
import jax.numpy as jnp
from jax import lax
from jax.experimental import pallas as pl
from jax.experimental.pallas import tpu as pltpu
from jax.sharding import PartitionSpec as P

F32 = jnp.float32
BF16 = jnp.bfloat16
LANES = 128
VMEM = pl.BlockSpec(memory_space=pltpu.VMEM)
ANY = pl.BlockSpec(memory_space=pl.ANY)
PACK_LIMIT = 60 * 2**20


BLOCK = 2 * 96


def strip_row(field, slot):
    return field * 96 + slot * 32


def column_row(field):
    return field * 96 + 64


def forward_weights(source, forward):
    zero = jnp.zeros((LANES // 2, LANES // 2), BF16)
    for a in range(3):
        taps = [source[a, b] for b in range(3)]
        left = jnp.concatenate(taps + [zero], axis=0)
        right = jnp.concatenate([zero] + taps, axis=0)
        forward[a * 256 : (a + 1) * 256, :] = jnp.concatenate([left, right], axis=1)


def back_weights(source, back):
    zero = jnp.zeros((LANES // 2, LANES // 2), BF16)
    for a in range(3):
        turned = [source[2 - a, 2 - b] for b in range(3)]
        upper = jnp.concatenate(turned + [zero], axis=1)
        lower = jnp.concatenate([zero] + turned, axis=1)
        back[:, a * 256 : (a + 1) * 256] = jnp.concatenate([upper, lower], axis=0)


def across(taps, slot, count):
    rows = taps.shape[3]
    parts = [
        taps[slot, a, right : count + right].reshape(count * rows, LANES)
        for a in range(3)
        for right in range(2)
    ]
    return jnp.concatenate(parts, axis=1)


CONTRACT_FIRST = (((0,), (0,)), ((), ()))
CONTRACT_LAST = (((1,), (1,)), ((), ()))


def pack_kernel(
    links_hbm, image_hbm, cotangent_hbm, out_ref,
    links_ref, image_ref, cotangent_ref, strip_ref, sems,
):
    slots, side, width = image_ref.shape
    pairs = width // LANES
    copies = [pltpu.make_async_copy(links_hbm, links_ref, sems.at[2 * slots])]
    copies[0].start()
    fields = ((image_hbm, image_ref), (cotangent_hbm, cotangent_ref))
    for field, (source, target) in enumerate(fields):
        for slot in range(slots):
            copy = pltpu.make_async_copy(source.at[slot], target.at[slot], sems.at[field * slots + slot])
            copy.start()
            copies.append(copy)
    me = lax.axis_index("tile")
    copies[0].wait()
    for field, (_, ref) in enumerate(fields):
        for slot in range(slots):
            copies[1 + field * slots + slot].wait()
            top = ref[slot, 0:16, :].astype(F32)
            bottom = ref[slot, side - 16 : side, :].astype(F32)
            for pair in range(pairs):
                lanes = slice(pair * LANES, (pair + 1) * LANES)
                rows = slice(2 * pair, 2 * pair + 2)
                strip_ref[0, rows, :] = top[0:2, lanes]
                strip_ref[1, rows, :] = bottom[14:16, lanes]
            for direction in range(8):
                link = links_ref[slot, direction]

                @pl.when(link >= 0)
                def _(slot=slot, direction=direction, link=link, field=field, ref=ref):
                    device = link // slots
                    if direction in (2, 3):
                        first = jnp.where(device == me, strip_row(field, slot), column_row(field))
                        lanes = slice(0, LANES) if direction == 2 else slice(width - LANES, width)
                        out_ref[device, pl.ds(pl.multiple_of(first, 32), 32), :] = ref[slot, :, lanes]
                    else:
                        which = 0 if direction in (0, 4, 5) else 1
                        first = strip_row(field, slot)
                        out_ref[device, first : first + 32, :] = strip_ref[which].astype(BF16)


def mix_kernel(
    links_hbm, tissue_hbm, image_ref, cotangent_ref, halo_ref, one_ref, two_ref,
    grads_ref, taps_hidden, taps_delta,
    links_ref, tissue_ref, wide_in, wide_up, narrow_hidden, narrow_delta,
    taps_in, taps_up, forward_ref, back_ref, acc_ref, sems,
):
    slots, side, width = image_ref.shape
    pairs = width // LANES
    half = LANES // 2
    tall = side + 16
    me = lax.axis_index("tile")

    small = [
        pltpu.make_async_copy(tissue_hbm, tissue_ref, sems.at[0]),
        pltpu.make_async_copy(links_hbm, links_ref, sems.at[1]),
    ]
    for copy in small:
        copy.start()
    forward_weights(one_ref, forward_ref)
    back_weights(two_ref, back_ref)
    for copy in small:
        copy.wait()

    for field, (ref, wide) in enumerate(((image_ref, wide_in), (cotangent_ref, wide_up))):
        wide[:, :, 0:16, :] = jnp.zeros((slots, pairs + 2, 16, LANES), F32)
        wide[:, :, 16 + side : 32 + side, :] = jnp.zeros((slots, pairs + 2, 16, LANES), F32)
        for slot in range(slots):
            present = tissue_ref[0, slot] > 0
            for pair in range(pairs):
                block = ref[slot, :, pair * LANES : (pair + 1) * LANES].astype(F32)
                wide[slot, pair + 1, 16 : 16 + side, :] = jnp.where(present, block, 0.0)
            for direction in range(8):
                link = links_ref[slot, direction]
                device, there = jnp.maximum(link, 0) // slots, jnp.maximum(link, 0) % slots
                first = strip_row(field, 0) + there * 32
                if direction in (2, 3):
                    first = jnp.where(device == me, first, column_row(field))
                got = halo_ref[device, pl.ds(pl.multiple_of(first, 32), 32), :].astype(F32)
                got = jnp.where(link >= 0, got, 0.0)
                row = 14 if direction in (0, 4, 5) else 16 + side
                if direction in (2, 3):
                    wide[slot, 0 if direction == 2 else pairs + 1, 16 : 16 + side, :] = got
                elif direction < 2:
                    for pair in range(pairs):
                        wide[slot, pair + 1, row : row + 2, :] = got[2 * pair : 2 * pair + 2, :]
                elif direction in (4, 6):
                    wide[slot, 0, row : row + 2, :] = got[2 * pairs - 2 : 2 * pairs, :]
                else:
                    wide[slot, pairs + 1, row : row + 2, :] = got[0:2, :]

    def spread(field, taps, count, start, rows):
        for pair in range(count):
            for slot in range(slots):
                for a in range(3):
                    taps[slot, a, pair] = field[slot, pair, start + a - 1 : start + a - 1 + rows, :].astype(BF16)

    spread(wide_in, taps_in, pairs + 2, 8, tall)
    spread(wide_up, taps_up, pairs + 2, 8, tall)

    row = lax.broadcasted_iota(jnp.int32, (tall, LANES), 0)
    lane = lax.broadcasted_iota(jnp.int32, (tall, LANES), 1)

    def column_mask(north, here, south):
        value = jnp.where(row == 7, north, jnp.where(row == 8 + side, south, here))
        return jnp.where((row >= 7) & (row <= 8 + side), value, 0)

    for slot in range(slots):
        there = [(links_ref[slot, k] >= 0).astype(jnp.int32) for k in range(8)]
        own = tissue_ref[0, slot]
        middle = column_mask(there[0], own, there[1])
        west = jnp.where(lane < half, column_mask(there[4], there[2], there[6]), middle)
        east = jnp.where(lane < half, middle, column_mask(there[5], there[3], there[7]))

        first = jnp.dot(
            across(taps_in, slot, pairs + 1), forward_ref[...], preferred_element_type=F32
        )
        acc_ref[slot, 0] = first.reshape(pairs + 1, tall, LANES)
        second = lax.dot_general(
            across(taps_up, slot, pairs + 1), back_ref[...], CONTRACT_LAST,
            preferred_element_type=F32,
        )
        acc_ref[slot, 1] = second.reshape(pairs + 1, tall, LANES)

        for pair in range(pairs + 1):
            mask = west if pair == 0 else east if pair == pairs else middle
            hidden = jnp.where(mask > 0, jnp.maximum(acc_ref[slot, 0, pair], 0.0), 0.0)
            hidden = hidden.astype(BF16).astype(F32)
            narrow_hidden[slot, pair] = hidden
            narrow_delta[slot, pair] = jnp.where(hidden > 0, acc_ref[slot, 1, pair], 0.0)

    spread(narrow_hidden, taps_hidden, pairs + 1, 8, side)
    spread(narrow_delta, taps_delta, pairs + 1, 8, side)

    first_grad = None
    second_grad = None
    for slot in range(slots):
        own_in, own_up = (
            wide[slot, 1 : pairs + 1, 16 : 16 + side, :].reshape(pairs * side, LANES).astype(BF16)
            for wide in (wide_in, wide_up)
        )
        term_one = lax.dot_general(
            own_in, across(taps_delta, slot, pairs), CONTRACT_FIRST, preferred_element_type=F32
        )
        term_two = lax.dot_general(
            own_up, across(taps_hidden, slot, pairs), CONTRACT_FIRST, preferred_element_type=F32
        )
        first_grad = term_one if first_grad is None else first_grad + term_one
        second_grad = term_two if second_grad is None else second_grad + term_two

    total = grads_ref.shape[0]
    lane = lax.broadcasted_iota(jnp.int32, (half, LANES), 1)
    for a in range(3):
        one = first_grad[:, (2 - a) * 256 : (3 - a) * 256]
        two = second_grad[:, a * 256 : (a + 1) * 256].T
        blocks = [one[:half, 0:LANES], one[:half, LANES:256], one[half:, 0:LANES], one[half:, LANES:256]]
        turned = [pltpu.roll(block, half, 1) for block in blocks]
        left = (blocks[0] + turned[2], turned[0] + blocks[3], blocks[1] + turned[3])
        for b in range(3):
            upper = two[b * half : (b + 1) * half]
            lower = two[(b + 1) * half : (b + 2) * half]
            right = pltpu.roll(upper, half, 1) + lower
            rows = slice((a * 3 + b) * half, (a * 3 + b + 1) * half)
            grads_ref[rows, :] = jnp.where(lane < half, left[2 - b], right).astype(BF16)
    if total > 576:
        grads_ref[576:total, :] = jnp.zeros((total - 576, LANES), BF16)


def outer_kernel(
    taps_hidden, taps_delta, one_ref, two_ref,
    output_hbm, grad_input_hbm,
    forward_ref, back_ref, output_ref, grad_input_ref, sems,
):
    slots, side, width = output_ref.shape
    pairs = width // LANES
    forward_weights(two_ref, forward_ref)
    back_weights(one_ref, back_ref)
    copies = []
    for slot in range(slots):
        out = jnp.dot(across(taps_hidden, slot, pairs), forward_ref[...], preferred_element_type=F32)
        back = lax.dot_general(
            across(taps_delta, slot, pairs), back_ref[...], CONTRACT_LAST, preferred_element_type=F32
        )
        for pair in range(pairs):
            lanes = slice(pair * LANES, (pair + 1) * LANES)
            rows = slice(pair * side, (pair + 1) * side)
            output_ref[slot, :, lanes] = out[rows].astype(BF16)
            grad_input_ref[slot, :, lanes] = back[rows].astype(BF16)
        for k, (source, target) in enumerate(((output_ref, output_hbm), (grad_input_ref, grad_input_hbm))):
            copies.append(pltpu.make_async_copy(source.at[slot], target.at[slot], sems.at[2 * slot + k]))
            copies[-1].start()
    for copy in copies:
        copy.wait()


def local(slide_image, cotangent, weight_one, weight_two, tissue, neighbours):
    devices_tile = lax.axis_size("tile")
    devices = devices_tile * lax.axis_size("slide")
    _, slots, side, width = slide_image.shape
    pairs = width // LANES
    tall = side + 16
    image, upstream = slide_image[0], cotangent[0]
    links = neighbours[0]
    packed = pl.pallas_call(
        pack_kernel,
        out_shape=jax.ShapeDtypeStruct((devices_tile, BLOCK, LANES), BF16),
        in_specs=[ANY] * 3,
        out_specs=VMEM,
        scratch_shapes=[
            pltpu.SMEM(links.shape, jnp.int32),
            pltpu.VMEM(image.shape, BF16),
            pltpu.VMEM(image.shape, BF16),
            pltpu.VMEM((2, 32, LANES), F32),
            pltpu.SemaphoreType.DMA((2 * slots + 1,)),
        ],
        compiler_params=pltpu.CompilerParams(vmem_limit_bytes=PACK_LIMIT),
        name="pack",
    )(links, image, upstream)
    halo = lax.all_to_all(packed, "tile", 0, 0, tiled=True)

    chunk = -(-576 // (2 * devices))
    total = 2 * chunk * devices
    taps = jax.ShapeDtypeStruct((slots, 3, pairs + 1, side, LANES), BF16)
    grads, taps_hidden, taps_delta = pl.pallas_call(
        mix_kernel,
        out_shape=(jax.ShapeDtypeStruct((total, LANES), BF16), taps, taps),
        in_specs=[ANY, ANY] + [VMEM] * 5,
        out_specs=(VMEM,) * 3,
        scratch_shapes=[
            pltpu.SMEM(links.shape, jnp.int32),
            pltpu.SMEM(tissue.shape, jnp.int32),
            pltpu.VMEM((slots, pairs + 2, side + 32, LANES), F32),
            pltpu.VMEM((slots, pairs + 2, side + 32, LANES), F32),
            pltpu.VMEM((slots, pairs + 1, tall, LANES), F32),
            pltpu.VMEM((slots, pairs + 1, tall, LANES), F32),
            pltpu.VMEM((slots, 3, pairs + 2, tall, LANES), BF16),
            pltpu.VMEM((slots, 3, pairs + 2, tall, LANES), BF16),
            pltpu.VMEM((768, LANES), BF16),
            pltpu.VMEM((LANES, 768), BF16),
            pltpu.VMEM((slots, 2, pairs + 1, tall, LANES), F32),
            pltpu.SemaphoreType.DMA((2,)),
        ],
        compiler_params=pltpu.CompilerParams(vmem_limit_bytes=40 * 2**20),
        cost_estimate=pl.CostEstimate(flops=4 * 10**9, bytes_accessed=10**7, transcendentals=0),
        name="mix",
    )(links, tissue, image, upstream, halo, weight_one, weight_two)
    output, grad_input = pl.pallas_call(
        outer_kernel,
        out_shape=(jax.ShapeDtypeStruct((slots, side, width), BF16),) * 2,
        in_specs=[VMEM] * 4,
        out_specs=(ANY, ANY),
        scratch_shapes=[
            pltpu.VMEM((768, LANES), BF16),
            pltpu.VMEM((LANES, 768), BF16),
            pltpu.VMEM((slots, side, width), BF16),
            pltpu.VMEM((slots, side, width), BF16),
            pltpu.SemaphoreType.DMA((2 * slots,)),
        ],
        compiler_params=pltpu.CompilerParams(vmem_limit_bytes=24 * 2**20),
        cost_estimate=pl.CostEstimate(flops=4 * 10**9, bytes_accessed=10**7, transcendentals=0),
        name="outer",
    )(taps_hidden, taps_delta, weight_one, weight_two)

    parts = lax.all_to_all(grads.reshape(devices, chunk, 2, LANES), ("slide", "tile"), 0, 0, tiled=True)
    mine = jnp.sum(lax.optimization_barrier(parts.astype(F32)), axis=0).astype(BF16)
    sums = jnp.broadcast_to(mine[None], parts.shape)
    whole = lax.all_to_all(sums, ("slide", "tile"), 0, 0, tiled=True)
    whole = lax.optimization_barrier(whole.reshape(total, LANES).astype(F32))
    grad_one = whole[:576, : LANES // 2]
    grad_two = whole[:576, LANES // 2 :]
    shape = weight_one.shape
    return output[None], grad_input[None], grad_one.reshape(shape), grad_two.reshape(shape)


def solution(mesh):
    placed = (
        P("slide", "tile", None, None),
        P("slide", "tile", None, None),
        P(),
        P(),
        P("slide", "tile"),
        P("slide", "tile", None),
    )
    return jax.shard_map(
        local,
        mesh=mesh,
        in_specs=placed,
        out_specs=(P("slide", "tile", None, None), P("slide", "tile", None, None), P(), P()),
        check_vma=False,
    )
```

```python
import functools

import jax
import jax.numpy as jnp
from jax import lax
from jax.experimental import pallas as pl
from jax.experimental.pallas import tpu as pltpu
from jax.sharding import PartitionSpec as P

F32 = jnp.float32
BF16 = jnp.bfloat16
LANES = 128
VMEM = pl.BlockSpec(memory_space=pltpu.VMEM)
ANY = pl.BlockSpec(memory_space=pl.ANY)
PACK_LIMIT = 60 * 2**20


BLOCK = 2 * 48


def strip_row(field, slot):
    return field * 48 + slot * 16


def column_row(field):
    return field * 48 + 32


def forward_weights(source, forward):
    zero = jnp.zeros((LANES // 2, LANES // 2), BF16)
    for a in range(3):
        taps = [source[a, b] for b in range(3)]
        left = jnp.concatenate(taps + [zero], axis=0)
        right = jnp.concatenate([zero] + taps, axis=0)
        forward[a * 256 : (a + 1) * 256, :] = jnp.concatenate([left, right], axis=1)


def back_weights(source, back):
    zero = jnp.zeros((LANES // 2, LANES // 2), BF16)
    for a in range(3):
        turned = [source[2 - a, 2 - b] for b in range(3)]
        upper = jnp.concatenate(turned + [zero], axis=1)
        lower = jnp.concatenate([zero] + turned, axis=1)
        back[:, a * 256 : (a + 1) * 256] = jnp.concatenate([upper, lower], axis=0)


def across(taps, slot, count):
    rows = taps.shape[3]
    parts = [
        taps[slot, a, right : count + right].reshape(count * rows, LANES)
        for a in range(3)
        for right in range(2)
    ]
    return jnp.concatenate(parts, axis=1)


CONTRACT_FIRST = (((0,), (0,)), ((), ()))
CONTRACT_LAST = (((1,), (1,)), ((), ()))


def pack_kernel(
    links_hbm, image_hbm, cotangent_hbm, inner_ref, outer_ref,
    links_ref, image_ref, cotangent_ref, strip_ref, sems,
):
    slots, side, width = image_ref.shape
    pairs = width // LANES
    half = LANES // 2
    copies = [pltpu.make_async_copy(links_hbm, links_ref, sems.at[2 * slots])]
    copies[0].start()
    fields = ((image_hbm, image_ref), (cotangent_hbm, cotangent_ref))
    for field, (source, target) in enumerate(fields):
        for slot in range(slots):
            copy = pltpu.make_async_copy(source.at[slot], target.at[slot], sems.at[field * slots + slot])
            copy.start()
            copies.append(copy)
    me = lax.axis_index("tile")
    left = lax.broadcasted_iota(jnp.int32, (16, LANES), 1) < half
    copies[0].wait()
    for field, (_, ref) in enumerate(fields):
        for slot in range(slots):
            copies[1 + field * slots + slot].wait()
            top = ref[slot, 0:16, :].astype(F32)
            bottom = ref[slot, side - 16 : side, :].astype(F32)
            for pair in range(pairs):
                lanes = slice(pair * LANES, (pair + 1) * LANES)
                strip_ref[0, pair : pair + 1, :] = top[0:1, lanes]
                strip_ref[1, pair : pair + 1, :] = top[1:2, lanes]
                strip_ref[2, pair : pair + 1, :] = bottom[15:16, lanes]
                strip_ref[3, pair : pair + 1, :] = bottom[14:15, lanes]
            for direction in range(8):
                link = links_ref[slot, direction]

                @pl.when(link >= 0)
                def _(slot=slot, direction=direction, link=link, field=field, ref=ref):
                    device = link // slots
                    if direction in (2, 3):
                        first = jnp.where(device == me, strip_row(field, slot), column_row(field))
                        at = pl.ds(pl.multiple_of(first, 16), 16)
                        lanes = slice(0, LANES) if direction == 2 else slice(width - LANES, width)
                        block = ref[slot, :, lanes].astype(F32)
                        other = pltpu.roll(block, half, 1)
                        low = jnp.where(left, block[0:16], other[16:32]).astype(BF16)
                        high = jnp.where(left, other[0:16], block[16:32]).astype(BF16)
                        inner_ref[device, at, :] = low if direction == 2 else high
                        outer_ref[device, at, :] = high if direction == 2 else low
                    else:
                        which = 0 if direction in (0, 4, 5) else 2
                        first = strip_row(field, slot)
                        inner_ref[device, first : first + 16, :] = strip_ref[which].astype(BF16)
                        outer_ref[device, first : first + 16, :] = strip_ref[which + 1].astype(BF16)


def place_halo(links_ref, halos, wide, slot, field, slots, side, pairs, me):
    half = LANES // 2
    left = lax.broadcasted_iota(jnp.int32, (16, LANES), 1) < half
    none = jnp.zeros((16, LANES), F32)
    for direction in range(8):
        link = links_ref[slot, direction]
        device, there = jnp.maximum(link, 0) // slots, jnp.maximum(link, 0) % slots
        first = strip_row(field, 0) + there * 16
        if direction in (2, 3):
            first = jnp.where(device == me, first, column_row(field))
        at = pl.ds(pl.multiple_of(first, 16), 16)
        got = [jnp.where(link >= 0, halo[device, at, :].astype(F32), 0.0) for halo in halos]
        if direction in (2, 3):
            inner, outer = got[0], got[1] if len(got) > 1 else none
            low, high = (outer, inner) if direction == 2 else (inner, outer)
            column = 0 if direction == 2 else pairs + 1
            wide[slot, column, 16:32, :] = jnp.where(left, low, pltpu.roll(high, half, 1))
            wide[slot, column, 32:48, :] = jnp.where(left, pltpu.roll(low, half, 1), high)
        else:
            north = direction in (0, 4, 5)
            for ring, strip in enumerate(got):
                row = 15 - ring if north else 16 + side + ring
                if direction < 2:
                    for pair in range(pairs):
                        wide[slot, pair + 1, row : row + 1, :] = strip[pair : pair + 1, :]
                elif direction in (4, 6):
                    wide[slot, 0, row : row + 1, :] = strip[pairs - 1 : pairs, :]
                else:
                    wide[slot, pairs + 1, row : row + 1, :] = strip[0:1, :]


def place_own(tissue_ref, ref, wide, slot, side, pairs):
    present = tissue_ref[0, slot] > 0
    for pair in range(pairs):
        block = ref[slot, :, pair * LANES : (pair + 1) * LANES].astype(F32)
        wide[slot, pair + 1, 16 : 16 + side, :] = jnp.where(present, block, 0.0)


def shift_rows(field, taps, count, start, rows):
    for pair in range(count):
        for slot in range(field.shape[0]):
            for a in range(3):
                taps[slot, a, pair] = field[slot, pair, start + a - 1 : start + a - 1 + rows, :].astype(BF16)


def grads_kernel(
    links_hbm, tissue_hbm, image_ref, cotangent_ref, inner_ref, one_ref, two_ref,
    grads_ref,
    links_ref, tissue_ref, wide_in, wide_up, own_hidden, own_delta,
    taps_in, taps_up, forward_ref, back_ref, acc_ref, sems,
):
    slots, side, width = image_ref.shape
    pairs = width // LANES
    half = LANES // 2
    me = lax.axis_index("tile")

    small = [
        pltpu.make_async_copy(tissue_hbm, tissue_ref, sems.at[0]),
        pltpu.make_async_copy(links_hbm, links_ref, sems.at[1]),
    ]
    for copy in small:
        copy.start()
    forward_weights(one_ref, forward_ref)
    back_weights(two_ref, back_ref)
    for copy in small:
        copy.wait()
    for field, (ref, wide) in enumerate(((image_ref, wide_in), (cotangent_ref, wide_up))):
        for slot in range(slots):
            place_own(tissue_ref, ref, wide, slot, side, pairs)
            place_halo(links_ref, (inner_ref,), wide, slot, field, slots, side, pairs, me)
    shift_rows(wide_in, taps_in, pairs + 2, 16, side)
    shift_rows(wide_up, taps_up, pairs + 2, 16, side)

    left = lax.broadcasted_iota(jnp.int32, (side, LANES), 1) < half
    first_grad = None
    second_grad = None
    for slot in range(slots):
        before = jnp.dot(across(taps_in, slot, pairs + 1), forward_ref[...], preferred_element_type=F32)
        acc_ref[slot, 0] = before.reshape(pairs + 1, side, LANES)
        after = lax.dot_general(
            across(taps_up, slot, pairs + 1), back_ref[...], CONTRACT_LAST, preferred_element_type=F32
        )
        acc_ref[slot, 1] = after.reshape(pairs + 1, side, LANES)
        for pair in range(pairs + 1):
            hidden = jnp.maximum(acc_ref[slot, 0, pair], 0.0)
            if pair == 0:
                hidden = jnp.where(left, 0.0, hidden)
            if pair == pairs:
                hidden = jnp.where(left, hidden, 0.0)
            hidden = hidden.astype(BF16)
            own_hidden[slot, pair] = hidden
            delta = jnp.where(hidden.astype(F32) > 0, acc_ref[slot, 1, pair], 0.0)
            own_delta[slot, pair] = delta.astype(BF16)
        term_one = lax.dot_general(
            own_delta[slot].reshape((pairs + 1) * side, LANES), across(taps_in, slot, pairs + 1),
            CONTRACT_FIRST, preferred_element_type=F32,
        )
        term_two = lax.dot_general(
            own_hidden[slot].reshape((pairs + 1) * side, LANES), across(taps_up, slot, pairs + 1),
            CONTRACT_FIRST, preferred_element_type=F32,
        )
        first_grad = term_one if first_grad is None else first_grad + term_one
        second_grad = term_two if second_grad is None else second_grad + term_two

    total = grads_ref.shape[0]
    left = lax.broadcasted_iota(jnp.int32, (half, LANES), 1) < half
    for a in range(3):
        one = first_grad[:, a * 256 : (a + 1) * 256].T
        two = second_grad[:, (2 - a) * 256 : (3 - a) * 256]
        blocks = [two[:half, 0:LANES], two[:half, LANES:256], two[half:, 0:LANES], two[half:, LANES:256]]
        turned = [pltpu.roll(block, half, 1) for block in blocks]
        right = (turned[0] + blocks[2], blocks[0] + turned[3], turned[1] + blocks[3])
        for b in range(3):
            upper = one[b * half : (b + 1) * half]
            lower = one[(b + 1) * half : (b + 2) * half]
            rows = slice((a * 3 + b) * half, (a * 3 + b + 1) * half)
            both = jnp.where(left, upper + pltpu.roll(lower, half, 1), right[2 - b])
            grads_ref[rows, :] = both.astype(BF16)
    if total > 576:
        grads_ref[576:total, :] = jnp.zeros((total - 576, LANES), BF16)


def fields_kernel(
    links_hbm, tissue_hbm, image_ref, cotangent_ref, inner_ref, outer_ref, one_ref, two_ref,
    output_hbm, grad_input_hbm,
    links_ref, tissue_ref, wide_in, wide_up, narrow_hidden, narrow_delta,
    taps_in, taps_up, taps_hidden, taps_delta, forward_one, forward_two, back_one, back_two,
    acc_ref, output_ref, grad_input_ref, sems,
):
    slots, side, width = image_ref.shape
    pairs = width // LANES
    half = LANES // 2
    tall = side + 16
    me = lax.axis_index("tile")

    small = [
        pltpu.make_async_copy(tissue_hbm, tissue_ref, sems.at[2 * slots]),
        pltpu.make_async_copy(links_hbm, links_ref, sems.at[2 * slots + 1]),
    ]
    for copy in small:
        copy.start()
    forward_weights(one_ref, forward_one)
    forward_weights(two_ref, forward_two)
    back_weights(one_ref, back_one)
    back_weights(two_ref, back_two)
    for copy in small:
        copy.wait()
    for field, (ref, wide) in enumerate(((image_ref, wide_in), (cotangent_ref, wide_up))):
        wide[:, :, 0:16, :] = jnp.zeros((slots, pairs + 2, 16, LANES), F32)
        wide[:, :, 16 + side : 32 + side, :] = jnp.zeros((slots, pairs + 2, 16, LANES), F32)
        for slot in range(slots):
            place_own(tissue_ref, ref, wide, slot, side, pairs)
            place_halo(links_ref, (inner_ref, outer_ref), wide, slot, field, slots, side, pairs, me)
    shift_rows(wide_in, taps_in, pairs + 2, 8, tall)
    shift_rows(wide_up, taps_up, pairs + 2, 8, tall)

    row = lax.broadcasted_iota(jnp.int32, (tall, LANES), 0)
    lane = lax.broadcasted_iota(jnp.int32, (tall, LANES), 1)

    def column_mask(north, here, south):
        value = jnp.where(row == 7, north, jnp.where(row == 8 + side, south, here))
        return jnp.where((row >= 7) & (row <= 8 + side), value, 0)

    for slot in range(slots):
        there = [(links_ref[slot, k] >= 0).astype(jnp.int32) for k in range(8)]
        own = tissue_ref[0, slot]
        middle = column_mask(there[0], own, there[1])
        west = jnp.where(lane < half, column_mask(there[4], there[2], there[6]), middle)
        east = jnp.where(lane < half, middle, column_mask(there[5], there[3], there[7]))
        before = jnp.dot(across(taps_in, slot, pairs + 1), forward_one[...], preferred_element_type=F32)
        acc_ref[slot, 0] = before.reshape(pairs + 1, tall, LANES)
        after = lax.dot_general(
            across(taps_up, slot, pairs + 1), back_two[...], CONTRACT_LAST, preferred_element_type=F32
        )
        acc_ref[slot, 1] = after.reshape(pairs + 1, tall, LANES)
        for pair in range(pairs + 1):
            mask = west if pair == 0 else east if pair == pairs else middle
            hidden = jnp.where(mask > 0, jnp.maximum(acc_ref[slot, 0, pair], 0.0), 0.0)
            hidden = hidden.astype(BF16).astype(F32)
            narrow_hidden[slot, pair] = hidden
            narrow_delta[slot, pair] = jnp.where(hidden > 0, acc_ref[slot, 1, pair], 0.0)
    shift_rows(narrow_hidden, taps_hidden, pairs + 1, 8, side)
    shift_rows(narrow_delta, taps_delta, pairs + 1, 8, side)

    copies = []
    for slot in range(slots):
        out = jnp.dot(across(taps_hidden, slot, pairs), forward_two[...], preferred_element_type=F32)
        back = lax.dot_general(
            across(taps_delta, slot, pairs), back_one[...], CONTRACT_LAST, preferred_element_type=F32
        )
        for pair in range(pairs):
            lanes = slice(pair * LANES, (pair + 1) * LANES)
            rows = slice(pair * side, (pair + 1) * side)
            output_ref[slot, :, lanes] = out[rows].astype(BF16)
            grad_input_ref[slot, :, lanes] = back[rows].astype(BF16)
        for k, (source, target) in enumerate(((output_ref, output_hbm), (grad_input_ref, grad_input_hbm))):
            copies.append(pltpu.make_async_copy(source.at[slot], target.at[slot], sems.at[2 * slot + k]))
            copies[-1].start()
    for copy in copies:
        copy.wait()


def local(slide_image, cotangent, weight_one, weight_two, tissue, neighbours):
    devices_tile = lax.axis_size("tile")
    devices = devices_tile * lax.axis_size("slide")
    _, slots, side, width = slide_image.shape
    pairs = width // LANES
    tall = side + 16
    image, upstream = slide_image[0], cotangent[0]
    links = neighbours[0]
    block = jax.ShapeDtypeStruct((devices_tile, BLOCK, LANES), BF16)
    packed_inner, packed_outer = pl.pallas_call(
        pack_kernel,
        out_shape=(block, block),
        in_specs=[ANY] * 3,
        out_specs=(VMEM, VMEM),
        scratch_shapes=[
            pltpu.SMEM(links.shape, jnp.int32),
            pltpu.VMEM(image.shape, BF16),
            pltpu.VMEM(image.shape, BF16),
            pltpu.VMEM((4, 16, LANES), F32),
            pltpu.SemaphoreType.DMA((2 * slots + 1,)),
        ],
        compiler_params=pltpu.CompilerParams(vmem_limit_bytes=PACK_LIMIT),
        name="pack",
    )(links, image, upstream)
    inner = lax.all_to_all(packed_inner, "tile", 0, 0, tiled=True)
    outer = lax.all_to_all(packed_outer, "tile", 0, 0, tiled=True)

    chunk = -(-576 // (2 * devices))
    total = 2 * chunk * devices
    wide = pltpu.VMEM((slots, pairs + 2, side + 32, LANES), F32)
    weights = [pltpu.VMEM((768, LANES), BF16), pltpu.VMEM((LANES, 768), BF16)]
    cost = pl.CostEstimate(flops=4 * 10**9, bytes_accessed=10**7, transcendentals=0)
    grads = pl.pallas_call(
        grads_kernel,
        out_shape=jax.ShapeDtypeStruct((total, LANES), BF16),
        in_specs=[ANY, ANY] + [VMEM] * 5,
        out_specs=VMEM,
        scratch_shapes=[
            pltpu.SMEM(links.shape, jnp.int32),
            pltpu.SMEM(tissue.shape, jnp.int32),
            wide,
            wide,
            pltpu.VMEM((slots, pairs + 1, side, LANES), BF16),
            pltpu.VMEM((slots, pairs + 1, side, LANES), BF16),
            pltpu.VMEM((slots, 3, pairs + 2, side, LANES), BF16),
            pltpu.VMEM((slots, 3, pairs + 2, side, LANES), BF16),
            *weights,
            pltpu.VMEM((slots, 2, pairs + 1, side, LANES), F32),
            pltpu.SemaphoreType.DMA((2,)),
        ],
        compiler_params=pltpu.CompilerParams(vmem_limit_bytes=32 * 2**20),
        cost_estimate=cost,
        name="grads",
    )(links, tissue, image, upstream, inner, weight_one, weight_two)
    output, grad_input = pl.pallas_call(
        fields_kernel,
        out_shape=(jax.ShapeDtypeStruct((slots, side, width), BF16),) * 2,
        in_specs=[ANY, ANY] + [VMEM] * 6,
        out_specs=(ANY, ANY),
        scratch_shapes=[
            pltpu.SMEM(links.shape, jnp.int32),
            pltpu.SMEM(tissue.shape, jnp.int32),
            wide,
            wide,
            pltpu.VMEM((slots, pairs + 1, tall, LANES), F32),
            pltpu.VMEM((slots, pairs + 1, tall, LANES), F32),
            pltpu.VMEM((slots, 3, pairs + 2, tall, LANES), BF16),
            pltpu.VMEM((slots, 3, pairs + 2, tall, LANES), BF16),
            pltpu.VMEM((slots, 3, pairs + 1, side, LANES), BF16),
            pltpu.VMEM((slots, 3, pairs + 1, side, LANES), BF16),
            weights[0],
            weights[0],
            weights[1],
            weights[1],
            pltpu.VMEM((slots, 2, pairs + 1, tall, LANES), F32),
            pltpu.VMEM((slots, side, width), BF16),
            pltpu.VMEM((slots, side, width), BF16),
            pltpu.SemaphoreType.DMA((2 * slots + 2,)),
        ],
        compiler_params=pltpu.CompilerParams(vmem_limit_bytes=40 * 2**20),
        cost_estimate=cost,
        name="fields",
    )(links, tissue, image, upstream, inner, outer, weight_one, weight_two)

    parts = lax.all_to_all(grads.reshape(devices, chunk, 2, LANES), ("slide", "tile"), 0, 0, tiled=True)
    mine = jnp.sum(lax.optimization_barrier(parts.astype(F32)), axis=0).astype(BF16)
    sums = jnp.broadcast_to(mine[None], parts.shape)
    whole = lax.all_to_all(sums, ("slide", "tile"), 0, 0, tiled=True)
    whole = lax.optimization_barrier(whole.reshape(total, LANES).astype(F32))
    grad_one = whole[:576, : LANES // 2]
    grad_two = whole[:576, LANES // 2 :]
    shape = weight_one.shape
    return output[None], grad_input[None], grad_one.reshape(shape), grad_two.reshape(shape)


def solution(mesh):
    placed = (
        P("slide", "tile", None, None),
        P("slide", "tile", None, None),
        P(),
        P(),
        P("slide", "tile"),
        P("slide", "tile", None),
    )
    return jax.shard_map(
        local,
        mesh=mesh,
        in_specs=placed,
        out_specs=(P("slide", "tile", None, None), P("slide", "tile", None, None), P(), P()),
        check_vma=False,
    )
```

```python
import functools

import jax
import jax.numpy as jnp
from jax import lax
from jax.experimental import pallas as pl
from jax.experimental.pallas import tpu as pltpu
from jax.sharding import PartitionSpec as P

F32 = jnp.float32
BF16 = jnp.bfloat16
LANES = 128
VMEM = pl.BlockSpec(memory_space=pltpu.VMEM)
ANY = pl.BlockSpec(memory_space=pl.ANY)
PACK_LIMIT = 60 * 2**20


BLOCK = 2 * 96


def strip_row(field, slot):
    return field * 96 + slot * 32


def column_row(field):
    return field * 96 + 64


def band_weights(source, forward, back):
    half = LANES // 2
    zero = jnp.zeros((half, half), BF16)
    for a in range(3):
        taps = [source[a, b] for b in range(3)]
        left = jnp.concatenate(taps + [zero], axis=0)
        right = jnp.concatenate([zero] + taps, axis=0)
        forward[a * 256 : (a + 1) * 256, :] = jnp.concatenate([left, right], axis=1)
        turned = [source[2 - a, 2 - b] for b in range(3)]
        upper = jnp.concatenate(turned + [zero], axis=1)
        lower = jnp.concatenate([zero] + turned, axis=1)
        back[:, a * 256 : (a + 1) * 256] = jnp.concatenate([upper, lower], axis=0)


def pack_kernel(
    links_hbm, image_hbm, cotangent_hbm, out_ref,
    links_ref, image_ref, cotangent_ref, strip_ref, sems,
):
    slots, side, width = image_ref.shape
    pairs = width // LANES
    copies = [pltpu.make_async_copy(links_hbm, links_ref, sems.at[2 * slots])]
    copies[0].start()
    fields = ((image_hbm, image_ref), (cotangent_hbm, cotangent_ref))
    for field, (source, target) in enumerate(fields):
        for slot in range(slots):
            copy = pltpu.make_async_copy(source.at[slot], target.at[slot], sems.at[field * slots + slot])
            copy.start()
            copies.append(copy)
    me = lax.axis_index("tile")
    copies[0].wait()
    for field, (_, ref) in enumerate(fields):
        for slot in range(slots):
            copies[1 + field * slots + slot].wait()
            top = ref[slot, 0:16, :].astype(F32)
            bottom = ref[slot, side - 16 : side, :].astype(F32)
            for pair in range(pairs):
                lanes = slice(pair * LANES, (pair + 1) * LANES)
                rows = slice(2 * pair, 2 * pair + 2)
                strip_ref[0, rows, :] = top[0:2, lanes]
                strip_ref[1, rows, :] = bottom[14:16, lanes]
            for direction in range(8):
                link = links_ref[slot, direction]

                @pl.when(link >= 0)
                def _(slot=slot, direction=direction, link=link, field=field, ref=ref):
                    device = link // slots
                    if direction in (2, 3):
                        first = jnp.where(device == me, strip_row(field, slot), column_row(field))
                        lanes = slice(0, LANES) if direction == 2 else slice(width - LANES, width)
                        out_ref[device, pl.ds(pl.multiple_of(first, 32), 32), :] = ref[slot, :, lanes]
                    else:
                        which = 0 if direction in (0, 4, 5) else 1
                        first = strip_row(field, slot)
                        out_ref[device, first : first + 32, :] = strip_ref[which].astype(BF16)


def mix_kernel(
    links_hbm, tissue_hbm, image_ref, cotangent_ref, halo_ref, one_ref, two_ref,
    output_hbm, grad_input_hbm, grads_ref,
    links_ref, tissue_ref, wide_in, wide_up, narrow_hidden, narrow_delta,
    taps_in, taps_up, taps_hidden, taps_delta, forward_ref, back_ref, acc_ref, output_ref, grad_input_ref, sems,
):
    slots, side, width = image_ref.shape
    pairs = width // LANES
    half = LANES // 2
    tall = side + 16
    me = lax.axis_index("tile")

    small = [
        pltpu.make_async_copy(tissue_hbm, tissue_ref, sems.at[2 * slots]),
        pltpu.make_async_copy(links_hbm, links_ref, sems.at[2 * slots + 1]),
    ]
    for copy in small:
        copy.start()
    band_weights(one_ref, forward_ref.at[0], back_ref.at[0])
    band_weights(two_ref, forward_ref.at[1], back_ref.at[1])
    for copy in small:
        copy.wait()

    for field, (ref, wide) in enumerate(((image_ref, wide_in), (cotangent_ref, wide_up))):
        wide[:, :, 0:16, :] = jnp.zeros((slots, pairs + 2, 16, LANES), F32)
        wide[:, :, 16 + side : 32 + side, :] = jnp.zeros((slots, pairs + 2, 16, LANES), F32)
        for slot in range(slots):
            present = tissue_ref[0, slot] > 0
            for pair in range(pairs):
                block = ref[slot, :, pair * LANES : (pair + 1) * LANES].astype(F32)
                wide[slot, pair + 1, 16 : 16 + side, :] = jnp.where(present, block, 0.0)
            for direction in range(8):
                link = links_ref[slot, direction]
                device, there = jnp.maximum(link, 0) // slots, jnp.maximum(link, 0) % slots
                first = strip_row(field, 0) + there * 32
                if direction in (2, 3):
                    first = jnp.where(device == me, first, column_row(field))
                got = halo_ref[device, pl.ds(pl.multiple_of(first, 32), 32), :].astype(F32)
                got = jnp.where(link >= 0, got, 0.0)
                row = 14 if direction in (0, 4, 5) else 16 + side
                if direction in (2, 3):
                    wide[slot, 0 if direction == 2 else pairs + 1, 16 : 16 + side, :] = got
                elif direction < 2:
                    for pair in range(pairs):
                        wide[slot, pair + 1, row : row + 2, :] = got[2 * pair : 2 * pair + 2, :]
                elif direction in (4, 6):
                    wide[slot, 0, row : row + 2, :] = got[2 * pairs - 2 : 2 * pairs, :]
                else:
                    wide[slot, pairs + 1, row : row + 2, :] = got[0:2, :]

    def spread(field, taps, count, start, rows):
        for pair in range(count):
            for slot in range(slots):
                for a in range(3):
                    taps[slot, a, pair] = field[slot, pair, start + a - 1 : start + a - 1 + rows, :].astype(BF16)

    spread(wide_in, taps_in, pairs + 2, 8, tall)
    spread(wide_up, taps_up, pairs + 2, 8, tall)

    row = lax.broadcasted_iota(jnp.int32, (tall, LANES), 0)
    lane = lax.broadcasted_iota(jnp.int32, (tall, LANES), 1)

    def column_mask(north, here, south):
        value = jnp.where(row == 7, north, jnp.where(row == 8 + side, south, here))
        return jnp.where((row >= 7) & (row <= 8 + side), value, 0)

    def across(taps, slot, count, rows):
        parts = [
            taps[slot, a, right : count + right].reshape(count * rows, LANES)
            for a in range(3)
            for right in range(2)
        ]
        return jnp.concatenate(parts, axis=1)

    contract_last = (((1,), (1,)), ((), ()))
    for slot in range(slots):
        there = [(links_ref[slot, k] >= 0).astype(jnp.int32) for k in range(8)]
        own = tissue_ref[0, slot]
        middle = column_mask(there[0], own, there[1])
        west = jnp.where(lane < half, column_mask(there[4], there[2], there[6]), middle)
        east = jnp.where(lane < half, middle, column_mask(there[5], there[3], there[7]))

        first = jnp.dot(
            across(taps_in, slot, pairs + 1, tall), forward_ref[0], preferred_element_type=F32
        )
        acc_ref[slot, 0] = first.reshape(pairs + 1, tall, LANES)
        second = lax.dot_general(
            across(taps_up, slot, pairs + 1, tall), back_ref[1], contract_last,
            preferred_element_type=F32,
        )
        acc_ref[slot, 1] = second.reshape(pairs + 1, tall, LANES)

        for pair in range(pairs + 1):
            mask = west if pair == 0 else east if pair == pairs else middle
            hidden = jnp.where(mask > 0, jnp.maximum(acc_ref[slot, 0, pair], 0.0), 0.0)
            hidden = hidden.astype(BF16).astype(F32)
            narrow_hidden[slot, pair] = hidden
            narrow_delta[slot, pair] = jnp.where(hidden > 0, acc_ref[slot, 1, pair], 0.0)

    spread(narrow_hidden, taps_hidden, pairs + 1, 8, side)
    spread(narrow_delta, taps_delta, pairs + 1, 8, side)

    first_grad = None
    second_grad = None
    copies = []
    contract_first = (((0,), (0,)), ((), ()))
    for slot in range(slots):
        out = jnp.dot(across(taps_hidden, slot, pairs, side), forward_ref[1], preferred_element_type=F32)
        back = lax.dot_general(
            across(taps_delta, slot, pairs, side), back_ref[0], contract_last, preferred_element_type=F32
        )
        for pair in range(pairs):
            lanes = slice(pair * LANES, (pair + 1) * LANES)
            rows = slice(pair * side, (pair + 1) * side)
            output_ref[slot, :, lanes] = out[rows].astype(BF16)
            grad_input_ref[slot, :, lanes] = back[rows].astype(BF16)
        for k, (source, target) in enumerate(((output_ref, output_hbm), (grad_input_ref, grad_input_hbm))):
            copies.append(pltpu.make_async_copy(source.at[slot], target.at[slot], sems.at[2 * slot + k]))
            copies[-1].start()
    for slot in range(slots):
        own_in, own_up = (
            wide[slot, 1 : pairs + 1, 16 : 16 + side, :].reshape(pairs * side, LANES).astype(BF16)
            for wide in (wide_in, wide_up)
        )
        term_one = lax.dot_general(
            own_in, across(taps_delta, slot, pairs, side), contract_first, preferred_element_type=F32
        )
        term_two = lax.dot_general(
            own_up, across(taps_hidden, slot, pairs, side), contract_first, preferred_element_type=F32
        )
        first_grad = term_one if first_grad is None else first_grad + term_one
        second_grad = term_two if second_grad is None else second_grad + term_two

    total = grads_ref.shape[0]
    lane = lax.broadcasted_iota(jnp.int32, (half, LANES), 1)
    for a in range(3):
        one = first_grad[:, (2 - a) * 256 : (3 - a) * 256]
        two = second_grad[:, a * 256 : (a + 1) * 256].T
        blocks = [one[:half, 0:LANES], one[:half, LANES:256], one[half:, 0:LANES], one[half:, LANES:256]]
        turned = [pltpu.roll(block, half, 1) for block in blocks]
        left = (blocks[0] + turned[2], turned[0] + blocks[3], blocks[1] + turned[3])
        for b in range(3):
            upper = two[b * half : (b + 1) * half]
            lower = two[(b + 1) * half : (b + 2) * half]
            right = pltpu.roll(upper, half, 1) + lower
            rows = slice((a * 3 + b) * half, (a * 3 + b + 1) * half)
            grads_ref[rows, :] = jnp.where(lane < half, left[2 - b], right).astype(BF16)
    if total > 576:
        grads_ref[576:total, :] = jnp.zeros((total - 576, LANES), BF16)
    for copy in copies:
        copy.wait()


def summed(blocks, axis):
    parts = lax.all_to_all(blocks, axis, 0, 0, tiled=True)
    return jnp.sum(lax.optimization_barrier(parts.astype(F32)), axis=0).astype(BF16)


def gathered(share, count, axis):
    copies = jnp.broadcast_to(share[None], (count,) + share.shape)
    return lax.all_to_all(copies, axis, 0, 0, tiled=True)


def local(slide_image, cotangent, weight_one, weight_two, tissue, neighbours):
    devices_tile = lax.axis_size("tile")
    devices = devices_tile * lax.axis_size("slide")
    _, slots, side, width = slide_image.shape
    pairs = width // LANES
    tall = side + 16
    image, upstream = slide_image[0], cotangent[0]
    links = neighbours[0]
    packed = pl.pallas_call(
        pack_kernel,
        out_shape=jax.ShapeDtypeStruct((devices_tile, BLOCK, LANES), BF16),
        in_specs=[ANY] * 3,
        out_specs=VMEM,
        scratch_shapes=[
            pltpu.SMEM(links.shape, jnp.int32),
            pltpu.VMEM(image.shape, BF16),
            pltpu.VMEM(image.shape, BF16),
            pltpu.VMEM((2, 32, LANES), F32),
            pltpu.SemaphoreType.DMA((2 * slots + 1,)),
        ],
        compiler_params=pltpu.CompilerParams(vmem_limit_bytes=PACK_LIMIT),
        name="pack",
    )(links, image, upstream)
    halo = lax.all_to_all(packed, "tile", 0, 0, tiled=True)

    chunk = -(-576 // (2 * devices))
    total = 2 * chunk * devices
    output, grad_input, grads = pl.pallas_call(
        mix_kernel,
        out_shape=(
            jax.ShapeDtypeStruct((slots, side, width), BF16),
            jax.ShapeDtypeStruct((slots, side, width), BF16),
            jax.ShapeDtypeStruct((total, LANES), BF16),
        ),
        in_specs=[ANY, ANY] + [VMEM] * 5,
        out_specs=(ANY, ANY, VMEM),
        scratch_shapes=[
            pltpu.SMEM(links.shape, jnp.int32),
            pltpu.SMEM(tissue.shape, jnp.int32),
            pltpu.VMEM((slots, pairs + 2, side + 32, LANES), F32),
            pltpu.VMEM((slots, pairs + 2, side + 32, LANES), F32),
            pltpu.VMEM((slots, pairs + 1, tall, LANES), F32),
            pltpu.VMEM((slots, pairs + 1, tall, LANES), F32),
            pltpu.VMEM((slots, 3, pairs + 2, tall, LANES), BF16),
            pltpu.VMEM((slots, 3, pairs + 2, tall, LANES), BF16),
            pltpu.VMEM((slots, 3, pairs + 1, side, LANES), BF16),
            pltpu.VMEM((slots, 3, pairs + 1, side, LANES), BF16),
            pltpu.VMEM((2, 768, LANES), BF16),
            pltpu.VMEM((2, LANES, 768), BF16),
            pltpu.VMEM((slots, 2, pairs + 1, tall, LANES), F32),
            pltpu.VMEM((slots, side, width), BF16),
            pltpu.VMEM((slots, side, width), BF16),
            pltpu.SemaphoreType.DMA((2 * slots + 2,)),
        ],
        compiler_params=pltpu.CompilerParams(vmem_limit_bytes=48 * 2**20),
        name="mix",
    )(links, tissue, image, upstream, halo, weight_one, weight_two)

    slides = devices // devices_tile
    share = summed(grads.reshape(slides, devices_tile * chunk, 2, LANES), "slide")
    share = summed(share.reshape(devices_tile, chunk, 2, LANES), "tile")
    share = gathered(share, devices_tile, "tile").reshape(devices_tile * chunk, 2, LANES)
    whole = gathered(share, slides, "slide").reshape(total, LANES)
    whole = lax.optimization_barrier(whole.astype(F32))
    grad_one = whole[:576, : LANES // 2]
    grad_two = whole[:576, LANES // 2 :]
    shape = weight_one.shape
    return output[None], grad_input[None], grad_one.reshape(shape), grad_two.reshape(shape)


def solution(mesh):
    placed = (
        P("slide", "tile", None, None),
        P("slide", "tile", None, None),
        P(),
        P(),
        P("slide", "tile"),
        P("slide", "tile", None),
    )
    return jax.shard_map(
        local,
        mesh=mesh,
        in_specs=placed,
        out_specs=(P("slide", "tile", None, None), P("slide", "tile", None, None), P(), P()),
        check_vma=False,
    )
```

```python
import functools

import jax
import jax.numpy as jnp
from jax import lax
from jax.experimental import pallas as pl
from jax.experimental.pallas import tpu as pltpu
from jax.sharding import PartitionSpec as P

F32 = jnp.float32
BF16 = jnp.bfloat16
LANES = 128
VMEM = pl.BlockSpec(memory_space=pltpu.VMEM)
ANY = pl.BlockSpec(memory_space=pl.ANY)
PACK_LIMIT = 60 * 2**20


BLOCK = 2 * 64


def strip_row(field, slot):
    return field * 64 + slot * 32


def band_weights(source, forward, back):
    half = LANES // 2
    zero = jnp.zeros((half, half), BF16)
    for a in range(3):
        taps = [source[a, b] for b in range(3)]
        left = jnp.concatenate(taps + [zero], axis=0)
        right = jnp.concatenate([zero] + taps, axis=0)
        forward[a * 256 : (a + 1) * 256, :] = jnp.concatenate([left, right], axis=1)
        turned = [source[2 - a, 2 - b] for b in range(3)]
        upper = jnp.concatenate(turned + [zero], axis=1)
        lower = jnp.concatenate([zero] + turned, axis=1)
        back[:, a * 256 : (a + 1) * 256] = jnp.concatenate([upper, lower], axis=0)


def pack_kernel(
    links_hbm, image_hbm, cotangent_hbm, out_ref,
    links_ref, image_ref, cotangent_ref, strip_ref, sems,
):
    slots, side, width = image_ref.shape
    pairs = width // LANES
    copies = [pltpu.make_async_copy(links_hbm, links_ref, sems.at[2 * slots])]
    copies[0].start()
    fields = ((image_hbm, image_ref), (cotangent_hbm, cotangent_ref))
    for field, (source, target) in enumerate(fields):
        for slot in range(slots):
            copy = pltpu.make_async_copy(source.at[slot], target.at[slot], sems.at[field * slots + slot])
            copy.start()
            copies.append(copy)
    copies[0].wait()
    for field, (_, ref) in enumerate(fields):
        for slot in range(slots):
            copies[1 + field * slots + slot].wait()
            top = ref[slot, 0:16, :].astype(F32)
            bottom = ref[slot, side - 16 : side, :].astype(F32)
            for pair in range(pairs):
                lanes = slice(pair * LANES, (pair + 1) * LANES)
                rows = slice(2 * pair, 2 * pair + 2)
                strip_ref[0, rows, :] = top[0:2, lanes]
                strip_ref[1, rows, :] = bottom[14:16, lanes]
            for direction in (0, 1, 4, 5, 6, 7):
                link = links_ref[slot, direction]

                @pl.when(link >= 0)
                def _(slot=slot, direction=direction, link=link, field=field):
                    which = 0 if direction in (0, 4, 5) else 1
                    first = strip_row(field, slot)
                    out_ref[link // slots, first : first + 32, :] = strip_ref[which].astype(BF16)


def columns_kernel(tissue_hbm, image_hbm, cotangent_hbm, east_ref, west_ref, tissue_ref, edge_ref, sems):
    slots, side, _ = edge_ref.shape[2:]
    width = image_hbm.shape[2]
    copies = [pltpu.make_async_copy(tissue_hbm, tissue_ref, sems.at[4])]
    for field, source in enumerate((image_hbm, cotangent_hbm)):
        for end, first in enumerate((width - LANES, 0)):
            copies.append(
                pltpu.make_async_copy(
                    source.at[:, :, first : first + LANES], edge_ref.at[field, end], sems.at[2 * field + end]
                )
            )
    for copy in copies:
        copy.start()
    for copy in copies:
        copy.wait()
    for field in range(2):
        last = edge_ref[field, 0, 0].astype(F32)
        for slot in range(1, slots):
            last = jnp.where(tissue_ref[0, slot] > 0, edge_ref[field, 0, slot].astype(F32), last)
        east_ref[field] = last.astype(BF16)
        west_ref[field] = edge_ref[field, 1, 0]


def mix_kernel(
    links_hbm, tissue_hbm, image_ref, cotangent_ref, halo_ref, from_west_ref, from_east_ref, one_ref, two_ref,
    output_hbm, grad_input_hbm, grads_ref,
    links_ref, tissue_ref, wide_in, wide_up, narrow_hidden, narrow_delta,
    taps_in, taps_up, taps_hidden, taps_delta, forward_ref, back_ref, acc_ref, output_ref, grad_input_ref, sems,
):
    slots, side, width = image_ref.shape
    pairs = width // LANES
    half = LANES // 2
    tall = side + 16
    me = lax.axis_index("tile")

    small = [
        pltpu.make_async_copy(tissue_hbm, tissue_ref, sems.at[2 * slots]),
        pltpu.make_async_copy(links_hbm, links_ref, sems.at[2 * slots + 1]),
    ]
    for copy in small:
        copy.start()
    band_weights(one_ref, forward_ref.at[0], back_ref.at[0])
    band_weights(two_ref, forward_ref.at[1], back_ref.at[1])
    for copy in small:
        copy.wait()

    for field, (ref, wide) in enumerate(((image_ref, wide_in), (cotangent_ref, wide_up))):
        wide[:, :, 0:16, :] = jnp.zeros((slots, pairs + 2, 16, LANES), F32)
        wide[:, :, 16 + side : 32 + side, :] = jnp.zeros((slots, pairs + 2, 16, LANES), F32)
        for slot in range(slots):
            present = tissue_ref[0, slot] > 0
            for pair in range(pairs):
                block = ref[slot, :, pair * LANES : (pair + 1) * LANES].astype(F32)
                wide[slot, pair + 1, 16 : 16 + side, :] = jnp.where(present, block, 0.0)
            for direction in range(8):
                link = links_ref[slot, direction]
                device, there = jnp.maximum(link, 0) // slots, jnp.maximum(link, 0) % slots
                if direction in (2, 3):
                    lanes = slice(width - LANES, width) if direction == 2 else slice(0, LANES)
                    far = (from_west_ref if direction == 2 else from_east_ref)[field].astype(F32)
                    got = jnp.where(device == me, ref[there, :, lanes].astype(F32), far)
                else:
                    first = pl.multiple_of(strip_row(field, 0) + there * 32, 32)
                    got = halo_ref[device, pl.ds(first, 32), :].astype(F32)
                got = jnp.where(link >= 0, got, 0.0)
                row = 14 if direction in (0, 4, 5) else 16 + side
                if direction in (2, 3):
                    wide[slot, 0 if direction == 2 else pairs + 1, 16 : 16 + side, :] = got
                elif direction < 2:
                    for pair in range(pairs):
                        wide[slot, pair + 1, row : row + 2, :] = got[2 * pair : 2 * pair + 2, :]
                elif direction in (4, 6):
                    wide[slot, 0, row : row + 2, :] = got[2 * pairs - 2 : 2 * pairs, :]
                else:
                    wide[slot, pairs + 1, row : row + 2, :] = got[0:2, :]

    def spread(field, taps, count, start, rows):
        for pair in range(count):
            for slot in range(slots):
                for a in range(3):
                    taps[slot, a, pair] = field[slot, pair, start + a - 1 : start + a - 1 + rows, :].astype(BF16)

    spread(wide_in, taps_in, pairs + 2, 8, tall)
    spread(wide_up, taps_up, pairs + 2, 8, tall)

    row = lax.broadcasted_iota(jnp.int32, (tall, LANES), 0)
    lane = lax.broadcasted_iota(jnp.int32, (tall, LANES), 1)

    def column_mask(north, here, south):
        value = jnp.where(row == 7, north, jnp.where(row == 8 + side, south, here))
        return jnp.where((row >= 7) & (row <= 8 + side), value, 0)

    def across(taps, slot, count, rows):
        parts = [
            taps[slot, a, right : count + right].reshape(count * rows, LANES)
            for a in range(3)
            for right in range(2)
        ]
        return jnp.concatenate(parts, axis=1)

    contract_last = (((1,), (1,)), ((), ()))
    for slot in range(slots):
        there = [(links_ref[slot, k] >= 0).astype(jnp.int32) for k in range(8)]
        own = tissue_ref[0, slot]
        middle = column_mask(there[0], own, there[1])
        west = jnp.where(lane < half, column_mask(there[4], there[2], there[6]), middle)
        east = jnp.where(lane < half, middle, column_mask(there[5], there[3], there[7]))

        first = jnp.dot(
            across(taps_in, slot, pairs + 1, tall), forward_ref[0], preferred_element_type=F32
        )
        acc_ref[slot, 0] = first.reshape(pairs + 1, tall, LANES)
        second = lax.dot_general(
            across(taps_up, slot, pairs + 1, tall), back_ref[1], contract_last,
            preferred_element_type=F32,
        )
        acc_ref[slot, 1] = second.reshape(pairs + 1, tall, LANES)

        for pair in range(pairs + 1):
            mask = west if pair == 0 else east if pair == pairs else middle
            hidden = jnp.where(mask > 0, jnp.maximum(acc_ref[slot, 0, pair], 0.0), 0.0)
            hidden = hidden.astype(BF16).astype(F32)
            narrow_hidden[slot, pair] = hidden
            narrow_delta[slot, pair] = jnp.where(hidden > 0, acc_ref[slot, 1, pair], 0.0)

    spread(narrow_hidden, taps_hidden, pairs + 1, 8, side)
    spread(narrow_delta, taps_delta, pairs + 1, 8, side)

    first_grad = None
    second_grad = None
    copies = []
    contract_first = (((0,), (0,)), ((), ()))
    for slot in range(slots):
        out = jnp.dot(across(taps_hidden, slot, pairs, side), forward_ref[1], preferred_element_type=F32)
        back = lax.dot_general(
            across(taps_delta, slot, pairs, side), back_ref[0], contract_last, preferred_element_type=F32
        )
        for pair in range(pairs):
            lanes = slice(pair * LANES, (pair + 1) * LANES)
            rows = slice(pair * side, (pair + 1) * side)
            output_ref[slot, :, lanes] = out[rows].astype(BF16)
            grad_input_ref[slot, :, lanes] = back[rows].astype(BF16)
        for k, (source, target) in enumerate(((output_ref, output_hbm), (grad_input_ref, grad_input_hbm))):
            copies.append(pltpu.make_async_copy(source.at[slot], target.at[slot], sems.at[2 * slot + k]))
            copies[-1].start()
    for slot in range(slots):
        own_in, own_up = (
            wide[slot, 1 : pairs + 1, 16 : 16 + side, :].reshape(pairs * side, LANES).astype(BF16)
            for wide in (wide_in, wide_up)
        )
        term_one = lax.dot_general(
            own_in, across(taps_delta, slot, pairs, side), contract_first, preferred_element_type=F32
        )
        term_two = lax.dot_general(
            own_up, across(taps_hidden, slot, pairs, side), contract_first, preferred_element_type=F32
        )
        first_grad = term_one if first_grad is None else first_grad + term_one
        second_grad = term_two if second_grad is None else second_grad + term_two

    total = grads_ref.shape[0]
    lane = lax.broadcasted_iota(jnp.int32, (half, LANES), 1)
    for a in range(3):
        one = first_grad[:, (2 - a) * 256 : (3 - a) * 256]
        two = second_grad[:, a * 256 : (a + 1) * 256].T
        blocks = [one[:half, 0:LANES], one[:half, LANES:256], one[half:, 0:LANES], one[half:, LANES:256]]
        turned = [pltpu.roll(block, half, 1) for block in blocks]
        left = (blocks[0] + turned[2], turned[0] + blocks[3], blocks[1] + turned[3])
        for b in range(3):
            upper = two[b * half : (b + 1) * half]
            lower = two[(b + 1) * half : (b + 2) * half]
            right = pltpu.roll(upper, half, 1) + lower
            rows = slice((a * 3 + b) * half, (a * 3 + b + 1) * half)
            grads_ref[rows, :] = jnp.where(lane < half, left[2 - b], right).astype(BF16)
    if total > 576:
        grads_ref[576:total, :] = jnp.zeros((total - 576, LANES), BF16)
    for copy in copies:
        copy.wait()


def local(slide_image, cotangent, weight_one, weight_two, tissue, neighbours):
    devices_tile = lax.axis_size("tile")
    devices = devices_tile * lax.axis_size("slide")
    _, slots, side, width = slide_image.shape
    pairs = width // LANES
    tall = side + 16
    image, upstream = slide_image[0], cotangent[0]
    links = neighbours[0]
    packed = pl.pallas_call(
        pack_kernel,
        out_shape=jax.ShapeDtypeStruct((devices_tile, BLOCK, LANES), BF16),
        in_specs=[ANY] * 3,
        out_specs=VMEM,
        scratch_shapes=[
            pltpu.SMEM(links.shape, jnp.int32),
            pltpu.VMEM(image.shape, BF16),
            pltpu.VMEM(image.shape, BF16),
            pltpu.VMEM((2, 32, LANES), F32),
            pltpu.SemaphoreType.DMA((2 * slots + 1,)),
        ],
        compiler_params=pltpu.CompilerParams(vmem_limit_bytes=PACK_LIMIT),
        name="pack",
    )(links, image, upstream)
    packed, tissue_after = lax.optimization_barrier((packed, tissue))
    halo = lax.all_to_all(packed, "tile", 0, 0, tiled=True)

    edge = jax.ShapeDtypeStruct((2, side, LANES), BF16)
    east, west = pl.pallas_call(
        columns_kernel,
        out_shape=(edge, edge),
        in_specs=[ANY] * 3,
        out_specs=(VMEM, VMEM),
        scratch_shapes=[
            pltpu.SMEM(tissue.shape, jnp.int32),
            pltpu.VMEM((2, 2, slots, side, LANES), BF16),
            pltpu.SemaphoreType.DMA((5,)),
        ],
        compiler_params=pltpu.CompilerParams(vmem_limit_bytes=PACK_LIMIT),
        cost_estimate=pl.CostEstimate(flops=4 * 10**9, bytes_accessed=10**7, transcendentals=0),
        name="columns",
    )(tissue_after, image, upstream)
    onward = [(k, k + 1) for k in range(devices_tile - 1)]
    from_west = lax.ppermute(east, "tile", onward)
    from_east = lax.ppermute(west, "tile", [(k + 1, k) for k, _ in onward])

    chunk = -(-576 // (2 * devices))
    total = 2 * chunk * devices
    output, grad_input, grads = pl.pallas_call(
        mix_kernel,
        out_shape=(
            jax.ShapeDtypeStruct((slots, side, width), BF16),
            jax.ShapeDtypeStruct((slots, side, width), BF16),
            jax.ShapeDtypeStruct((total, LANES), BF16),
        ),
        in_specs=[ANY, ANY] + [VMEM] * 7,
        out_specs=(ANY, ANY, VMEM),
        scratch_shapes=[
            pltpu.SMEM(links.shape, jnp.int32),
            pltpu.SMEM(tissue.shape, jnp.int32),
            pltpu.VMEM((slots, pairs + 2, side + 32, LANES), F32),
            pltpu.VMEM((slots, pairs + 2, side + 32, LANES), F32),
            pltpu.VMEM((slots, pairs + 1, tall, LANES), F32),
            pltpu.VMEM((slots, pairs + 1, tall, LANES), F32),
            pltpu.VMEM((slots, 3, pairs + 2, tall, LANES), BF16),
            pltpu.VMEM((slots, 3, pairs + 2, tall, LANES), BF16),
            pltpu.VMEM((slots, 3, pairs + 1, side, LANES), BF16),
            pltpu.VMEM((slots, 3, pairs + 1, side, LANES), BF16),
            pltpu.VMEM((2, 768, LANES), BF16),
            pltpu.VMEM((2, LANES, 768), BF16),
            pltpu.VMEM((slots, 2, pairs + 1, tall, LANES), F32),
            pltpu.VMEM((slots, side, width), BF16),
            pltpu.VMEM((slots, side, width), BF16),
            pltpu.SemaphoreType.DMA((2 * slots + 2,)),
        ],
        compiler_params=pltpu.CompilerParams(vmem_limit_bytes=48 * 2**20),
        name="mix",
    )(links, tissue, image, upstream, halo, from_west, from_east, weight_one, weight_two)

    parts = lax.all_to_all(grads.reshape(devices, chunk, 2, LANES), ("slide", "tile"), 0, 0, tiled=True)
    mine = jnp.sum(lax.optimization_barrier(parts.astype(F32)), axis=0).astype(BF16)
    sums = jnp.broadcast_to(mine[None], parts.shape)
    whole = lax.all_to_all(sums, ("slide", "tile"), 0, 0, tiled=True)
    whole = lax.optimization_barrier(whole.reshape(total, LANES).astype(F32))
    grad_one = whole[:576, : LANES // 2]
    grad_two = whole[:576, LANES // 2 :]
    shape = weight_one.shape
    return output[None], grad_input[None], grad_one.reshape(shape), grad_two.reshape(shape)


def solution(mesh):
    placed = (
        P("slide", "tile", None, None),
        P("slide", "tile", None, None),
        P(),
        P(),
        P("slide", "tile"),
        P("slide", "tile", None),
    )
    return jax.shard_map(
        local,
        mesh=mesh,
        in_specs=placed,
        out_specs=(P("slide", "tile", None, None), P("slide", "tile", None, None), P(), P()),
        check_vma=False,
    )
```

```python
import functools

import jax
import jax.numpy as jnp
from jax import lax
from jax.experimental import pallas as pl
from jax.experimental.pallas import tpu as pltpu
from jax.sharding import PartitionSpec as P

F32 = jnp.float32
BF16 = jnp.bfloat16
LANES = 128
VMEM = pl.BlockSpec(memory_space=pltpu.VMEM)
ANY = pl.BlockSpec(memory_space=pl.ANY)
PACK_LIMIT = 60 * 2**20


RING = 2 * 48


def strip_row(field, slot):
    return field * 48 + slot * 16


def column_row(field):
    return field * 48 + 32


def forward_weights(source, forward):
    zero = jnp.zeros((LANES // 2, LANES // 2), BF16)
    for a in range(3):
        taps = [source[a, b] for b in range(3)]
        left = jnp.concatenate(taps + [zero], axis=0)
        right = jnp.concatenate([zero] + taps, axis=0)
        forward[a * 256 : (a + 1) * 256, :] = jnp.concatenate([left, right], axis=1)


def back_weights(source, back):
    zero = jnp.zeros((LANES // 2, LANES // 2), BF16)
    for a in range(3):
        turned = [source[2 - a, 2 - b] for b in range(3)]
        upper = jnp.concatenate(turned + [zero], axis=1)
        lower = jnp.concatenate([zero] + turned, axis=1)
        back[:, a * 256 : (a + 1) * 256] = jnp.concatenate([upper, lower], axis=0)


def across(taps, slot, count):
    rows = taps.shape[3]
    parts = [
        taps[slot, a, right : count + right].reshape(count * rows, LANES)
        for a in range(3)
        for right in range(2)
    ]
    return jnp.concatenate(parts, axis=1)


CONTRACT_FIRST = (((0,), (0,)), ((), ()))
CONTRACT_LAST = (((1,), (1,)), ((), ()))


def pack_kernel(
    links_hbm, image_hbm, cotangent_hbm, out_ref,
    links_ref, image_ref, cotangent_ref, strip_ref, sems,
):
    slots, side, width = image_ref.shape
    pairs = width // LANES
    half = LANES // 2
    copies = [pltpu.make_async_copy(links_hbm, links_ref, sems.at[2 * slots])]
    copies[0].start()
    fields = ((image_hbm, image_ref), (cotangent_hbm, cotangent_ref))
    for field, (source, target) in enumerate(fields):
        for slot in range(slots):
            copy = pltpu.make_async_copy(source.at[slot], target.at[slot], sems.at[field * slots + slot])
            copy.start()
            copies.append(copy)
    me = lax.axis_index("tile")
    left = lax.broadcasted_iota(jnp.int32, (16, LANES), 1) < half
    copies[0].wait()
    for field, (_, ref) in enumerate(fields):
        for slot in range(slots):
            copies[1 + field * slots + slot].wait()
            top = ref[slot, 0:16, :].astype(F32)
            bottom = ref[slot, side - 16 : side, :].astype(F32)
            for pair in range(pairs):
                lanes = slice(pair * LANES, (pair + 1) * LANES)
                strip_ref[0, pair : pair + 1, :] = top[0:1, lanes]
                strip_ref[1, pair : pair + 1, :] = top[1:2, lanes]
                strip_ref[2, pair : pair + 1, :] = bottom[15:16, lanes]
                strip_ref[3, pair : pair + 1, :] = bottom[14:15, lanes]
            for direction in range(8):
                link = links_ref[slot, direction]

                @pl.when(link >= 0)
                def _(slot=slot, direction=direction, link=link, field=field, ref=ref):
                    device = link // slots
                    if direction in (2, 3):
                        first = jnp.where(device == me, strip_row(field, slot), column_row(field))
                        inner = pl.ds(pl.multiple_of(first, 16), 16)
                        outer = pl.ds(pl.multiple_of(first + RING, 16), 16)
                        lanes = slice(0, LANES) if direction == 2 else slice(width - LANES, width)
                        block = ref[slot, :, lanes].astype(F32)
                        other = pltpu.roll(block, half, 1)
                        low = jnp.where(left, block[0:16], other[16:32]).astype(BF16)
                        high = jnp.where(left, other[0:16], block[16:32]).astype(BF16)
                        out_ref[device, inner, :] = low if direction == 2 else high
                        out_ref[device, outer, :] = high if direction == 2 else low
                    else:
                        which = 0 if direction in (0, 4, 5) else 2
                        first = strip_row(field, slot)
                        out_ref[device, first : first + 16, :] = strip_ref[which].astype(BF16)
                        first += RING
                        out_ref[device, first : first + 16, :] = strip_ref[which + 1].astype(BF16)


def place_halo(links_ref, halo_ref, rings, wide, slot, field, slots, side, pairs, me):
    half = LANES // 2
    left = lax.broadcasted_iota(jnp.int32, (16, LANES), 1) < half
    none = jnp.zeros((16, LANES), F32)
    for direction in range(8):
        link = links_ref[slot, direction]
        device, there = jnp.maximum(link, 0) // slots, jnp.maximum(link, 0) % slots
        first = strip_row(field, 0) + there * 16
        if direction in (2, 3):
            first = jnp.where(device == me, first, column_row(field))
        got = []
        for ring in range(rings):
            at = pl.ds(pl.multiple_of(first + ring * RING, 16), 16)
            got.append(jnp.where(link >= 0, halo_ref[device, at, :].astype(F32), 0.0))
        if direction in (2, 3):
            inner, outer = got[0], got[1] if len(got) > 1 else none
            low, high = (outer, inner) if direction == 2 else (inner, outer)
            column = 0 if direction == 2 else pairs + 1
            wide[slot, column, 16:32, :] = jnp.where(left, low, pltpu.roll(high, half, 1))
            wide[slot, column, 32:48, :] = jnp.where(left, pltpu.roll(low, half, 1), high)
        else:
            north = direction in (0, 4, 5)
            for ring, strip in enumerate(got):
                row = 15 - ring if north else 16 + side + ring
                if direction < 2:
                    for pair in range(pairs):
                        wide[slot, pair + 1, row : row + 1, :] = strip[pair : pair + 1, :]
                elif direction in (4, 6):
                    wide[slot, 0, row : row + 1, :] = strip[pairs - 1 : pairs, :]
                else:
                    wide[slot, pairs + 1, row : row + 1, :] = strip[0:1, :]


def place_own(tissue_ref, ref, wide, slot, side, pairs):
    present = tissue_ref[0, slot] > 0
    for pair in range(pairs):
        block = ref[slot, :, pair * LANES : (pair + 1) * LANES].astype(F32)
        wide[slot, pair + 1, 16 : 16 + side, :] = jnp.where(present, block, 0.0)


def shift_rows(field, taps, count, start, rows):
    for pair in range(count):
        for slot in range(field.shape[0]):
            for a in range(3):
                taps[slot, a, pair] = field[slot, pair, start + a - 1 : start + a - 1 + rows, :].astype(BF16)


def grads_kernel(
    links_hbm, tissue_hbm, image_ref, cotangent_ref, halo_ref, one_ref, two_ref,
    grads_ref,
    links_ref, tissue_ref, wide_in, wide_up, own_hidden, own_delta,
    taps_in, taps_up, forward_ref, back_ref, acc_ref, sems,
):
    slots, side, width = image_ref.shape
    pairs = width // LANES
    half = LANES // 2
    me = lax.axis_index("tile")

    small = [
        pltpu.make_async_copy(tissue_hbm, tissue_ref, sems.at[0]),
        pltpu.make_async_copy(links_hbm, links_ref, sems.at[1]),
    ]
    for copy in small:
        copy.start()
    forward_weights(one_ref, forward_ref)
    back_weights(two_ref, back_ref)
    for copy in small:
        copy.wait()
    for field, (ref, wide) in enumerate(((image_ref, wide_in), (cotangent_ref, wide_up))):
        for slot in range(slots):
            place_own(tissue_ref, ref, wide, slot, side, pairs)
            place_halo(links_ref, halo_ref, 1, wide, slot, field, slots, side, pairs, me)
    shift_rows(wide_in, taps_in, pairs + 2, 16, side)
    shift_rows(wide_up, taps_up, pairs + 2, 16, side)

    left = lax.broadcasted_iota(jnp.int32, (side, LANES), 1) < half
    first_grad = None
    second_grad = None
    for slot in range(slots):
        before = jnp.dot(across(taps_in, slot, pairs + 1), forward_ref[...], preferred_element_type=F32)
        acc_ref[slot, 0] = before.reshape(pairs + 1, side, LANES)
        after = lax.dot_general(
            across(taps_up, slot, pairs + 1), back_ref[...], CONTRACT_LAST, preferred_element_type=F32
        )
        acc_ref[slot, 1] = after.reshape(pairs + 1, side, LANES)
        for pair in range(pairs + 1):
            hidden = jnp.maximum(acc_ref[slot, 0, pair], 0.0)
            if pair == 0:
                hidden = jnp.where(left, 0.0, hidden)
            if pair == pairs:
                hidden = jnp.where(left, hidden, 0.0)
            hidden = hidden.astype(BF16)
            own_hidden[slot, pair] = hidden
            delta = jnp.where(hidden.astype(F32) > 0, acc_ref[slot, 1, pair], 0.0)
            own_delta[slot, pair] = delta.astype(BF16)
        term_one = lax.dot_general(
            own_delta[slot].reshape((pairs + 1) * side, LANES), across(taps_in, slot, pairs + 1),
            CONTRACT_FIRST, preferred_element_type=F32,
        )
        term_two = lax.dot_general(
            own_hidden[slot].reshape((pairs + 1) * side, LANES), across(taps_up, slot, pairs + 1),
            CONTRACT_FIRST, preferred_element_type=F32,
        )
        first_grad = term_one if first_grad is None else first_grad + term_one
        second_grad = term_two if second_grad is None else second_grad + term_two

    total = grads_ref.shape[0]
    left = lax.broadcasted_iota(jnp.int32, (half, LANES), 1) < half
    for a in range(3):
        one = first_grad[:, a * 256 : (a + 1) * 256].T
        two = second_grad[:, (2 - a) * 256 : (3 - a) * 256]
        blocks = [two[:half, 0:LANES], two[:half, LANES:256], two[half:, 0:LANES], two[half:, LANES:256]]
        turned = [pltpu.roll(block, half, 1) for block in blocks]
        right = (turned[0] + blocks[2], blocks[0] + turned[3], turned[1] + blocks[3])
        for b in range(3):
            upper = one[b * half : (b + 1) * half]
            lower = one[(b + 1) * half : (b + 2) * half]
            rows = slice((a * 3 + b) * half, (a * 3 + b + 1) * half)
            both = jnp.where(left, upper + pltpu.roll(lower, half, 1), right[2 - b])
            grads_ref[rows, :] = both.astype(BF16)
    if total > 576:
        grads_ref[576:total, :] = jnp.zeros((total - 576, LANES), BF16)


def fields_kernel(
    links_hbm, tissue_hbm, image_ref, cotangent_ref, halo_ref, one_ref, two_ref,
    output_hbm, grad_input_hbm,
    links_ref, tissue_ref, wide_in, wide_up, narrow_hidden, narrow_delta,
    taps_in, taps_up, taps_hidden, taps_delta, forward_one, forward_two, back_one, back_two,
    acc_ref, output_ref, grad_input_ref, sems,
):
    slots, side, width = image_ref.shape
    pairs = width // LANES
    half = LANES // 2
    tall = side + 16
    me = lax.axis_index("tile")

    small = [
        pltpu.make_async_copy(tissue_hbm, tissue_ref, sems.at[2 * slots]),
        pltpu.make_async_copy(links_hbm, links_ref, sems.at[2 * slots + 1]),
    ]
    for copy in small:
        copy.start()
    forward_weights(one_ref, forward_one)
    forward_weights(two_ref, forward_two)
    back_weights(one_ref, back_one)
    back_weights(two_ref, back_two)
    for copy in small:
        copy.wait()
    for field, (ref, wide) in enumerate(((image_ref, wide_in), (cotangent_ref, wide_up))):
        wide[:, :, 0:16, :] = jnp.zeros((slots, pairs + 2, 16, LANES), F32)
        wide[:, :, 16 + side : 32 + side, :] = jnp.zeros((slots, pairs + 2, 16, LANES), F32)
        for slot in range(slots):
            place_own(tissue_ref, ref, wide, slot, side, pairs)
            place_halo(links_ref, halo_ref, 2, wide, slot, field, slots, side, pairs, me)
    shift_rows(wide_in, taps_in, pairs + 2, 8, tall)
    shift_rows(wide_up, taps_up, pairs + 2, 8, tall)

    row = lax.broadcasted_iota(jnp.int32, (tall, LANES), 0)
    lane = lax.broadcasted_iota(jnp.int32, (tall, LANES), 1)

    def column_mask(north, here, south):
        value = jnp.where(row == 7, north, jnp.where(row == 8 + side, south, here))
        return jnp.where((row >= 7) & (row <= 8 + side), value, 0)

    for slot in range(slots):
        there = [(links_ref[slot, k] >= 0).astype(jnp.int32) for k in range(8)]
        own = tissue_ref[0, slot]
        middle = column_mask(there[0], own, there[1])
        west = jnp.where(lane < half, column_mask(there[4], there[2], there[6]), middle)
        east = jnp.where(lane < half, middle, column_mask(there[5], there[3], there[7]))
        before = jnp.dot(across(taps_in, slot, pairs + 1), forward_one[...], preferred_element_type=F32)
        acc_ref[slot, 0] = before.reshape(pairs + 1, tall, LANES)
        after = lax.dot_general(
            across(taps_up, slot, pairs + 1), back_two[...], CONTRACT_LAST, preferred_element_type=F32
        )
        acc_ref[slot, 1] = after.reshape(pairs + 1, tall, LANES)
        for pair in range(pairs + 1):
            mask = west if pair == 0 else east if pair == pairs else middle
            hidden = jnp.where(mask > 0, jnp.maximum(acc_ref[slot, 0, pair], 0.0), 0.0)
            hidden = hidden.astype(BF16).astype(F32)
            narrow_hidden[slot, pair] = hidden
            narrow_delta[slot, pair] = jnp.where(hidden > 0, acc_ref[slot, 1, pair], 0.0)
    shift_rows(narrow_hidden, taps_hidden, pairs + 1, 8, side)
    shift_rows(narrow_delta, taps_delta, pairs + 1, 8, side)

    copies = []
    for slot in range(slots):
        out = jnp.dot(across(taps_hidden, slot, pairs), forward_two[...], preferred_element_type=F32)
        back = lax.dot_general(
            across(taps_delta, slot, pairs), back_one[...], CONTRACT_LAST, preferred_element_type=F32
        )
        for pair in range(pairs):
            lanes = slice(pair * LANES, (pair + 1) * LANES)
            rows = slice(pair * side, (pair + 1) * side)
            output_ref[slot, :, lanes] = out[rows].astype(BF16)
            grad_input_ref[slot, :, lanes] = back[rows].astype(BF16)
        for k, (source, target) in enumerate(((output_ref, output_hbm), (grad_input_ref, grad_input_hbm))):
            copies.append(pltpu.make_async_copy(source.at[slot], target.at[slot], sems.at[2 * slot + k]))
            copies[-1].start()
    for copy in copies:
        copy.wait()


def local(slide_image, cotangent, weight_one, weight_two, tissue, neighbours):
    devices_tile = lax.axis_size("tile")
    devices = devices_tile * lax.axis_size("slide")
    _, slots, side, width = slide_image.shape
    pairs = width // LANES
    tall = side + 16
    image, upstream = slide_image[0], cotangent[0]
    links = neighbours[0]
    packed = pl.pallas_call(
        pack_kernel,
        out_shape=jax.ShapeDtypeStruct((devices_tile, 2 * RING, LANES), BF16),
        in_specs=[ANY] * 3,
        out_specs=VMEM,
        scratch_shapes=[
            pltpu.SMEM(links.shape, jnp.int32),
            pltpu.VMEM(image.shape, BF16),
            pltpu.VMEM(image.shape, BF16),
            pltpu.VMEM((4, 16, LANES), F32),
            pltpu.SemaphoreType.DMA((2 * slots + 1,)),
        ],
        compiler_params=pltpu.CompilerParams(vmem_limit_bytes=PACK_LIMIT),
        name="pack",
    )(links, image, upstream)
    halo = lax.all_to_all(packed, "tile", 0, 0, tiled=True)

    chunk = -(-576 // (2 * devices))
    total = 2 * chunk * devices
    wide = pltpu.VMEM((slots, pairs + 2, side + 32, LANES), F32)
    weights = [pltpu.VMEM((768, LANES), BF16), pltpu.VMEM((LANES, 768), BF16)]
    cost = pl.CostEstimate(flops=4 * 10**9, bytes_accessed=10**7, transcendentals=0)
    grads = pl.pallas_call(
        grads_kernel,
        out_shape=jax.ShapeDtypeStruct((total, LANES), BF16),
        in_specs=[ANY, ANY] + [VMEM] * 5,
        out_specs=VMEM,
        scratch_shapes=[
            pltpu.SMEM(links.shape, jnp.int32),
            pltpu.SMEM(tissue.shape, jnp.int32),
            wide,
            wide,
            pltpu.VMEM((slots, pairs + 1, side, LANES), BF16),
            pltpu.VMEM((slots, pairs + 1, side, LANES), BF16),
            pltpu.VMEM((slots, 3, pairs + 2, side, LANES), BF16),
            pltpu.VMEM((slots, 3, pairs + 2, side, LANES), BF16),
            *weights,
            pltpu.VMEM((slots, 2, pairs + 1, side, LANES), F32),
            pltpu.SemaphoreType.DMA((2,)),
        ],
        compiler_params=pltpu.CompilerParams(vmem_limit_bytes=32 * 2**20),
        cost_estimate=cost,
        name="grads",
    )(links, tissue, image, upstream, halo, weight_one, weight_two)
    output, grad_input = pl.pallas_call(
        fields_kernel,
        out_shape=(jax.ShapeDtypeStruct((slots, side, width), BF16),) * 2,
        in_specs=[ANY, ANY] + [VMEM] * 5,
        out_specs=(ANY, ANY),
        scratch_shapes=[
            pltpu.SMEM(links.shape, jnp.int32),
            pltpu.SMEM(tissue.shape, jnp.int32),
            wide,
            wide,
            pltpu.VMEM((slots, pairs + 1, tall, LANES), F32),
            pltpu.VMEM((slots, pairs + 1, tall, LANES), F32),
            pltpu.VMEM((slots, 3, pairs + 2, tall, LANES), BF16),
            pltpu.VMEM((slots, 3, pairs + 2, tall, LANES), BF16),
            pltpu.VMEM((slots, 3, pairs + 1, side, LANES), BF16),
            pltpu.VMEM((slots, 3, pairs + 1, side, LANES), BF16),
            weights[0],
            weights[0],
            weights[1],
            weights[1],
            pltpu.VMEM((slots, 2, pairs + 1, tall, LANES), F32),
            pltpu.VMEM((slots, side, width), BF16),
            pltpu.VMEM((slots, side, width), BF16),
            pltpu.SemaphoreType.DMA((2 * slots + 2,)),
        ],
        compiler_params=pltpu.CompilerParams(vmem_limit_bytes=40 * 2**20),
        cost_estimate=cost,
        name="fields",
    )(links, tissue, image, upstream, halo, weight_one, weight_two)

    parts = lax.all_to_all(grads.reshape(devices, chunk, 2, LANES), ("slide", "tile"), 0, 0, tiled=True)
    mine = jnp.sum(lax.optimization_barrier(parts.astype(F32)), axis=0).astype(BF16)
    mine, output, grad_input = lax.optimization_barrier((mine, output, grad_input))
    sums = jnp.broadcast_to(mine[None], parts.shape)
    whole = lax.all_to_all(sums, ("slide", "tile"), 0, 0, tiled=True)
    whole = lax.optimization_barrier(whole.reshape(total, LANES).astype(F32))
    grad_one = whole[:576, : LANES // 2]
    grad_two = whole[:576, LANES // 2 :]
    shape = weight_one.shape
    return output[None], grad_input[None], grad_one.reshape(shape), grad_two.reshape(shape)


def solution(mesh):
    placed = (
        P("slide", "tile", None, None),
        P("slide", "tile", None, None),
        P(),
        P(),
        P("slide", "tile"),
        P("slide", "tile", None),
    )
    return jax.shard_map(
        local,
        mesh=mesh,
        in_specs=placed,
        out_specs=(P("slide", "tile", None, None), P("slide", "tile", None, None), P(), P()),
        check_vma=False,
    )
```

```python
import functools

import jax
import jax.numpy as jnp
from jax import lax
from jax.experimental import pallas as pl
from jax.experimental.pallas import tpu as pltpu
from jax.sharding import PartitionSpec as P

F32 = jnp.float32
BF16 = jnp.bfloat16
LANES = 128
VMEM = pl.BlockSpec(memory_space=pltpu.VMEM)
ANY = pl.BlockSpec(memory_space=pl.ANY)
PACK_LIMIT = 60 * 2**20


RING = 2 * 48
BLOCK = RING + 2 * 32


def strip_row(field, slot):
    return field * 48 + slot * 16


def outer_row(field, slot):
    return RING + field * 32 + slot * 16


def column_row(field):
    return field * 48 + 32


def forward_weights(source, forward):
    zero = jnp.zeros((LANES // 2, LANES // 2), BF16)
    for a in range(3):
        taps = [source[a, b] for b in range(3)]
        left = jnp.concatenate(taps + [zero], axis=0)
        right = jnp.concatenate([zero] + taps, axis=0)
        forward[a * 256 : (a + 1) * 256, :] = jnp.concatenate([left, right], axis=1)


def back_weights(source, back):
    zero = jnp.zeros((LANES // 2, LANES // 2), BF16)
    for a in range(3):
        turned = [source[2 - a, 2 - b] for b in range(3)]
        upper = jnp.concatenate(turned + [zero], axis=1)
        lower = jnp.concatenate([zero] + turned, axis=1)
        back[:, a * 256 : (a + 1) * 256] = jnp.concatenate([upper, lower], axis=0)


def across(taps, slot, count):
    rows = taps.shape[3]
    parts = [
        taps[slot, a, right : count + right].reshape(count * rows, LANES)
        for a in range(3)
        for right in range(2)
    ]
    return jnp.concatenate(parts, axis=1)


CONTRACT_FIRST = (((0,), (0,)), ((), ()))
CONTRACT_LAST = (((1,), (1,)), ((), ()))


def pack_kernel(
    links_hbm, image_hbm, cotangent_hbm, out_ref,
    links_ref, image_ref, cotangent_ref, strip_ref, sems,
):
    slots, side, width = image_ref.shape
    pairs = width // LANES
    half = LANES // 2
    copies = [pltpu.make_async_copy(links_hbm, links_ref, sems.at[2 * slots])]
    copies[0].start()
    fields = ((image_hbm, image_ref), (cotangent_hbm, cotangent_ref))
    for field, (source, target) in enumerate(fields):
        for slot in range(slots):
            copy = pltpu.make_async_copy(source.at[slot], target.at[slot], sems.at[field * slots + slot])
            copy.start()
            copies.append(copy)
    left = lax.broadcasted_iota(jnp.int32, (16, LANES), 1) < half
    copies[0].wait()
    for field, (_, ref) in enumerate(fields):
        for slot in range(slots):
            copies[1 + field * slots + slot].wait()
            top = ref[slot, 0:16, :].astype(F32)
            bottom = ref[slot, side - 16 : side, :].astype(F32)
            for pair in range(pairs):
                lanes = slice(pair * LANES, (pair + 1) * LANES)
                strip_ref[0, pair : pair + 1, :] = top[0:1, lanes]
                strip_ref[1, pair : pair + 1, :] = top[1:2, lanes]
                strip_ref[2, pair : pair + 1, :] = bottom[15:16, lanes]
                strip_ref[3, pair : pair + 1, :] = bottom[14:15, lanes]
            for direction in range(8):
                link = links_ref[slot, direction]

                @pl.when(link >= 0)
                def _(slot=slot, direction=direction, link=link, field=field, ref=ref):
                    device = link // slots
                    if direction in (2, 3):
                        first = column_row(field)
                        lanes = slice(0, LANES) if direction == 2 else slice(width - LANES, width)
                        block = ref[slot, :, lanes].astype(F32)
                        other = pltpu.roll(block, half, 1)
                        if direction == 2:
                            inner = jnp.where(left, block[0:16], other[16:32])
                        else:
                            inner = jnp.where(left, other[0:16], block[16:32])
                        out_ref[device, first : first + 16, :] = inner.astype(BF16)
                    else:
                        which = 0 if direction in (0, 4, 5) else 2
                        first = strip_row(field, slot)
                        out_ref[device, first : first + 16, :] = strip_ref[which].astype(BF16)
                        first = outer_row(field, slot)
                        out_ref[device, first : first + 16, :] = strip_ref[which + 1].astype(BF16)


def columns_kernel(tissue_hbm, image_hbm, cotangent_hbm, east_ref, west_ref, tissue_ref, edge_ref, sems):
    slots, side, _ = edge_ref.shape[2:]
    width = image_hbm.shape[2]
    copies = [pltpu.make_async_copy(tissue_hbm, tissue_ref, sems.at[4])]
    for field, source in enumerate((image_hbm, cotangent_hbm)):
        for end, first in enumerate((width - LANES, 0)):
            copies.append(
                pltpu.make_async_copy(
                    source.at[:, :, first : first + LANES], edge_ref.at[field, end], sems.at[2 * field + end]
                )
            )
    for copy in copies:
        copy.start()
    for copy in copies:
        copy.wait()
    for field in range(2):
        last = edge_ref[field, 0, 0].astype(F32)
        for slot in range(1, slots):
            last = jnp.where(tissue_ref[0, slot] > 0, edge_ref[field, 0, slot].astype(F32), last)
        east_ref[field] = last.astype(BF16)
        west_ref[field] = edge_ref[field, 1, 0]


def place_halo(links_ref, halo_ref, far_refs, ref, wide, slot, field, slots, side, pairs, me):
    half = LANES // 2
    width = pairs * LANES
    left = lax.broadcasted_iota(jnp.int32, (16, LANES), 1) < half
    for direction in range(8):
        link = links_ref[slot, direction]
        device, there = jnp.maximum(link, 0) // slots, jnp.maximum(link, 0) % slots
        if direction in (2, 3):
            if far_refs:
                far = far_refs[direction - 2][field].astype(F32)
            else:
                first = column_row(field)
                inner = halo_ref[device, first : first + 16, :].astype(F32)
                other = pltpu.roll(inner, half, 1)
                if direction == 2:
                    parts = [jnp.where(left, 0.0, other), jnp.where(left, 0.0, inner)]
                else:
                    parts = [jnp.where(left, inner, 0.0), jnp.where(left, other, 0.0)]
                far = jnp.concatenate(parts, axis=0)
            lanes = slice(width - LANES, width) if direction == 2 else slice(0, LANES)
            got = jnp.where(device == me, ref[there, :, lanes].astype(F32), far)
            column = 0 if direction == 2 else pairs + 1
            wide[slot, column, 16 : 16 + side, :] = jnp.where(link >= 0, got, 0.0)
        else:
            north = direction in (0, 4, 5)
            for ring, first in enumerate((strip_row(field, 0), outer_row(field, 0))[: 2 if far_refs else 1]):
                at = pl.ds(pl.multiple_of(first + there * 16, 16), 16)
                strip = jnp.where(link >= 0, halo_ref[device, at, :].astype(F32), 0.0)
                row = 15 - ring if north else 16 + side + ring
                if direction < 2:
                    for pair in range(pairs):
                        wide[slot, pair + 1, row : row + 1, :] = strip[pair : pair + 1, :]
                elif direction in (4, 6):
                    wide[slot, 0, row : row + 1, :] = strip[pairs - 1 : pairs, :]
                else:
                    wide[slot, pairs + 1, row : row + 1, :] = strip[0:1, :]


def place_own(tissue_ref, ref, wide, slot, side, pairs):
    present = tissue_ref[0, slot] > 0
    for pair in range(pairs):
        block = ref[slot, :, pair * LANES : (pair + 1) * LANES].astype(F32)
        wide[slot, pair + 1, 16 : 16 + side, :] = jnp.where(present, block, 0.0)


def shift_rows(field, taps, count, start, rows):
    for pair in range(count):
        for slot in range(field.shape[0]):
            for a in range(3):
                taps[slot, a, pair] = field[slot, pair, start + a - 1 : start + a - 1 + rows, :].astype(BF16)


def grads_kernel(
    links_hbm, tissue_hbm, image_ref, cotangent_ref, halo_ref, one_ref, two_ref,
    grads_ref,
    links_ref, tissue_ref, wide_in, wide_up, own_hidden, own_delta,
    taps_in, taps_up, forward_ref, back_ref, acc_ref, sems,
):
    slots, side, width = image_ref.shape
    pairs = width // LANES
    half = LANES // 2
    me = lax.axis_index("tile")

    small = [
        pltpu.make_async_copy(tissue_hbm, tissue_ref, sems.at[0]),
        pltpu.make_async_copy(links_hbm, links_ref, sems.at[1]),
    ]
    for copy in small:
        copy.start()
    forward_weights(one_ref, forward_ref)
    back_weights(two_ref, back_ref)
    for copy in small:
        copy.wait()
    for field, (ref, wide) in enumerate(((image_ref, wide_in), (cotangent_ref, wide_up))):
        for slot in range(slots):
            place_own(tissue_ref, ref, wide, slot, side, pairs)
            place_halo(links_ref, halo_ref, (), ref, wide, slot, field, slots, side, pairs, me)
    shift_rows(wide_in, taps_in, pairs + 2, 16, side)
    shift_rows(wide_up, taps_up, pairs + 2, 16, side)

    left = lax.broadcasted_iota(jnp.int32, (side, LANES), 1) < half
    first_grad = None
    second_grad = None
    for slot in range(slots):
        before = jnp.dot(across(taps_in, slot, pairs + 1), forward_ref[...], preferred_element_type=F32)
        acc_ref[slot, 0] = before.reshape(pairs + 1, side, LANES)
        after = lax.dot_general(
            across(taps_up, slot, pairs + 1), back_ref[...], CONTRACT_LAST, preferred_element_type=F32
        )
        acc_ref[slot, 1] = after.reshape(pairs + 1, side, LANES)
        for pair in range(pairs + 1):
            hidden = jnp.maximum(acc_ref[slot, 0, pair], 0.0)
            if pair == 0:
                hidden = jnp.where(left, 0.0, hidden)
            if pair == pairs:
                hidden = jnp.where(left, hidden, 0.0)
            hidden = hidden.astype(BF16)
            own_hidden[slot, pair] = hidden
            delta = jnp.where(hidden.astype(F32) > 0, acc_ref[slot, 1, pair], 0.0)
            own_delta[slot, pair] = delta.astype(BF16)
        term_one = lax.dot_general(
            own_delta[slot].reshape((pairs + 1) * side, LANES), across(taps_in, slot, pairs + 1),
            CONTRACT_FIRST, preferred_element_type=F32,
        )
        term_two = lax.dot_general(
            own_hidden[slot].reshape((pairs + 1) * side, LANES), across(taps_up, slot, pairs + 1),
            CONTRACT_FIRST, preferred_element_type=F32,
        )
        first_grad = term_one if first_grad is None else first_grad + term_one
        second_grad = term_two if second_grad is None else second_grad + term_two

    total = grads_ref.shape[0]
    left = lax.broadcasted_iota(jnp.int32, (half, LANES), 1) < half
    for a in range(3):
        one = first_grad[:, a * 256 : (a + 1) * 256].T
        two = second_grad[:, (2 - a) * 256 : (3 - a) * 256]
        blocks = [two[:half, 0:LANES], two[:half, LANES:256], two[half:, 0:LANES], two[half:, LANES:256]]
        turned = [pltpu.roll(block, half, 1) for block in blocks]
        right = (turned[0] + blocks[2], blocks[0] + turned[3], turned[1] + blocks[3])
        for b in range(3):
            upper = one[b * half : (b + 1) * half]
            lower = one[(b + 1) * half : (b + 2) * half]
            rows = slice((a * 3 + b) * half, (a * 3 + b + 1) * half)
            both = jnp.where(left, upper + pltpu.roll(lower, half, 1), right[2 - b])
            grads_ref[rows, :] = both.astype(BF16)
    if total > 576:
        grads_ref[576:total, :] = jnp.zeros((total - 576, LANES), BF16)


def fields_kernel(
    links_hbm, tissue_hbm, image_ref, cotangent_ref, halo_ref, from_west_ref, from_east_ref, one_ref, two_ref,
    output_hbm, grad_input_hbm,
    links_ref, tissue_ref, wide_in, wide_up, narrow_hidden, narrow_delta,
    taps_in, taps_up, taps_hidden, taps_delta, forward_one, forward_two, back_one, back_two,
    acc_ref, output_ref, grad_input_ref, sems,
):
    slots, side, width = image_ref.shape
    pairs = width // LANES
    half = LANES // 2
    tall = side + 16
    me = lax.axis_index("tile")

    small = [
        pltpu.make_async_copy(tissue_hbm, tissue_ref, sems.at[2 * slots]),
        pltpu.make_async_copy(links_hbm, links_ref, sems.at[2 * slots + 1]),
    ]
    for copy in small:
        copy.start()
    forward_weights(one_ref, forward_one)
    forward_weights(two_ref, forward_two)
    back_weights(one_ref, back_one)
    back_weights(two_ref, back_two)
    for copy in small:
        copy.wait()
    for field, (ref, wide) in enumerate(((image_ref, wide_in), (cotangent_ref, wide_up))):
        wide[:, :, 0:16, :] = jnp.zeros((slots, pairs + 2, 16, LANES), F32)
        wide[:, :, 16 + side : 32 + side, :] = jnp.zeros((slots, pairs + 2, 16, LANES), F32)
        for slot in range(slots):
            place_own(tissue_ref, ref, wide, slot, side, pairs)
            place_halo(links_ref, halo_ref, (from_west_ref, from_east_ref), ref, wide, slot, field, slots, side, pairs, me)
    shift_rows(wide_in, taps_in, pairs + 2, 8, tall)
    shift_rows(wide_up, taps_up, pairs + 2, 8, tall)

    row = lax.broadcasted_iota(jnp.int32, (tall, LANES), 0)
    lane = lax.broadcasted_iota(jnp.int32, (tall, LANES), 1)

    def column_mask(north, here, south):
        value = jnp.where(row == 7, north, jnp.where(row == 8 + side, south, here))
        return jnp.where((row >= 7) & (row <= 8 + side), value, 0)

    for slot in range(slots):
        there = [(links_ref[slot, k] >= 0).astype(jnp.int32) for k in range(8)]
        own = tissue_ref[0, slot]
        middle = column_mask(there[0], own, there[1])
        west = jnp.where(lane < half, column_mask(there[4], there[2], there[6]), middle)
        east = jnp.where(lane < half, middle, column_mask(there[5], there[3], there[7]))
        before = jnp.dot(across(taps_in, slot, pairs + 1), forward_one[...], preferred_element_type=F32)
        acc_ref[slot, 0] = before.reshape(pairs + 1, tall, LANES)
        after = lax.dot_general(
            across(taps_up, slot, pairs + 1), back_two[...], CONTRACT_LAST, preferred_element_type=F32
        )
        acc_ref[slot, 1] = after.reshape(pairs + 1, tall, LANES)
        for pair in range(pairs + 1):
            mask = west if pair == 0 else east if pair == pairs else middle
            hidden = jnp.where(mask > 0, jnp.maximum(acc_ref[slot, 0, pair], 0.0), 0.0)
            hidden = hidden.astype(BF16).astype(F32)
            narrow_hidden[slot, pair] = hidden
            narrow_delta[slot, pair] = jnp.where(hidden > 0, acc_ref[slot, 1, pair], 0.0)
    shift_rows(narrow_hidden, taps_hidden, pairs + 1, 8, side)
    shift_rows(narrow_delta, taps_delta, pairs + 1, 8, side)

    copies = []
    for slot in range(slots):
        out = jnp.dot(across(taps_hidden, slot, pairs), forward_two[...], preferred_element_type=F32)
        back = lax.dot_general(
            across(taps_delta, slot, pairs), back_one[...], CONTRACT_LAST, preferred_element_type=F32
        )
        for pair in range(pairs):
            lanes = slice(pair * LANES, (pair + 1) * LANES)
            rows = slice(pair * side, (pair + 1) * side)
            output_ref[slot, :, lanes] = out[rows].astype(BF16)
            grad_input_ref[slot, :, lanes] = back[rows].astype(BF16)
        for k, (source, target) in enumerate(((output_ref, output_hbm), (grad_input_ref, grad_input_hbm))):
            copies.append(pltpu.make_async_copy(source.at[slot], target.at[slot], sems.at[2 * slot + k]))
            copies[-1].start()
    for copy in copies:
        copy.wait()


def local(slide_image, cotangent, weight_one, weight_two, tissue, neighbours):
    devices_tile = lax.axis_size("tile")
    devices = devices_tile * lax.axis_size("slide")
    _, slots, side, width = slide_image.shape
    pairs = width // LANES
    tall = side + 16
    image, upstream = slide_image[0], cotangent[0]
    links = neighbours[0]
    packed = pl.pallas_call(
        pack_kernel,
        out_shape=jax.ShapeDtypeStruct((devices_tile, BLOCK, LANES), BF16),
        in_specs=[ANY] * 3,
        out_specs=VMEM,
        scratch_shapes=[
            pltpu.SMEM(links.shape, jnp.int32),
            pltpu.VMEM(image.shape, BF16),
            pltpu.VMEM(image.shape, BF16),
            pltpu.VMEM((4, 16, LANES), F32),
            pltpu.SemaphoreType.DMA((2 * slots + 1,)),
        ],
        compiler_params=pltpu.CompilerParams(vmem_limit_bytes=PACK_LIMIT),
        name="pack",
    )(links, image, upstream)
    packed, tissue_after = lax.optimization_barrier((packed, tissue))
    halo = lax.all_to_all(packed, "tile", 0, 0, tiled=True)

    edge = jax.ShapeDtypeStruct((2, side, LANES), BF16)
    east, west = pl.pallas_call(
        columns_kernel,
        out_shape=(edge, edge),
        in_specs=[ANY] * 3,
        out_specs=(VMEM, VMEM),
        scratch_shapes=[
            pltpu.SMEM(tissue.shape, jnp.int32),
            pltpu.VMEM((2, 2, slots, side, LANES), BF16),
            pltpu.SemaphoreType.DMA((5,)),
        ],
        compiler_params=pltpu.CompilerParams(vmem_limit_bytes=PACK_LIMIT),
        cost_estimate=pl.CostEstimate(flops=4 * 10**9, bytes_accessed=10**7, transcendentals=0),
        name="columns",
    )(tissue_after, image, upstream)
    onward = [(k, k + 1) for k in range(devices_tile - 1)]
    from_west = lax.ppermute(east, "tile", onward)
    from_east = lax.ppermute(west, "tile", [(k + 1, k) for k, _ in onward])


    chunk = -(-576 // (2 * devices))
    total = 2 * chunk * devices
    wide = pltpu.VMEM((slots, pairs + 2, side + 32, LANES), F32)
    weights = [pltpu.VMEM((768, LANES), BF16), pltpu.VMEM((LANES, 768), BF16)]
    cost = pl.CostEstimate(flops=4 * 10**9, bytes_accessed=10**7, transcendentals=0)
    grads = pl.pallas_call(
        grads_kernel,
        out_shape=jax.ShapeDtypeStruct((total, LANES), BF16),
        in_specs=[ANY, ANY] + [VMEM] * 5,
        out_specs=VMEM,
        scratch_shapes=[
            pltpu.SMEM(links.shape, jnp.int32),
            pltpu.SMEM(tissue.shape, jnp.int32),
            wide,
            wide,
            pltpu.VMEM((slots, pairs + 1, side, LANES), BF16),
            pltpu.VMEM((slots, pairs + 1, side, LANES), BF16),
            pltpu.VMEM((slots, 3, pairs + 2, side, LANES), BF16),
            pltpu.VMEM((slots, 3, pairs + 2, side, LANES), BF16),
            *weights,
            pltpu.VMEM((slots, 2, pairs + 1, side, LANES), F32),
            pltpu.SemaphoreType.DMA((2,)),
        ],
        compiler_params=pltpu.CompilerParams(vmem_limit_bytes=32 * 2**20),
        cost_estimate=cost,
        name="grads",
    )(links, tissue, image, upstream, halo, weight_one, weight_two)
    output, grad_input = pl.pallas_call(
        fields_kernel,
        out_shape=(jax.ShapeDtypeStruct((slots, side, width), BF16),) * 2,
        in_specs=[ANY, ANY] + [VMEM] * 7,
        out_specs=(ANY, ANY),
        scratch_shapes=[
            pltpu.SMEM(links.shape, jnp.int32),
            pltpu.SMEM(tissue.shape, jnp.int32),
            wide,
            wide,
            pltpu.VMEM((slots, pairs + 1, tall, LANES), F32),
            pltpu.VMEM((slots, pairs + 1, tall, LANES), F32),
            pltpu.VMEM((slots, 3, pairs + 2, tall, LANES), BF16),
            pltpu.VMEM((slots, 3, pairs + 2, tall, LANES), BF16),
            pltpu.VMEM((slots, 3, pairs + 1, side, LANES), BF16),
            pltpu.VMEM((slots, 3, pairs + 1, side, LANES), BF16),
            weights[0],
            weights[0],
            weights[1],
            weights[1],
            pltpu.VMEM((slots, 2, pairs + 1, tall, LANES), F32),
            pltpu.VMEM((slots, side, width), BF16),
            pltpu.VMEM((slots, side, width), BF16),
            pltpu.SemaphoreType.DMA((2 * slots + 2,)),
        ],
        compiler_params=pltpu.CompilerParams(vmem_limit_bytes=40 * 2**20),
        cost_estimate=cost,
        name="fields",
    )(links, tissue, image, upstream, halo, from_west, from_east, weight_one, weight_two)

    parts = lax.all_to_all(grads.reshape(devices, chunk, 2, LANES), ("slide", "tile"), 0, 0, tiled=True)
    mine = jnp.sum(lax.optimization_barrier(parts.astype(F32)), axis=0).astype(BF16)
    sums = jnp.broadcast_to(mine[None], parts.shape)
    whole = lax.all_to_all(sums, ("slide", "tile"), 0, 0, tiled=True)
    whole = lax.optimization_barrier(whole.reshape(total, LANES).astype(F32))
    grad_one = whole[:576, : LANES // 2]
    grad_two = whole[:576, LANES // 2 :]
    shape = weight_one.shape
    return output[None], grad_input[None], grad_one.reshape(shape), grad_two.reshape(shape)


def solution(mesh):
    placed = (
        P("slide", "tile", None, None),
        P("slide", "tile", None, None),
        P(),
        P(),
        P("slide", "tile"),
        P("slide", "tile", None),
    )
    return jax.shard_map(
        local,
        mesh=mesh,
        in_specs=placed,
        out_specs=(P("slide", "tile", None, None), P("slide", "tile", None, None), P(), P()),
        check_vma=False,
    )
```

```python
import functools

import jax
import jax.numpy as jnp
from jax import lax
from jax.experimental import pallas as pl
from jax.experimental.pallas import tpu as pltpu
from jax.sharding import PartitionSpec as P

F32 = jnp.float32
BF16 = jnp.bfloat16
LANES = 128
VMEM = pl.BlockSpec(memory_space=pltpu.VMEM)
ANY = pl.BlockSpec(memory_space=pl.ANY)
PACK_LIMIT = 60 * 2**20


RING = 2 * 48


def strip_row(field, slot):
    return field * 48 + slot * 16


def column_row(field):
    return field * 48 + 32


def forward_weights(source, forward):
    zero = jnp.zeros((LANES // 2, LANES // 2), BF16)
    for a in range(3):
        taps = [source[a, b] for b in range(3)]
        left = jnp.concatenate(taps + [zero], axis=0)
        right = jnp.concatenate([zero] + taps, axis=0)
        forward[a * 256 : (a + 1) * 256, :] = jnp.concatenate([left, right], axis=1)


def back_weights(source, back):
    zero = jnp.zeros((LANES // 2, LANES // 2), BF16)
    for a in range(3):
        turned = [source[2 - a, 2 - b] for b in range(3)]
        upper = jnp.concatenate(turned + [zero], axis=1)
        lower = jnp.concatenate([zero] + turned, axis=1)
        back[:, a * 256 : (a + 1) * 256] = jnp.concatenate([upper, lower], axis=0)


def across(taps, slot, count):
    rows = taps.shape[3]
    parts = [
        taps[slot, a, right : count + right].reshape(count * rows, LANES)
        for a in range(3)
        for right in range(2)
    ]
    return jnp.concatenate(parts, axis=1)


CONTRACT_FIRST = (((0,), (0,)), ((), ()))
CONTRACT_LAST = (((1,), (1,)), ((), ()))


def pack_kernel(
    links_hbm, image_hbm, cotangent_hbm, out_ref,
    links_ref, image_ref, cotangent_ref, strip_ref, sems,
):
    slots, side, width = image_ref.shape
    pairs = width // LANES
    half = LANES // 2
    copies = [pltpu.make_async_copy(links_hbm, links_ref, sems.at[2 * slots])]
    copies[0].start()
    fields = ((image_hbm, image_ref), (cotangent_hbm, cotangent_ref))
    for field, (source, target) in enumerate(fields):
        for slot in range(slots):
            copy = pltpu.make_async_copy(source.at[slot], target.at[slot], sems.at[field * slots + slot])
            copy.start()
            copies.append(copy)
    me = lax.axis_index("tile")
    left = lax.broadcasted_iota(jnp.int32, (16, LANES), 1) < half
    copies[0].wait()
    for field, (_, ref) in enumerate(fields):
        for slot in range(slots):
            copies[1 + field * slots + slot].wait()
            top = ref[slot, 0:16, :].astype(F32)
            bottom = ref[slot, side - 16 : side, :].astype(F32)
            for pair in range(pairs):
                lanes = slice(pair * LANES, (pair + 1) * LANES)
                strip_ref[0, pair : pair + 1, :] = top[0:1, lanes]
                strip_ref[1, pair : pair + 1, :] = top[1:2, lanes]
                strip_ref[2, pair : pair + 1, :] = bottom[15:16, lanes]
                strip_ref[3, pair : pair + 1, :] = bottom[14:15, lanes]
            for direction in range(8):
                link = links_ref[slot, direction]

                @pl.when(link >= 0)
                def _(slot=slot, direction=direction, link=link, field=field, ref=ref):
                    device = link // slots
                    if direction in (2, 3):
                        first = jnp.where(device == me, strip_row(field, slot), column_row(field))
                        inner = pl.ds(pl.multiple_of(first, 16), 16)
                        outer = pl.ds(pl.multiple_of(first + RING, 16), 16)
                        lanes = slice(0, LANES) if direction == 2 else slice(width - LANES, width)
                        block = ref[slot, :, lanes].astype(F32)
                        other = pltpu.roll(block, half, 1)
                        low = jnp.where(left, block[0:16], other[16:32]).astype(BF16)
                        high = jnp.where(left, other[0:16], block[16:32]).astype(BF16)
                        out_ref[device, inner, :] = low if direction == 2 else high
                        out_ref[device, outer, :] = high if direction == 2 else low
                    else:
                        which = 0 if direction in (0, 4, 5) else 2
                        first = strip_row(field, slot)
                        out_ref[device, first : first + 16, :] = strip_ref[which].astype(BF16)
                        first += RING
                        out_ref[device, first : first + 16, :] = strip_ref[which + 1].astype(BF16)


def place_halo(links_ref, halo_ref, rings, wide, slot, field, slots, side, pairs, me):
    half = LANES // 2
    left = lax.broadcasted_iota(jnp.int32, (16, LANES), 1) < half
    none = jnp.zeros((16, LANES), F32)
    for direction in range(8):
        link = links_ref[slot, direction]
        device, there = jnp.maximum(link, 0) // slots, jnp.maximum(link, 0) % slots
        first = strip_row(field, 0) + there * 16
        if direction in (2, 3):
            first = jnp.where(device == me, first, column_row(field))
        got = []
        for ring in range(rings):
            at = pl.ds(pl.multiple_of(first + ring * RING, 16), 16)
            got.append(jnp.where(link >= 0, halo_ref[device, at, :].astype(F32), 0.0))
        if direction in (2, 3):
            inner, outer = got[0], got[1] if len(got) > 1 else none
            low, high = (outer, inner) if direction == 2 else (inner, outer)
            column = 0 if direction == 2 else pairs + 1
            wide[slot, column, 16:32, :] = jnp.where(left, low, pltpu.roll(high, half, 1))
            wide[slot, column, 32:48, :] = jnp.where(left, pltpu.roll(low, half, 1), high)
        else:
            north = direction in (0, 4, 5)
            for ring, strip in enumerate(got):
                row = 15 - ring if north else 16 + side + ring
                if direction < 2:
                    for pair in range(pairs):
                        wide[slot, pair + 1, row : row + 1, :] = strip[pair : pair + 1, :]
                elif direction in (4, 6):
                    wide[slot, 0, row : row + 1, :] = strip[pairs - 1 : pairs, :]
                else:
                    wide[slot, pairs + 1, row : row + 1, :] = strip[0:1, :]


def place_own(tissue_ref, ref, wide, slot, side, pairs):
    present = tissue_ref[0, slot] > 0
    for pair in range(pairs):
        block = ref[slot, :, pair * LANES : (pair + 1) * LANES].astype(F32)
        wide[slot, pair + 1, 16 : 16 + side, :] = jnp.where(present, block, 0.0)


def shift_rows(field, taps, count, start, rows):
    for pair in range(count):
        for slot in range(field.shape[0]):
            for a in range(3):
                taps[slot, a, pair] = field[slot, pair, start + a - 1 : start + a - 1 + rows, :].astype(BF16)


def grads_kernel(
    links_hbm, tissue_hbm, image_ref, cotangent_ref, halo_ref, one_ref, two_ref,
    grads_hbm,
    grads_ref, links_ref, tissue_ref, wide_in, wide_up, own_hidden, own_delta,
    taps_in, taps_up, forward_ref, back_ref, acc_ref, sems,
):
    slots, side, width = image_ref.shape
    pairs = width // LANES
    half = LANES // 2
    me = lax.axis_index("tile")

    small = [
        pltpu.make_async_copy(tissue_hbm, tissue_ref, sems.at[0]),
        pltpu.make_async_copy(links_hbm, links_ref, sems.at[1]),
    ]
    for copy in small:
        copy.start()
    forward_weights(one_ref, forward_ref)
    back_weights(two_ref, back_ref)
    for copy in small:
        copy.wait()
    for field, (ref, wide) in enumerate(((image_ref, wide_in), (cotangent_ref, wide_up))):
        for slot in range(slots):
            place_own(tissue_ref, ref, wide, slot, side, pairs)
            place_halo(links_ref, halo_ref, 1, wide, slot, field, slots, side, pairs, me)
    shift_rows(wide_in, taps_in, pairs + 2, 16, side)
    shift_rows(wide_up, taps_up, pairs + 2, 16, side)

    left = lax.broadcasted_iota(jnp.int32, (side, LANES), 1) < half
    first_grad = None
    second_grad = None
    for slot in range(slots):
        before = jnp.dot(across(taps_in, slot, pairs + 1), forward_ref[...], preferred_element_type=F32)
        acc_ref[slot, 0] = before.reshape(pairs + 1, side, LANES)
        after = lax.dot_general(
            across(taps_up, slot, pairs + 1), back_ref[...], CONTRACT_LAST, preferred_element_type=F32
        )
        acc_ref[slot, 1] = after.reshape(pairs + 1, side, LANES)
        for pair in range(pairs + 1):
            hidden = jnp.maximum(acc_ref[slot, 0, pair], 0.0)
            if pair == 0:
                hidden = jnp.where(left, 0.0, hidden)
            if pair == pairs:
                hidden = jnp.where(left, hidden, 0.0)
            hidden = hidden.astype(BF16)
            own_hidden[slot, pair] = hidden
            delta = jnp.where(hidden.astype(F32) > 0, acc_ref[slot, 1, pair], 0.0)
            own_delta[slot, pair] = delta.astype(BF16)
        term_one = lax.dot_general(
            own_delta[slot].reshape((pairs + 1) * side, LANES), across(taps_in, slot, pairs + 1),
            CONTRACT_FIRST, preferred_element_type=F32,
        )
        term_two = lax.dot_general(
            own_hidden[slot].reshape((pairs + 1) * side, LANES), across(taps_up, slot, pairs + 1),
            CONTRACT_FIRST, preferred_element_type=F32,
        )
        first_grad = term_one if first_grad is None else first_grad + term_one
        second_grad = term_two if second_grad is None else second_grad + term_two

    total = grads_ref.shape[0]
    copies = []
    left = lax.broadcasted_iota(jnp.int32, (half, LANES), 1) < half
    for a in range(3):
        one = first_grad[:, a * 256 : (a + 1) * 256].T
        two = second_grad[:, (2 - a) * 256 : (3 - a) * 256]
        blocks = [two[:half, 0:LANES], two[:half, LANES:256], two[half:, 0:LANES], two[half:, LANES:256]]
        turned = [pltpu.roll(block, half, 1) for block in blocks]
        right = (turned[0] + blocks[2], blocks[0] + turned[3], turned[1] + blocks[3])
        for b in range(3):
            upper = one[b * half : (b + 1) * half]
            lower = one[(b + 1) * half : (b + 2) * half]
            rows = slice((a * 3 + b) * half, (a * 3 + b + 1) * half)
            both = jnp.where(left, upper + pltpu.roll(lower, half, 1), right[2 - b])
            grads_ref[rows, :] = both.astype(BF16)
        rows = slice(a * 192, (a + 1) * 192 if a < 2 else total)
        copies.append(pltpu.make_async_copy(grads_ref.at[rows], grads_hbm.at[rows], sems.at[2 + a]))
        if a < 2:
            copies[a].start()
    if total > 576:
        grads_ref[576:total, :] = jnp.zeros((total - 576, LANES), BF16)
    copies[2].start()
    for copy in copies:
        copy.wait()


def fields_kernel(
    links_hbm, tissue_hbm, image_ref, cotangent_ref, halo_ref, one_ref, two_ref,
    output_hbm, grad_input_hbm,
    links_ref, tissue_ref, wide_in, wide_up, narrow_hidden, narrow_delta,
    taps_in, taps_up, taps_hidden, taps_delta, forward_one, forward_two, back_one, back_two,
    acc_ref, output_ref, grad_input_ref, sems,
):
    slots, side, width = image_ref.shape
    pairs = width // LANES
    half = LANES // 2
    tall = side + 16
    me = lax.axis_index("tile")

    small = [
        pltpu.make_async_copy(tissue_hbm, tissue_ref, sems.at[2 * slots]),
        pltpu.make_async_copy(links_hbm, links_ref, sems.at[2 * slots + 1]),
    ]
    for copy in small:
        copy.start()
    forward_weights(one_ref, forward_one)
    forward_weights(two_ref, forward_two)
    back_weights(one_ref, back_one)
    back_weights(two_ref, back_two)
    for copy in small:
        copy.wait()
    for field, (ref, wide) in enumerate(((image_ref, wide_in), (cotangent_ref, wide_up))):
        wide[:, :, 0:16, :] = jnp.zeros((slots, pairs + 2, 16, LANES), F32)
        wide[:, :, 16 + side : 32 + side, :] = jnp.zeros((slots, pairs + 2, 16, LANES), F32)
        for slot in range(slots):
            place_own(tissue_ref, ref, wide, slot, side, pairs)
            place_halo(links_ref, halo_ref, 2, wide, slot, field, slots, side, pairs, me)
    shift_rows(wide_in, taps_in, pairs + 2, 8, tall)
    shift_rows(wide_up, taps_up, pairs + 2, 8, tall)

    row = lax.broadcasted_iota(jnp.int32, (tall, LANES), 0)
    lane = lax.broadcasted_iota(jnp.int32, (tall, LANES), 1)

    def column_mask(north, here, south):
        value = jnp.where(row == 7, north, jnp.where(row == 8 + side, south, here))
        return jnp.where((row >= 7) & (row <= 8 + side), value, 0)

    for slot in range(slots):
        there = [(links_ref[slot, k] >= 0).astype(jnp.int32) for k in range(8)]
        own = tissue_ref[0, slot]
        middle = column_mask(there[0], own, there[1])
        west = jnp.where(lane < half, column_mask(there[4], there[2], there[6]), middle)
        east = jnp.where(lane < half, middle, column_mask(there[5], there[3], there[7]))
        before = jnp.dot(across(taps_in, slot, pairs + 1), forward_one[...], preferred_element_type=F32)
        acc_ref[slot, 0] = before.reshape(pairs + 1, tall, LANES)
        after = lax.dot_general(
            across(taps_up, slot, pairs + 1), back_two[...], CONTRACT_LAST, preferred_element_type=F32
        )
        acc_ref[slot, 1] = after.reshape(pairs + 1, tall, LANES)
        for pair in range(pairs + 1):
            mask = west if pair == 0 else east if pair == pairs else middle
            hidden = jnp.where(mask > 0, jnp.maximum(acc_ref[slot, 0, pair], 0.0), 0.0)
            hidden = hidden.astype(BF16).astype(F32)
            narrow_hidden[slot, pair] = hidden
            narrow_delta[slot, pair] = jnp.where(hidden > 0, acc_ref[slot, 1, pair], 0.0)
    shift_rows(narrow_hidden, taps_hidden, pairs + 1, 8, side)
    shift_rows(narrow_delta, taps_delta, pairs + 1, 8, side)

    copies = []
    for slot in range(slots):
        out = jnp.dot(across(taps_hidden, slot, pairs), forward_two[...], preferred_element_type=F32)
        back = lax.dot_general(
            across(taps_delta, slot, pairs), back_one[...], CONTRACT_LAST, preferred_element_type=F32
        )
        for pair in range(pairs):
            lanes = slice(pair * LANES, (pair + 1) * LANES)
            rows = slice(pair * side, (pair + 1) * side)
            output_ref[slot, :, lanes] = out[rows].astype(BF16)
            grad_input_ref[slot, :, lanes] = back[rows].astype(BF16)
        for k, (source, target) in enumerate(((output_ref, output_hbm), (grad_input_ref, grad_input_hbm))):
            copies.append(pltpu.make_async_copy(source.at[slot], target.at[slot], sems.at[2 * slot + k]))
            copies[-1].start()
    for copy in copies:
        copy.wait()


def local(slide_image, cotangent, weight_one, weight_two, tissue, neighbours):
    devices_tile = lax.axis_size("tile")
    devices = devices_tile * lax.axis_size("slide")
    _, slots, side, width = slide_image.shape
    pairs = width // LANES
    tall = side + 16
    image, upstream = slide_image[0], cotangent[0]
    links = neighbours[0]
    packed = pl.pallas_call(
        pack_kernel,
        out_shape=jax.ShapeDtypeStruct((devices_tile, 2 * RING, LANES), BF16),
        in_specs=[ANY] * 3,
        out_specs=VMEM,
        scratch_shapes=[
            pltpu.SMEM(links.shape, jnp.int32),
            pltpu.VMEM(image.shape, BF16),
            pltpu.VMEM(image.shape, BF16),
            pltpu.VMEM((4, 16, LANES), F32),
            pltpu.SemaphoreType.DMA((2 * slots + 1,)),
        ],
        compiler_params=pltpu.CompilerParams(vmem_limit_bytes=PACK_LIMIT),
        name="pack",
    )(links, image, upstream)
    halo = lax.all_to_all(packed, "tile", 0, 0, tiled=True)

    chunk = -(-576 // (2 * devices))
    total = 2 * chunk * devices
    wide = pltpu.VMEM((slots, pairs + 2, side + 32, LANES), F32)
    weights = [pltpu.VMEM((768, LANES), BF16), pltpu.VMEM((LANES, 768), BF16)]
    cost = pl.CostEstimate(flops=4 * 10**9, bytes_accessed=10**7, transcendentals=0)
    grads = pl.pallas_call(
        grads_kernel,
        out_shape=jax.ShapeDtypeStruct((total, LANES), BF16),
        in_specs=[ANY, ANY] + [VMEM] * 5,
        out_specs=ANY,
        scratch_shapes=[
            pltpu.VMEM((total, LANES), BF16),
            pltpu.SMEM(links.shape, jnp.int32),
            pltpu.SMEM(tissue.shape, jnp.int32),
            wide,
            wide,
            pltpu.VMEM((slots, pairs + 1, side, LANES), BF16),
            pltpu.VMEM((slots, pairs + 1, side, LANES), BF16),
            pltpu.VMEM((slots, 3, pairs + 2, side, LANES), BF16),
            pltpu.VMEM((slots, 3, pairs + 2, side, LANES), BF16),
            *weights,
            pltpu.VMEM((slots, 2, pairs + 1, side, LANES), F32),
            pltpu.SemaphoreType.DMA((5,)),
        ],
        compiler_params=pltpu.CompilerParams(vmem_limit_bytes=32 * 2**20),
        cost_estimate=cost,
        name="grads",
    )(links, tissue, image, upstream, halo, weight_one, weight_two)
    output, grad_input = pl.pallas_call(
        fields_kernel,
        out_shape=(jax.ShapeDtypeStruct((slots, side, width), BF16),) * 2,
        in_specs=[ANY, ANY] + [VMEM] * 5,
        out_specs=(ANY, ANY),
        scratch_shapes=[
            pltpu.SMEM(links.shape, jnp.int32),
            pltpu.SMEM(tissue.shape, jnp.int32),
            wide,
            wide,
            pltpu.VMEM((slots, pairs + 1, tall, LANES), F32),
            pltpu.VMEM((slots, pairs + 1, tall, LANES), F32),
            pltpu.VMEM((slots, 3, pairs + 2, tall, LANES), BF16),
            pltpu.VMEM((slots, 3, pairs + 2, tall, LANES), BF16),
            pltpu.VMEM((slots, 3, pairs + 1, side, LANES), BF16),
            pltpu.VMEM((slots, 3, pairs + 1, side, LANES), BF16),
            weights[0],
            weights[0],
            weights[1],
            weights[1],
            pltpu.VMEM((slots, 2, pairs + 1, tall, LANES), F32),
            pltpu.VMEM((slots, side, width), BF16),
            pltpu.VMEM((slots, side, width), BF16),
            pltpu.SemaphoreType.DMA((2 * slots + 2,)),
        ],
        compiler_params=pltpu.CompilerParams(vmem_limit_bytes=40 * 2**20),
        cost_estimate=cost,
        name="fields",
    )(links, tissue, image, upstream, halo, weight_one, weight_two)

    parts = lax.all_to_all(grads.reshape(devices, chunk, 2, LANES), ("slide", "tile"), 0, 0, tiled=True)
    mine = jnp.sum(lax.optimization_barrier(parts.astype(F32)), axis=0).astype(BF16)
    mine, output, grad_input = lax.optimization_barrier((mine, output, grad_input))
    sums = jnp.broadcast_to(mine[None], parts.shape)
    whole = lax.all_to_all(sums, ("slide", "tile"), 0, 0, tiled=True)
    whole = lax.optimization_barrier(whole.reshape(total, LANES).astype(F32))
    grad_one = whole[:576, : LANES // 2]
    grad_two = whole[:576, LANES // 2 :]
    shape = weight_one.shape
    return output[None], grad_input[None], grad_one.reshape(shape), grad_two.reshape(shape)


def solution(mesh):
    placed = (
        P("slide", "tile", None, None),
        P("slide", "tile", None, None),
        P(),
        P(),
        P("slide", "tile"),
        P("slide", "tile", None),
    )
    return jax.shard_map(
        local,
        mesh=mesh,
        in_specs=placed,
        out_specs=(P("slide", "tile", None, None), P("slide", "tile", None, None), P(), P()),
        check_vma=False,
    )
```

```python
import functools

import jax
import jax.numpy as jnp
from jax import lax
from jax.experimental import pallas as pl
from jax.experimental.pallas import tpu as pltpu
from jax.sharding import PartitionSpec as P

F32 = jnp.float32
BF16 = jnp.bfloat16
LANES = 128
VMEM = pl.BlockSpec(memory_space=pltpu.VMEM)
ANY = pl.BlockSpec(memory_space=pl.ANY)
PACK_LIMIT = 60 * 2**20


RING = 2 * 48


def strip_row(field, slot):
    return field * 48 + slot * 16


def column_row(field):
    return field * 48 + 32


def forward_weights(source, forward):
    zero = jnp.zeros((LANES // 2, LANES // 2), BF16)
    for a in range(3):
        taps = [source[a, b] for b in range(3)]
        left = jnp.concatenate(taps + [zero], axis=0)
        right = jnp.concatenate([zero] + taps, axis=0)
        forward[a * 256 : (a + 1) * 256, :] = jnp.concatenate([left, right], axis=1)


def back_weights(source, back):
    zero = jnp.zeros((LANES // 2, LANES // 2), BF16)
    for a in range(3):
        turned = [source[2 - a, 2 - b] for b in range(3)]
        upper = jnp.concatenate(turned + [zero], axis=1)
        lower = jnp.concatenate([zero] + turned, axis=1)
        back[:, a * 256 : (a + 1) * 256] = jnp.concatenate([upper, lower], axis=0)


def across(taps, slot, count):
    rows = taps.shape[3]
    parts = [
        taps[slot, a, right : count + right].reshape(count * rows, LANES)
        for a in range(3)
        for right in range(2)
    ]
    return jnp.concatenate(parts, axis=1)


CONTRACT_FIRST = (((0,), (0,)), ((), ()))
CONTRACT_LAST = (((1,), (1,)), ((), ()))


def pack_kernel(
    links_hbm, image_hbm, cotangent_hbm, out_hbm,
    out_ref, links_ref, image_ref, cotangent_ref, strip_ref, sems,
):
    slots, side, width = image_ref.shape
    pairs = width // LANES
    half = LANES // 2
    copies = [pltpu.make_async_copy(links_hbm, links_ref, sems.at[2 * slots])]
    copies[0].start()
    fields = ((image_hbm, image_ref), (cotangent_hbm, cotangent_ref))
    for field, (source, target) in enumerate(fields):
        for slot in range(slots):
            copy = pltpu.make_async_copy(source.at[slot], target.at[slot], sems.at[field * slots + slot])
            copy.start()
            copies.append(copy)
    me = lax.axis_index("tile")
    left = lax.broadcasted_iota(jnp.int32, (16, LANES), 1) < half
    copies[0].wait()
    sends = []
    for field, (_, ref) in enumerate(fields):
        for slot in range(slots):
            copies[1 + field * slots + slot].wait()
            top = ref[slot, 0:16, :].astype(F32)
            bottom = ref[slot, side - 16 : side, :].astype(F32)
            for pair in range(pairs):
                lanes = slice(pair * LANES, (pair + 1) * LANES)
                strip_ref[0, pair : pair + 1, :] = top[0:1, lanes]
                strip_ref[1, pair : pair + 1, :] = top[1:2, lanes]
                strip_ref[2, pair : pair + 1, :] = bottom[15:16, lanes]
                strip_ref[3, pair : pair + 1, :] = bottom[14:15, lanes]
            for direction in range(8):
                link = links_ref[slot, direction]

                @pl.when(link >= 0)
                def _(slot=slot, direction=direction, link=link, field=field, ref=ref):
                    device = link // slots
                    if direction in (2, 3):
                        first = jnp.where(device == me, strip_row(field, slot), column_row(field))
                        inner = pl.ds(pl.multiple_of(first, 16), 16)
                        outer = pl.ds(pl.multiple_of(first + RING, 16), 16)
                        lanes = slice(0, LANES) if direction == 2 else slice(width - LANES, width)
                        block = ref[slot, :, lanes].astype(F32)
                        other = pltpu.roll(block, half, 1)
                        low = jnp.where(left, block[0:16], other[16:32]).astype(BF16)
                        high = jnp.where(left, other[0:16], block[16:32]).astype(BF16)
                        out_ref[device, inner, :] = low if direction == 2 else high
                        out_ref[device, outer, :] = high if direction == 2 else low
                    else:
                        which = 0 if direction in (0, 4, 5) else 2
                        first = strip_row(field, slot)
                        out_ref[device, first : first + 16, :] = strip_ref[which].astype(BF16)
                        first += RING
                        out_ref[device, first : first + 16, :] = strip_ref[which + 1].astype(BF16)
        for ring in range(2):
            rows = slice(ring * RING + field * 48, ring * RING + field * 48 + 48)
            send = pltpu.make_async_copy(
                out_ref.at[:, rows], out_hbm.at[:, rows], sems.at[2 * slots + 1 + 2 * field + ring]
            )
            send.start()
            sends.append(send)
    for send in sends:
        send.wait()


def place_halo(links_ref, halo_ref, rings, wide, slot, field, slots, side, pairs, me):
    half = LANES // 2
    left = lax.broadcasted_iota(jnp.int32, (16, LANES), 1) < half
    none = jnp.zeros((16, LANES), F32)
    for direction in range(8):
        link = links_ref[slot, direction]
        device, there = jnp.maximum(link, 0) // slots, jnp.maximum(link, 0) % slots
        first = strip_row(field, 0) + there * 16
        if direction in (2, 3):
            first = jnp.where(device == me, first, column_row(field))
        got = []
        for ring in range(rings):
            at = pl.ds(pl.multiple_of(first + ring * RING, 16), 16)
            got.append(jnp.where(link >= 0, halo_ref[device, at, :].astype(F32), 0.0))
        if direction in (2, 3):
            inner, outer = got[0], got[1] if len(got) > 1 else none
            low, high = (outer, inner) if direction == 2 else (inner, outer)
            column = 0 if direction == 2 else pairs + 1
            wide[slot, column, 16:32, :] = jnp.where(left, low, pltpu.roll(high, half, 1))
            wide[slot, column, 32:48, :] = jnp.where(left, pltpu.roll(low, half, 1), high)
        else:
            north = direction in (0, 4, 5)
            for ring, strip in enumerate(got):
                row = 15 - ring if north else 16 + side + ring
                if direction < 2:
                    for pair in range(pairs):
                        wide[slot, pair + 1, row : row + 1, :] = strip[pair : pair + 1, :]
                elif direction in (4, 6):
                    wide[slot, 0, row : row + 1, :] = strip[pairs - 1 : pairs, :]
                else:
                    wide[slot, pairs + 1, row : row + 1, :] = strip[0:1, :]


def place_own(tissue_ref, ref, wide, slot, side, pairs):
    present = tissue_ref[0, slot] > 0
    for pair in range(pairs):
        block = ref[slot, :, pair * LANES : (pair + 1) * LANES].astype(F32)
        wide[slot, pair + 1, 16 : 16 + side, :] = jnp.where(present, block, 0.0)


def shift_rows(field, taps, count, start, rows):
    for pair in range(count):
        for slot in range(field.shape[0]):
            for a in range(3):
                taps[slot, a, pair] = field[slot, pair, start + a - 1 : start + a - 1 + rows, :].astype(BF16)


def grads_kernel(
    links_hbm, tissue_hbm, image_ref, cotangent_ref, halo_ref, one_ref, two_ref,
    grads_ref,
    links_ref, tissue_ref, wide_in, wide_up, own_hidden, own_delta,
    taps_in, taps_up, forward_ref, back_ref, acc_ref, sems,
):
    slots, side, width = image_ref.shape
    pairs = width // LANES
    half = LANES // 2
    me = lax.axis_index("tile")

    small = [
        pltpu.make_async_copy(tissue_hbm, tissue_ref, sems.at[0]),
        pltpu.make_async_copy(links_hbm, links_ref, sems.at[1]),
    ]
    for copy in small:
        copy.start()
    forward_weights(one_ref, forward_ref)
    back_weights(two_ref, back_ref)
    for copy in small:
        copy.wait()
    for field, (ref, wide) in enumerate(((image_ref, wide_in), (cotangent_ref, wide_up))):
        for slot in range(slots):
            place_own(tissue_ref, ref, wide, slot, side, pairs)
            place_halo(links_ref, halo_ref, 1, wide, slot, field, slots, side, pairs, me)
    shift_rows(wide_in, taps_in, pairs + 2, 16, side)
    shift_rows(wide_up, taps_up, pairs + 2, 16, side)

    left = lax.broadcasted_iota(jnp.int32, (side, LANES), 1) < half
    first_grad = None
    second_grad = None
    for slot in range(slots):
        before = jnp.dot(across(taps_in, slot, pairs + 1), forward_ref[...], preferred_element_type=F32)
        acc_ref[slot, 0] = before.reshape(pairs + 1, side, LANES)
        after = lax.dot_general(
            across(taps_up, slot, pairs + 1), back_ref[...], CONTRACT_LAST, preferred_element_type=F32
        )
        acc_ref[slot, 1] = after.reshape(pairs + 1, side, LANES)
        for pair in range(pairs + 1):
            hidden = jnp.maximum(acc_ref[slot, 0, pair], 0.0)
            if pair == 0:
                hidden = jnp.where(left, 0.0, hidden)
            if pair == pairs:
                hidden = jnp.where(left, hidden, 0.0)
            hidden = hidden.astype(BF16)
            own_hidden[slot, pair] = hidden
            delta = jnp.where(hidden.astype(F32) > 0, acc_ref[slot, 1, pair], 0.0)
            own_delta[slot, pair] = delta.astype(BF16)
        term_one = lax.dot_general(
            own_delta[slot].reshape((pairs + 1) * side, LANES), across(taps_in, slot, pairs + 1),
            CONTRACT_FIRST, preferred_element_type=F32,
        )
        term_two = lax.dot_general(
            own_hidden[slot].reshape((pairs + 1) * side, LANES), across(taps_up, slot, pairs + 1),
            CONTRACT_FIRST, preferred_element_type=F32,
        )
        first_grad = term_one if first_grad is None else first_grad + term_one
        second_grad = term_two if second_grad is None else second_grad + term_two

    total = grads_ref.shape[0]
    left = lax.broadcasted_iota(jnp.int32, (half, LANES), 1) < half
    for a in range(3):
        one = first_grad[:, a * 256 : (a + 1) * 256].T
        two = second_grad[:, (2 - a) * 256 : (3 - a) * 256]
        blocks = [two[:half, 0:LANES], two[:half, LANES:256], two[half:, 0:LANES], two[half:, LANES:256]]
        turned = [pltpu.roll(block, half, 1) for block in blocks]
        right = (turned[0] + blocks[2], blocks[0] + turned[3], turned[1] + blocks[3])
        for b in range(3):
            upper = one[b * half : (b + 1) * half]
            lower = one[(b + 1) * half : (b + 2) * half]
            rows = slice((a * 3 + b) * half, (a * 3 + b + 1) * half)
            both = jnp.where(left, upper + pltpu.roll(lower, half, 1), right[2 - b])
            grads_ref[rows, :] = both.astype(BF16)
    if total > 576:
        grads_ref[576:total, :] = jnp.zeros((total - 576, LANES), BF16)


def fields_kernel(
    links_hbm, tissue_hbm, image_ref, cotangent_ref, halo_ref, one_ref, two_ref,
    output_hbm, grad_input_hbm,
    links_ref, tissue_ref, wide_in, wide_up, narrow_hidden, narrow_delta,
    taps_in, taps_up, taps_hidden, taps_delta, forward_one, forward_two, back_one, back_two,
    acc_ref, output_ref, grad_input_ref, sems,
):
    slots, side, width = image_ref.shape
    pairs = width // LANES
    half = LANES // 2
    tall = side + 16
    me = lax.axis_index("tile")

    small = [
        pltpu.make_async_copy(tissue_hbm, tissue_ref, sems.at[2 * slots]),
        pltpu.make_async_copy(links_hbm, links_ref, sems.at[2 * slots + 1]),
    ]
    for copy in small:
        copy.start()
    forward_weights(one_ref, forward_one)
    forward_weights(two_ref, forward_two)
    back_weights(one_ref, back_one)
    back_weights(two_ref, back_two)
    for copy in small:
        copy.wait()
    for field, (ref, wide) in enumerate(((image_ref, wide_in), (cotangent_ref, wide_up))):
        wide[:, :, 0:16, :] = jnp.zeros((slots, pairs + 2, 16, LANES), F32)
        wide[:, :, 16 + side : 32 + side, :] = jnp.zeros((slots, pairs + 2, 16, LANES), F32)
        for slot in range(slots):
            place_own(tissue_ref, ref, wide, slot, side, pairs)
            place_halo(links_ref, halo_ref, 2, wide, slot, field, slots, side, pairs, me)
    shift_rows(wide_in, taps_in, pairs + 2, 8, tall)
    shift_rows(wide_up, taps_up, pairs + 2, 8, tall)

    row = lax.broadcasted_iota(jnp.int32, (tall, LANES), 0)
    lane = lax.broadcasted_iota(jnp.int32, (tall, LANES), 1)

    def column_mask(north, here, south):
        value = jnp.where(row == 7, north, jnp.where(row == 8 + side, south, here))
        return jnp.where((row >= 7) & (row <= 8 + side), value, 0)

    for slot in range(slots):
        there = [(links_ref[slot, k] >= 0).astype(jnp.int32) for k in range(8)]
        own = tissue_ref[0, slot]
        middle = column_mask(there[0], own, there[1])
        west = jnp.where(lane < half, column_mask(there[4], there[2], there[6]), middle)
        east = jnp.where(lane < half, middle, column_mask(there[5], there[3], there[7]))
        before = jnp.dot(across(taps_in, slot, pairs + 1), forward_one[...], preferred_element_type=F32)
        acc_ref[slot, 0] = before.reshape(pairs + 1, tall, LANES)
        after = lax.dot_general(
            across(taps_up, slot, pairs + 1), back_two[...], CONTRACT_LAST, preferred_element_type=F32
        )
        acc_ref[slot, 1] = after.reshape(pairs + 1, tall, LANES)
        for pair in range(pairs + 1):
            mask = west if pair == 0 else east if pair == pairs else middle
            hidden = jnp.where(mask > 0, jnp.maximum(acc_ref[slot, 0, pair], 0.0), 0.0)
            hidden = hidden.astype(BF16).astype(F32)
            narrow_hidden[slot, pair] = hidden
            narrow_delta[slot, pair] = jnp.where(hidden > 0, acc_ref[slot, 1, pair], 0.0)
    shift_rows(narrow_hidden, taps_hidden, pairs + 1, 8, side)
    shift_rows(narrow_delta, taps_delta, pairs + 1, 8, side)

    copies = []
    for slot in range(slots):
        out = jnp.dot(across(taps_hidden, slot, pairs), forward_two[...], preferred_element_type=F32)
        back = lax.dot_general(
            across(taps_delta, slot, pairs), back_one[...], CONTRACT_LAST, preferred_element_type=F32
        )
        for pair in range(pairs):
            lanes = slice(pair * LANES, (pair + 1) * LANES)
            rows = slice(pair * side, (pair + 1) * side)
            output_ref[slot, :, lanes] = out[rows].astype(BF16)
            grad_input_ref[slot, :, lanes] = back[rows].astype(BF16)
        for k, (source, target) in enumerate(((output_ref, output_hbm), (grad_input_ref, grad_input_hbm))):
            copies.append(pltpu.make_async_copy(source.at[slot], target.at[slot], sems.at[2 * slot + k]))
            copies[-1].start()
    for copy in copies:
        copy.wait()


def local(slide_image, cotangent, weight_one, weight_two, tissue, neighbours):
    devices_tile = lax.axis_size("tile")
    devices = devices_tile * lax.axis_size("slide")
    _, slots, side, width = slide_image.shape
    pairs = width // LANES
    tall = side + 16
    image, upstream = slide_image[0], cotangent[0]
    links = neighbours[0]
    packed = pl.pallas_call(
        pack_kernel,
        out_shape=jax.ShapeDtypeStruct((devices_tile, 2 * RING, LANES), BF16),
        in_specs=[ANY] * 3,
        out_specs=ANY,
        scratch_shapes=[
            pltpu.VMEM((devices_tile, 2 * RING, LANES), BF16),
            pltpu.SMEM(links.shape, jnp.int32),
            pltpu.VMEM(image.shape, BF16),
            pltpu.VMEM(image.shape, BF16),
            pltpu.VMEM((4, 16, LANES), F32),
            pltpu.SemaphoreType.DMA((2 * slots + 5,)),
        ],
        compiler_params=pltpu.CompilerParams(vmem_limit_bytes=PACK_LIMIT),
        name="pack",
    )(links, image, upstream)
    halo = lax.all_to_all(packed, "tile", 0, 0, tiled=True)

    chunk = -(-576 // (2 * devices))
    total = 2 * chunk * devices
    wide = pltpu.VMEM((slots, pairs + 2, side + 32, LANES), F32)
    weights = [pltpu.VMEM((768, LANES), BF16), pltpu.VMEM((LANES, 768), BF16)]
    cost = pl.CostEstimate(flops=4 * 10**9, bytes_accessed=10**7, transcendentals=0)
    grads = pl.pallas_call(
        grads_kernel,
        out_shape=jax.ShapeDtypeStruct((total, LANES), BF16),
        in_specs=[ANY, ANY] + [VMEM] * 5,
        out_specs=VMEM,
        scratch_shapes=[
            pltpu.SMEM(links.shape, jnp.int32),
            pltpu.SMEM(tissue.shape, jnp.int32),
            wide,
            wide,
            pltpu.VMEM((slots, pairs + 1, side, LANES), BF16),
            pltpu.VMEM((slots, pairs + 1, side, LANES), BF16),
            pltpu.VMEM((slots, 3, pairs + 2, side, LANES), BF16),
            pltpu.VMEM((slots, 3, pairs + 2, side, LANES), BF16),
            *weights,
            pltpu.VMEM((slots, 2, pairs + 1, side, LANES), F32),
            pltpu.SemaphoreType.DMA((2,)),
        ],
        compiler_params=pltpu.CompilerParams(vmem_limit_bytes=32 * 2**20),
        cost_estimate=cost,
        name="grads",
    )(links, tissue, image, upstream, halo, weight_one, weight_two)
    output, grad_input = pl.pallas_call(
        fields_kernel,
        out_shape=(jax.ShapeDtypeStruct((slots, side, width), BF16),) * 2,
        in_specs=[ANY, ANY] + [VMEM] * 5,
        out_specs=(ANY, ANY),
        scratch_shapes=[
            pltpu.SMEM(links.shape, jnp.int32),
            pltpu.SMEM(tissue.shape, jnp.int32),
            wide,
            wide,
            pltpu.VMEM((slots, pairs + 1, tall, LANES), F32),
            pltpu.VMEM((slots, pairs + 1, tall, LANES), F32),
            pltpu.VMEM((slots, 3, pairs + 2, tall, LANES), BF16),
            pltpu.VMEM((slots, 3, pairs + 2, tall, LANES), BF16),
            pltpu.VMEM((slots, 3, pairs + 1, side, LANES), BF16),
            pltpu.VMEM((slots, 3, pairs + 1, side, LANES), BF16),
            weights[0],
            weights[0],
            weights[1],
            weights[1],
            pltpu.VMEM((slots, 2, pairs + 1, tall, LANES), F32),
            pltpu.VMEM((slots, side, width), BF16),
            pltpu.VMEM((slots, side, width), BF16),
            pltpu.SemaphoreType.DMA((2 * slots + 2,)),
        ],
        compiler_params=pltpu.CompilerParams(vmem_limit_bytes=40 * 2**20),
        cost_estimate=cost,
        name="fields",
    )(links, tissue, image, upstream, halo, weight_one, weight_two)

    parts = lax.all_to_all(grads.reshape(devices, chunk, 2, LANES), ("slide", "tile"), 0, 0, tiled=True)
    mine = jnp.sum(lax.optimization_barrier(parts.astype(F32)), axis=0).astype(BF16)
    mine, output, grad_input = lax.optimization_barrier((mine, output, grad_input))
    sums = jnp.broadcast_to(mine[None], parts.shape)
    whole = lax.all_to_all(sums, ("slide", "tile"), 0, 0, tiled=True)
    whole = lax.optimization_barrier(whole.reshape(total, LANES).astype(F32))
    grad_one = whole[:576, : LANES // 2]
    grad_two = whole[:576, LANES // 2 :]
    shape = weight_one.shape
    return output[None], grad_input[None], grad_one.reshape(shape), grad_two.reshape(shape)


def solution(mesh):
    placed = (
        P("slide", "tile", None, None),
        P("slide", "tile", None, None),
        P(),
        P(),
        P("slide", "tile"),
        P("slide", "tile", None),
    )
    return jax.shard_map(
        local,
        mesh=mesh,
        in_specs=placed,
        out_specs=(P("slide", "tile", None, None), P("slide", "tile", None, None), P(), P()),
        check_vma=False,
    )
```
